32 devices in a mesh: wide: 8 (over y, x, core), tp: 4 (over z).
Axes of the slice: x: 2, y: 2, z: 4, core: 2. Of those that a mesh axis runs over, the one named last changes fastest.
Arguments:
- tokens: bfloat16 [12288, 1536], P(('wide', 'tp')), may hold values from -6 to 6
- text_states: bfloat16 [512, 1536], P('wide'), may hold values from -6 to 6
- clip_start: int32 [8], replicated, may hold values from 512 to 1023
- ln1_gain: float32 [1536], replicated, may hold values from 0.5 to 1.5
- ln1_bias: float32 [1536], replicated, may hold values from -3 to 3
- self_query: bfloat16 [1536, 1536], P('wide', 'tp'), may hold values from -0.15625 to 0.15625
- self_key: bfloat16 [1536, 1536], P('wide', 'tp'), may hold values from -0.15625 to 0.15625
- self_value: bfloat16 [1536, 1536], P('wide', 'tp'), may hold values from -0.15625 to 0.15625
- self_out: bfloat16 [1536, 1536], P('tp', 'wide'), may hold values from -2.5 to 2.5
- ln2_gain: float32 [1536], replicated, may hold values from 0.5 to 1.5
- ln2_bias: float32 [1536], replicated, may hold values from -3 to 3
- cross_query: bfloat16 [1536, 1536], P('wide', 'tp'), may hold values from -0.15625 to 0.15625
- cross_key: bfloat16 [1536, 1536], P('wide', 'tp'), may hold values from -0.15625 to 0.15625
- cross_value: bfloat16 [1536, 1536], P('wide', 'tp'), may hold values from -0.15625 to 0.15625
- cross_out: bfloat16 [1536, 1536], P('tp', 'wide'), may hold values from -0.875 to 0.875
- ln3_gain: float32 [1536], replicated, may hold values from 0.5 to 1.5
- ln3_bias: float32 [1536], replicated, may hold values from -3 to 3
- fc_in: bfloat16 [1536, 6144], P('wide', 'tp'), may hold values from -0.15625 to 0.15625
- fc_out: bfloat16 [6144, 1536], P('tp', 'wide'), may hold values from -0.078125 to 0.078125
- out_grad: bfloat16 [12288, 1536], P(('wide', 'tp')), may hold values from -6 to 6
Outputs:
- layer_out: bfloat16 [12288, 1536], P(('wide', 'tp'))
- tokens_grad: float32 [12288, 1536], P(('wide', 'tp'))
- text_grad: float32 [512, 1536], P('wide')
- ln1_gain_grad: float32 [1536], replicated
- ln1_bias_grad: float32 [1536], replicated
- self_query_grad: float32 [1536, 1536], P('wide', 'tp')
- self_key_grad: float32 [1536, 1536], P('wide', 'tp')
- self_value_grad: float32 [1536, 1536], P('wide', 'tp')
- self_out_grad: float32 [1536, 1536], P('tp', 'wide')
- ln2_gain_grad: float32 [1536], replicated
- ln2_bias_grad: float32 [1536], replicated
- cross_query_grad: float32 [1536, 1536], P('wide', 'tp')
- cross_key_grad: float32 [1536, 1536], P('wide', 'tp')
- cross_value_grad: float32 [1536, 1536], P('wide', 'tp')
- cross_out_grad: float32 [1536, 1536], P('tp', 'wide')
- ln3_gain_grad: float32 [1536], replicated
- ln3_bias_grad: float32 [1536], replicated
- fc_in_grad: float32 [1536, 6144], P('wide', 'tp')
- fc_out_grad: float32 [6144, 1536], P('tp', 'wide')
The draws below stay inside these ranges and needn't reach their ends.
Inputs may be any that keep to these rules, and one draw needn't show every extreme that they name: clip_start gives, for every block, the frame at which the block's new clip begins.
All inputs are finite; a program needn't handle non-finite values.
Results may differ from the reference program's by a relative error of at most 0.02.
Values may be sent and summed in bfloat16 or wider, within the bound.
No kernel may reach another device: no remote copies, remote signals or barrier semaphores. Data moves between devices by JAX's collectives and lax.ppermute only.
A program may use at most 320 MiB of HBM per device.

```python
import jax
import jax.numpy as jnp
from jax import lax

D = 1536
HEADS = 24
HEAD_DIM = 64
FF = 6144
TEXT = 64
BLOCK_ROWS = 1536
FRAMES = 12288
TEXT_ROWS = 512
N_WIDE = 8


def set_ends(values, stream_key, low, high):
    index_at = [jax.random.randint(jax.random.fold_in(stream_key, axis), (), 0, length) for axis, length in enumerate(values.shape)]
    main_axis = values.shape.index(max(values.shape))
    neighbour = index_at[:main_axis] + [(index_at[main_axis] + 1) % values.shape[main_axis]] + index_at[main_axis + 1:]
    return values.at[tuple(index_at)].set(low).at[tuple(neighbour)].set(high)


def block_levels(own_key, extent, shards, smallest, largest):
    level = 1.0
    for axis_at, shards_of in shards:
        steps = jax.random.uniform(jax.random.fold_in(jax.random.fold_in(own_key, 6), axis_at), (shards_of,), jnp.float32, smallest / len(shards), largest / len(shards))
        level = level * jnp.repeat(jnp.exp(steps), extent[axis_at] // shards_of).reshape((-1,) + (1,) * (len(extent) - 1 - axis_at))
    return level


def bell_draw(own_key, shape, scale, most, split=(), kind=jnp.bfloat16):
    drawn = scale * jax.random.normal(own_key, shape, jnp.float32)
    if split:
        drawn = drawn * block_levels(own_key, shape, split, -0.22, 0.18)
    return jnp.clip(drawn, -most, most).astype(kind)


def setup_inputs(seed: int = 0) -> dict:
    arg_keys = jax.random.split(jax.random.key(seed), 21)
    tokens = bell_draw(arg_keys[0], (FRAMES, D), 1.0, 6.0, ((0, 32),))
    text_states = bell_draw(arg_keys[1], (TEXT_ROWS, D), 1.0, 6.0, ((0, 8),))
    clip_start = set_ends(jax.random.randint(arg_keys[2], (N_WIDE,), BLOCK_ROWS // 3, 2 * BLOCK_ROWS // 3), jax.random.fold_in(arg_keys[2], 1), BLOCK_ROWS // 3, (2 * BLOCK_ROWS // 3) - 1).astype(jnp.int32)
    ln1_gain = jnp.clip(1.0 + 0.1 * jax.random.normal(arg_keys[3], (D,), jnp.float32), 0.5, 1.5)
    ln1_bias = bell_draw(arg_keys[4], (D,), 0.5, 3.0, (), jnp.float32)
    self_query = bell_draw(arg_keys[5], (D, D), D ** -0.5, 0.15625, ((0, 8), (1, 4)))
    self_key = bell_draw(arg_keys[6], (D, D), D ** -0.5, 0.15625, ((0, 8), (1, 4)))
    self_value = bell_draw(arg_keys[7], (D, D), D ** -0.5, 0.15625, ((0, 8), (1, 4)))
    self_out = bell_draw(arg_keys[8], (D, D), (max(D * 6 // BLOCK_ROWS, 2)) ** -0.5, 2.5, ((0, 4), (1, 8)))
    ln2_gain = jnp.clip(1.0 + 0.1 * jax.random.normal(arg_keys[9], (D,), jnp.float32), 0.5, 1.5)
    ln2_bias = bell_draw(arg_keys[10], (D,), 0.5, 3.0, (), jnp.float32)
    cross_query = bell_draw(arg_keys[11], (D, D), D ** -0.5, 0.15625, ((0, 8), (1, 4)))
    cross_key = bell_draw(arg_keys[12], (D, D), D ** -0.5, 0.15625, ((0, 8), (1, 4)))
    cross_value = bell_draw(arg_keys[13], (D, D), D ** -0.5, 0.15625, ((0, 8), (1, 4)))
    cross_out = bell_draw(arg_keys[14], (D, D), (max(D * 2 // TEXT, 2)) ** -0.5, 0.875, ((0, 4), (1, 8)))
    ln3_gain = jnp.clip(1.0 + 0.1 * jax.random.normal(arg_keys[15], (D,), jnp.float32), 0.5, 1.5)
    ln3_bias = bell_draw(arg_keys[16], (D,), 0.5, 3.0, (), jnp.float32)
    fc_in = bell_draw(arg_keys[17], (D, FF), D ** -0.5, 0.15625, ((0, 8), (1, 4)))
    fc_out = bell_draw(arg_keys[18], (FF, D), FF ** -0.5, 0.078125, ((0, 4), (1, 8)))
    out_grad = bell_draw(arg_keys[19], (FRAMES, D), 1.0, 6.0, ((0, 32),))
    return {"tokens": tokens, "text_states": text_states, "clip_start": clip_start, "ln1_gain": ln1_gain, "ln1_bias": ln1_bias, "self_query": self_query, "self_key": self_key, "self_value": self_value, "self_out": self_out, "ln2_gain": ln2_gain, "ln2_bias": ln2_bias, "cross_query": cross_query, "cross_key": cross_key, "cross_value": cross_value, "cross_out": cross_out, "ln3_gain": ln3_gain, "ln3_bias": ln3_bias, "fc_in": fc_in, "fc_out": fc_out, "out_grad": out_grad}


@jax.custom_vjp
def low(v):
    return lax.optimization_barrier(v.astype(jnp.bfloat16)).astype(jnp.float32)

@jax.custom_vjp
def low_back(v):
    return v

def low_keep(v):
    return (low(v), None)

def low_pass(kept, grad):
    return (grad,)

def back_keep(v):
    return (v, None)

def back_low(kept, grad):
    return (low(grad),)
low.defvjp(low_keep, low_pass)
low_back.defvjp(back_keep, back_low)
epsilon = 1e-05
masked_score = -1e+30

def layer_norm(value, gain, shift):
    mean = lax.optimization_barrier(jnp.mean(value, axis=-1, keepdims=True))
    centred = value - mean
    spread = lax.optimization_barrier(jnp.mean(centred * centred, axis=-1, keepdims=True))
    return centred * lax.rsqrt(spread + epsilon) * gain + shift

def self_allowed(rows, here, before, width):
    places = lax.iota(jnp.int32, 2 * width) - width
    first = jnp.where(rows >= here, here, before - width)
    return (places[None, :] <= rows[:, None]) & (places[None, :] >= first[:, None])

def cross_allowed(rows, here, count):
    places = lax.iota(jnp.int32, 2 * count)
    return jnp.where(rows[:, None] < here, places[None, :] < count, places[None, :] >= count)

def matmul(left, right):
    return jnp.dot(left, right, precision=lax.Precision.HIGHEST)

def attend_rows(query, keys, values, allowed):
    factor = query.shape[-1] ** (-0.5)
    scores = low_back(jnp.einsum('qhe,khe->hqk', query, keys, precision=lax.Precision.HIGHEST) * factor)
    scores = jnp.where(allowed[None], scores, masked_score)
    probs = low(jax.nn.softmax(scores, axis=-1))
    return jnp.einsum('hqk,khe->qhe', probs, values, precision=lax.Precision.HIGHEST)

def attend_all(query, keys, values, here, before, allowed_fn):
    width = query.shape[1]
    step = min(512, width)

    def one_block(items):
        block_query, block_keys, block_values, block_here, block_before = items

        def one_rows(index):
            rows = index * step + lax.iota(jnp.int32, step)
            part = lax.dynamic_slice_in_dim(block_query, index * step, step, 0)
            return attend_rows(part, block_keys, block_values, allowed_fn(rows, block_here, block_before))
        mixed = lax.map(jax.checkpoint(one_rows), jnp.arange(width // step, dtype=jnp.int32))
        return mixed.reshape(block_query.shape)
    return lax.map(jax.checkpoint(one_block), (query, keys, values, here, before))

def reference(tokens, text_states, clip_start, ln1_gain, ln1_bias, self_query, self_key, self_value, self_out, ln2_gain, ln2_bias, cross_query, cross_key, cross_value, cross_out, ln3_gain, ln3_bias, fc_in, fc_out, out_grad):
    width = BLOCK_ROWS
    count = TEXT
    here = clip_start
    before = jnp.roll(clip_start, 1)

    def blocks(flat, size):
        return flat.reshape(N_WIDE, size, HEADS, HEAD_DIM)

    def with_prev(flat, size):
        shaped = blocks(flat, size)
        return jnp.concatenate([jnp.roll(shaped, 1, axis=0), shaped], axis=1)

    def self_mask(rows, block_here, block_before):
        return self_allowed(rows, block_here, block_before, width)

    def cross_mask(rows, block_here, block_before):
        return cross_allowed(rows, block_here, count)

    def forward(x, text, g1, b1, wq, wk, wv, wo, g2, b2, cq, ck, cv, co, g3, b3, wi, wf):
        a1 = low(layer_norm(x, g1, b1))
        query = low(low_back(matmul(a1, wq)))
        keys = low(low_back(matmul(a1, wk)))
        values = low(low_back(matmul(a1, wv)))
        text_keys = low(low_back(matmul(text, ck)))
        text_values = low(low_back(matmul(text, cv)))
        mixed = attend_all(blocks(query, width), with_prev(keys, width), with_prev(values, width), here, before, self_mask)
        mixed = low(low_back(mixed.reshape(FRAMES, D)))
        hidden1 = x + low_back(matmul(mixed, wo))
        a2 = low(layer_norm(hidden1, g2, b2))
        cross_q = low(low_back(matmul(a2, cq)))
        cmix = attend_all(blocks(cross_q, width), with_prev(text_keys, count), with_prev(text_values, count), here, before, cross_mask)
        cmix = low(low_back(cmix.reshape(FRAMES, D)))
        hidden2 = hidden1 + low_back(matmul(cmix, co))
        a3 = low(layer_norm(hidden2, g3, b3))
        inner = low_back(matmul(a3, wi))
        active = low(jax.nn.gelu(inner, approximate=False))
        return hidden2 + low_back(matmul(active, wf))
    primal = (tokens.astype(jnp.float32), text_states.astype(jnp.float32), ln1_gain, ln1_bias, self_query.astype(jnp.float32), self_key.astype(jnp.float32), self_value.astype(jnp.float32), self_out.astype(jnp.float32), ln2_gain, ln2_bias, cross_query.astype(jnp.float32), cross_key.astype(jnp.float32), cross_value.astype(jnp.float32), cross_out.astype(jnp.float32), ln3_gain, ln3_bias, fc_in.astype(jnp.float32), fc_out.astype(jnp.float32))
    result, pull = jax.vjp(forward, *primal)
    grads = pull(out_grad.astype(jnp.float32))
    return (result.astype(jnp.bfloat16), grads[0], grads[1], grads[2], grads[3], grads[4], grads[5], grads[6], grads[7], grads[8], grads[9], grads[10], grads[11], grads[12], grads[13], grads[14], grads[15], grads[16], grads[17])
```

```python
import functools

import jax
import jax.numpy as jnp
from jax import lax
from jax.experimental import pallas as pl
from jax.experimental.pallas import tpu as pltpu
from jax.sharding import PartitionSpec as P

HEAD_DIM = 64
PAIR = 2 * HEAD_DIM
LOG2E = 1.4426950408889634
MIN_START = 512

epsilon = 1e-05
masked_score = -1e30


def nn(a, b):
    return lax.dot_general(a, b, (((1,), (0,)), ((), ())), preferred_element_type=jnp.float32)


def nt(a, b):
    return lax.dot_general(a, b, (((1,), (1,)), ((), ())), preferred_element_type=jnp.float32)


def lanes_of(value, head):
    lane = lax.broadcasted_iota(jnp.int32, value.shape, 1)
    return jnp.where((lane >= head * HEAD_DIM) & (lane < (head + 1) * HEAD_DIM), value, 0).astype(value.dtype)


def half(ref, head):
    return slice(head * HEAD_DIM, (head + 1) * HEAD_DIM)


def first_of(rows, here, before, width):
    return jnp.where(rows >= here, here, before - width)


def self_fwd_kernel(tq, tk, skip, start_ref, q_ref, k_ref, v_ref, kp_ref, vp_ref, o_ref, ot_ref, l_ref, vt_ref, vpt_ref):
    width, old = q_ref.shape[0], kp_ref.shape[0]
    here, before = start_ref[0], start_ref[1]
    factor = HEAD_DIM ** (-0.5) * LOG2E
    vt_ref[...] = v_ref[...].T
    vpt_ref[...] = vp_ref[...].T
    for i in range(width // tq):
        rows = i * tq + lax.broadcasted_iota(jnp.int32, (1, tq), 1)
        first = first_of(rows, here, before, width)
        query = q_ref[i * tq:(i + 1) * tq, :]

        def tile(key_ref, value_ref, j, place, causal, carry):
            at = pl.multiple_of(j * tk, tk)
            keys = key_ref[pl.ds(at, tk), :]
            places = place + j * tk + lax.broadcasted_iota(jnp.int32, (tk, 1), 0)
            allowed = places >= first
            if causal:
                allowed = allowed & (places <= rows)
            out = []
            for head in range(2):
                top, total, acc = carry[head]
                scores = jnp.where(allowed, nt(lanes_of(keys, head), query) * factor, masked_score)
                peak = jnp.maximum(top, jnp.max(scores, axis=0, keepdims=True))
                shrink = jnp.exp2(top - peak)
                probs = jnp.exp2(scores - peak)
                total = total * shrink + jnp.sum(probs, axis=0, keepdims=True)
                part = nn(value_ref[half(value_ref, head), pl.ds(at, tk)], probs.astype(jnp.bfloat16))
                out.append((peak, total, acc * shrink + part))
            return tuple(out)

        carry = tuple(
            (jnp.full((1, tq), masked_score, jnp.float32), jnp.zeros((1, tq), jnp.float32), jnp.zeros((HEAD_DIM, tq), jnp.float32))
            for _ in range(2)
        )
        own_low = 0
        if i * tq < skip + old:
            low = jnp.where(here > i * tq, (before - skip) // tk, old // tk)
            carry = lax.fori_loop(low, old // tk, lambda j, c: tile(kp_ref, vpt_ref, j, skip - width, False, c), carry)
        own_low = jnp.where(here > i * tq, 0, here // tk)
        carry = lax.fori_loop(own_low, i * tq // tk, lambda j, c: tile(k_ref, vt_ref, j, 0, False, c), carry)
        for j in range(i * tq // tk, (i + 1) * tq // tk):
            carry = tile(k_ref, vt_ref, j, 0, True, carry)
        for head in range(2):
            top, total, acc = carry[head]
            ot_ref[half(ot_ref, head), i * tq:(i + 1) * tq] = acc / total
            l_ref[0, head:head + 1, i * tq:(i + 1) * tq] = top + jnp.log2(total)
    o_ref[...] = ot_ref[...].T.astype(jnp.bfloat16)


def self_fwd(start, query, kv, kv_old, tq=512, tk=512, interpret=False):
    width, cols = query.shape
    old = kv_old.shape[0]
    pairs = cols // PAIR
    return pl.pallas_call(
        functools.partial(self_fwd_kernel, tq, tk, width - old),
        grid=(pairs,),
        in_specs=[
            pl.BlockSpec(memory_space=pltpu.SMEM),
            pl.BlockSpec((width, PAIR), lambda p: (0, p)),
            pl.BlockSpec((width, PAIR), lambda p: (0, p)),
            pl.BlockSpec((width, PAIR), lambda p: (0, p + pairs)),
            pl.BlockSpec((old, PAIR), lambda p: (0, p)),
            pl.BlockSpec((old, PAIR), lambda p: (0, p + pairs)),
        ],
        out_specs=[
            pl.BlockSpec((width, PAIR), lambda p: (0, p)),
            pl.BlockSpec((PAIR, width), lambda p: (p, 0)),
            pl.BlockSpec((1, 8, width), lambda p: (p, 0, 0)),
        ],
        out_shape=[
            jax.ShapeDtypeStruct((width, cols), jnp.bfloat16),
            jax.ShapeDtypeStruct((cols, width), jnp.float32),
            jax.ShapeDtypeStruct((pairs, 8, width), jnp.float32),
        ],
        scratch_shapes=[pltpu.VMEM((PAIR, width), jnp.bfloat16), pltpu.VMEM((PAIR, old), jnp.bfloat16)],
        compiler_params=pltpu.CompilerParams(vmem_limit_bytes=40 * 2**20),
        cost_estimate=pl.CostEstimate(flops=8 * 10**9, bytes_accessed=12 * 10**6, transcendentals=0),
        name="self_fwd",
        interpret=interpret,
    )(start, query, kv, kv, kv_old, kv_old)


def self_bwd_kernel(tq, tk, skip, old, start_ref, q_ref, k_ref, v_ref, go_ref, ot_ref, l_ref, *rest):
    if old:
        gkv_ref, gq_ref, kt_ref, delta_ref = rest
    else:
        gq_in_ref, gkv_ref, gq_ref, kt_ref, delta_ref, sum_ref = rest
    width, count = q_ref.shape[0], k_ref.shape[0]
    here, before = start_ref[0], start_ref[1]
    factor = HEAD_DIM ** (-0.5) * LOG2E
    kt_ref[...] = k_ref[...].T
    got = go_ref[...].T.astype(jnp.float32) * ot_ref[...]
    for head in range(2):
        delta_ref[head:head + 1, :] = jnp.sum(got[half(got, head), :], axis=0, keepdims=True)
    acc_ref = gq_ref if old else sum_ref
    acc_ref[...] = jnp.zeros_like(acc_ref) if old else gq_in_ref[...]
    for j in range(count // tk):
        place = j * tk + (skip - width if old else 0)
        keys = k_ref[j * tk:(j + 1) * tk, :]
        values = v_ref[j * tk:(j + 1) * tk, :]
        keys_of = [lanes_of(keys, head) for head in range(2)]
        values_of = [lanes_of(values, head) for head in range(2)]
        places = place + lax.broadcasted_iota(jnp.int32, (tk, 1), 0)

        def tile(i, causal, carry):
            at = pl.multiple_of(i * tq, tq)
            query = q_ref[pl.ds(at, tq), :]
            grad = go_ref[pl.ds(at, tq), :]
            rows = i * tq + lax.broadcasted_iota(jnp.int32, (1, tq), 1)
            allowed = places >= first_of(rows, here, before, width)
            if causal:
                allowed = allowed & (places <= rows)
            grad_keys, grad_values = carry
            for head in range(2):
                scores = nt(keys_of[head], query) * factor - l_ref[0, head:head + 1, pl.ds(at, tq)]
                probs = jnp.where(allowed, jnp.exp2(scores), 0.0)
                grad_probs = nt(values_of[head], grad)
                grad_scores = (probs * (grad_probs - delta_ref[head:head + 1, pl.ds(at, tq)])).astype(jnp.bfloat16)
                grad_values = grad_values + nn(probs.astype(jnp.bfloat16), lanes_of(grad, head))
                grad_keys = grad_keys + nn(grad_scores, lanes_of(query, head))
                acc_ref[half(acc_ref, head), pl.ds(at, tq)] += nn(kt_ref[half(kt_ref, head), j * tk:(j + 1) * tk], grad_scores)
            return (grad_keys, grad_values)

        zero = jnp.zeros((tk, PAIR), jnp.float32)
        carry = (zero, zero)
        if old:
            high = jnp.where(before < place + tk + width, (here + tq - 1) // tq, 0)
            carry = lax.fori_loop(0, high, lambda i, c: tile(i, False, c), carry)
        else:
            low = place // tq
            high = jnp.where(here >= place + tk, (here + tq - 1) // tq, width // tq)
            carry = tile(low, True, carry)
            carry = lax.fori_loop(low + 1, high, lambda i, c: tile(i, False, c), carry)
        gkv_ref[0, j * tk:(j + 1) * tk, :] = (carry[0] * HEAD_DIM ** (-0.5)).astype(gkv_ref.dtype)
        gkv_ref[1, j * tk:(j + 1) * tk, :] = carry[1].astype(gkv_ref.dtype)
    if not old:
        gq_ref[...] = (acc_ref[...] * HEAD_DIM ** (-0.5)).T.astype(jnp.bfloat16)


def self_bwd(start, query, kv, grad_mixed, mixed_t, logs, grad_query_t=None, tq=512, tk=512, interpret=False):
    width, cols = query.shape
    old = grad_query_t is None
    count = kv.shape[0]
    pairs = cols // PAIR
    across = pl.BlockSpec((PAIR, width), lambda p: (p, 0))
    along = pl.BlockSpec((width, PAIR), lambda p: (0, p))
    return pl.pallas_call(
        functools.partial(self_bwd_kernel, tq, tk, width - count, old),
        grid=(pairs,),
        in_specs=[
            pl.BlockSpec(memory_space=pltpu.SMEM),
            along,
            pl.BlockSpec((count, PAIR), lambda p: (0, p)),
            pl.BlockSpec((count, PAIR), lambda p: (0, p + pairs)),
            along,
            across,
            pl.BlockSpec((1, 8, width), lambda p: (p, 0, 0)),
        ]
        + ([] if old else [across]),
        out_specs=[pl.BlockSpec((2, count, PAIR), lambda p: (0, 0, p)), across if old else along],
        out_shape=[
            jax.ShapeDtypeStruct((2, count, cols), jnp.bfloat16 if old else jnp.float32),
            jax.ShapeDtypeStruct((cols, width), jnp.float32)
            if old
            else jax.ShapeDtypeStruct((width, cols), jnp.bfloat16),
        ],
        scratch_shapes=[pltpu.VMEM((PAIR, count), jnp.bfloat16), pltpu.VMEM((8, width), jnp.float32)]
        + ([] if old else [pltpu.VMEM((PAIR, width), jnp.float32)]),
        compiler_params=pltpu.CompilerParams(vmem_limit_bytes=40 * 2**20),
        cost_estimate=pl.CostEstimate(flops=8 * 10**9, bytes_accessed=12 * 10**6, transcendentals=0),
        name="self_bwd_old" if old else "self_bwd_own",
        interpret=interpret,
    )(start, query, kv, kv, grad_mixed, mixed_t, logs, *([] if old else [grad_query_t]))


def cross_probs(start_ref, cq, tk_of, count):
    scores = nt(tk_of, cq) * (HEAD_DIM ** (-0.5) * LOG2E)
    rows = start_ref[1] + lax.broadcasted_iota(jnp.int32, (1, cq.shape[0]), 1)
    places = lax.broadcasted_iota(jnp.int32, (2 * count, 1), 0)
    scores = jnp.where((places < count) == (rows < start_ref[0]), scores, masked_score)
    probs = jnp.exp2(scores - jnp.max(scores, axis=0, keepdims=True))
    return probs / jnp.sum(probs, axis=0, keepdims=True)


def cross_fwd_kernel(start_ref, q_ref, k_ref, v_ref, o_ref):
    cq, keys = q_ref[...], k_ref[...]
    values_t = v_ref[...].T
    parts = []
    for head in range(2):
        probs = cross_probs(start_ref, cq, lanes_of(keys, head), keys.shape[0] // 2)
        parts.append(nn(values_t[half(values_t, head), :], probs.astype(jnp.bfloat16)))
    o_ref[...] = jnp.concatenate(parts, 0).T.astype(jnp.bfloat16)


def cross_fwd(start, query, kv, interpret=False):
    rows, cols = query.shape
    keys = kv.shape[0]
    pairs = cols // PAIR
    along = pl.BlockSpec((rows, PAIR), lambda p: (0, p))
    return pl.pallas_call(
        cross_fwd_kernel,
        grid=(pairs,),
        in_specs=[
            pl.BlockSpec(memory_space=pltpu.SMEM),
            along,
            pl.BlockSpec((keys, PAIR), lambda p: (0, p)),
            pl.BlockSpec((keys, PAIR), lambda p: (0, p + pairs)),
        ],
        out_specs=along,
        out_shape=jax.ShapeDtypeStruct((rows, cols), jnp.bfloat16),
        name="cross_fwd",
        interpret=interpret,
    )(start, query, kv, kv)


def cross_bwd_kernel(start_ref, q_ref, k_ref, v_ref, go_ref, gq_ref, gkv_ref):
    cq, keys, values, grad = q_ref[...], k_ref[...], v_ref[...], go_ref[...]
    keys_t = keys.T
    factor = HEAD_DIM ** (-0.5)
    parts = []
    grad_keys = grad_values = 0.0
    for head in range(2):
        probs = cross_probs(start_ref, cq, lanes_of(keys, head), keys.shape[0] // 2)
        grad_probs = nt(lanes_of(values, head), grad)
        total = jnp.sum(probs * grad_probs, axis=0, keepdims=True)
        grad_scores = (probs * (grad_probs - total)).astype(jnp.bfloat16)
        parts.append(nn(keys_t[half(keys_t, head), :], grad_scores))
        grad_keys = grad_keys + nn(grad_scores, lanes_of(cq, head))
        grad_values = grad_values + nn(probs.astype(jnp.bfloat16), lanes_of(grad, head))
    gq_ref[...] = (jnp.concatenate(parts, 0) * factor).T.astype(jnp.bfloat16)
    gkv_ref[0] = grad_keys * factor
    gkv_ref[1] = grad_values


def cross_bwd(start, query, kv, grad_mixed, interpret=False):
    rows, cols = query.shape
    keys = kv.shape[0]
    pairs = cols // PAIR
    along = pl.BlockSpec((rows, PAIR), lambda p: (0, p))
    return pl.pallas_call(
        cross_bwd_kernel,
        grid=(pairs,),
        in_specs=[
            pl.BlockSpec(memory_space=pltpu.SMEM),
            along,
            pl.BlockSpec((keys, PAIR), lambda p: (0, p)),
            pl.BlockSpec((keys, PAIR), lambda p: (0, p + pairs)),
            along,
        ],
        out_specs=[along, pl.BlockSpec((2, keys, PAIR), lambda p: (0, 0, p))],
        out_shape=[
            jax.ShapeDtypeStruct((rows, cols), jnp.bfloat16),
            jax.ShapeDtypeStruct((2, keys, cols), jnp.float32),
        ],
        name="cross_bwd",
        interpret=interpret,
    )(start, query, kv, kv, grad_mixed)


def layer_norm(value, gain, shift):
    mean = jnp.mean(value, axis=-1, keepdims=True)
    centred = value - mean
    spread = jnp.mean(centred * centred, axis=-1, keepdims=True)
    return centred * lax.rsqrt(spread + epsilon) * gain + shift


def norm_back(value, gain, shift, grad):
    return jax.vjp(layer_norm, value, gain, shift)[1](grad)


def turned(value, axis, steps):
    count = lax.axis_size(axis)
    return lax.ppermute(value, axis, [(source, (source + steps) % count) for source in range(count)])


def swapped(value, bit):
    return lax.ppermute(value, "tp", [(source, source ^ bit) for source in range(lax.axis_size("tp"))])


def moved(value, steps):
    count = lax.axis_size("tp")
    pairs = [(source, source + steps) for source in range(count) if 0 <= source + steps < count]
    return lax.ppermute(value, "tp", pairs)


def gathered_rows(value, place):
    count = lax.axis_size("tp")
    rows = value.shape[0]
    out = jnp.zeros((count * rows,) + value.shape[1:], value.dtype)
    put = lambda out, part, at: lax.dynamic_update_slice_in_dim(out, part, (at % count) * rows, 0)
    up, down = [value], [value]
    for _ in range(count - 1):
        up.append(moved(up[-1], 1))
        down.append(moved(down[-1], -1))
    out = put(out, value, place)
    for step in range(1, count):
        part = jnp.where(place >= step, up[step], down[count - step])
        out = put(out, part, place + count - step)
    return out


def exchanged(value, place):
    count = lax.axis_size("tp")
    out = jnp.zeros_like(value)
    own = lax.dynamic_index_in_dim(value, place, 0, keepdims=True)
    out = lax.dynamic_update_slice_in_dim(out, own, place, 0)
    for step in range(1, count):
        part = lax.dynamic_index_in_dim(value, (place + step) % count, 0, keepdims=True)
        out = lax.dynamic_update_slice_in_dim(out, turned(part, "tp", step), (place + count - step) % count, 0)
    return out


def dot(left, right):
    return jnp.dot(left, right, preferred_element_type=jnp.float32)


def dot_rows(left, right):
    return jnp.einsum("ra,rb->ab", left, right, preferred_element_type=jnp.float32)


def dot_last(left, right):
    return jnp.einsum("ra,ba->rb", left, right, preferred_element_type=jnp.float32)


def gelu_and_slope(value):
    chance = 0.5 * lax.erfc(value * -(0.5**0.5))
    density = jnp.exp(-0.5 * value * value) * 0.3989422804014327
    return (value * chance, chance + value * density)


def low(value):
    return value.astype(jnp.bfloat16)


def on_device(
    tokens,
    text_states,
    clip_start,
    ln1_gain,
    ln1_bias,
    self_query,
    self_key,
    self_value,
    self_out,
    ln2_gain,
    ln2_bias,
    cross_query,
    cross_key,
    cross_value,
    cross_out,
    ln3_gain,
    ln3_bias,
    fc_in,
    fc_out,
    out_grad,
):
    place, members = lax.axis_index("wide"), lax.axis_size("wide")
    part, parts = lax.axis_index("tp"), lax.axis_size("tp")
    here = lax.dynamic_index_in_dim(clip_start, place, 0, keepdims=False)
    before = lax.dynamic_index_in_dim(clip_start, (place + members - 1) % members, 0, keepdims=False)
    start = jnp.stack([here, before]).astype(jnp.int32)
    rows, depth = tokens.shape
    width = rows * parts
    cols = self_query.shape[1]
    texts = text_states.shape[0]
    cross_start = jnp.stack([here, part * rows]).astype(jnp.int32)

    weights1 = lax.all_gather(
        jnp.concatenate([self_query, self_key, self_value, cross_key, cross_value], 1), "wide", axis=0, tiled=True
    )
    packed = jnp.concatenate([self_out.T, cross_query, cross_out.T], 1)
    weights2 = lax.all_gather(packed, ("tp", "wide"), axis=0, tiled=True)
    weights2 = weights2.reshape(parts, depth, 3, cols).transpose(2, 1, 0, 3).reshape(3, depth, depth)
    self_out_t, cross_q_full, cross_out_t = weights2[0], weights2[1], weights2[2]
    fc_out_own_t = fc_out.T
    fc_in_half = lax.all_gather(jnp.concatenate([fc_in, swapped(fc_in, 2)], 1), "wide", axis=0, tiled=True)
    fc_out_half_t = lax.all_gather(
        jnp.concatenate([fc_out_own_t, swapped(fc_out_own_t, 2)], 1), "wide", axis=0, tiled=True
    )
    weights_qkv = weights1[:, : 3 * cols]
    weights_kv_text = weights1[:, 3 * cols :]

    block = gathered_rows(tokens, part)
    normed1 = low(layer_norm(block.astype(jnp.float32), ln1_gain, ln1_bias))
    kv = low(dot(normed1, weights_qkv[:, cols:]))
    kv_old = turned(kv[MIN_START:], "wide", 1)
    query = low(dot(normed1, weights_qkv[:, :cols]))
    text_kv = low(dot(text_states, weights_kv_text))
    text_kv = jnp.concatenate([turned(text_kv, "wide", 1), text_kv], 0)
    mixed, mixed_t, logs = self_fwd(start, query, kv, kv_old)
    mixed = exchanged(mixed.reshape(parts, rows, cols), part)
    mixed = mixed.transpose(1, 0, 2).reshape(rows, depth)
    x_in = tokens.astype(jnp.float32)
    hidden1 = x_in + dot_last(mixed, self_out_t)

    text_kv = exchanged(jnp.broadcast_to(text_kv[None], (parts,) + text_kv.shape), part)
    text_kv = text_kv.reshape(parts, 2 * texts, 2, cols).transpose(1, 2, 0, 3).reshape(2 * texts, 2 * depth)
    normed2 = low(layer_norm(hidden1, ln2_gain, ln2_bias))
    cross_q = low(dot(normed2, cross_q_full))
    cmix = cross_fwd(cross_start, cross_q, text_kv)
    hidden2 = hidden1 + dot_last(cmix, cross_out_t)

    normed3 = low(layer_norm(hidden2, ln3_gain, ln3_bias))
    normed3 = jnp.concatenate([normed3, swapped(normed3, 1)], 0)
    inner = dot(normed3, fc_in_half)
    active, slope = gelu_and_slope(inner)
    active = low(active)
    outer = dot_last(active, fc_out_half_t)
    layer_out = low(hidden2 + outer[:rows] + swapped(low(outer[rows:]), 1).astype(jnp.float32))

    grad = out_grad.astype(jnp.float32)
    grad_out = jnp.concatenate([out_grad, swapped(out_grad, 1)], 0)
    grad_fc_out_t = dot_rows(grad_out, active)
    grad_inner = low(dot(grad_out, fc_out_half_t) * slope)
    grad_fc_in = dot_rows(normed3, grad_inner)
    grad_normed3 = dot_last(grad_inner, fc_in_half)
    grad_normed3 = grad_normed3[:rows] + swapped(low(grad_normed3[rows:]), 1).astype(jnp.float32)
    grad_hidden2, grad_g3, grad_b3 = norm_back(hidden2, ln3_gain, ln3_bias, grad_normed3)
    grad = grad + grad_hidden2

    grad_low2 = low(grad)
    grad_cmix = low(dot(grad_low2, cross_out_t))
    grad_cq, grad_text_kv = cross_bwd(cross_start, cross_q, text_kv, grad_cmix)
    grad_cross_out_t = dot_rows(grad_low2, cmix)
    grad_cross_query = dot_rows(normed2, grad_cq)
    grad_hidden1, grad_g2, grad_b2 = norm_back(hidden1, ln2_gain, ln2_bias, dot_last(grad_cq, cross_q_full))
    grad = grad + grad_hidden1

    grad_low1 = low(grad)
    grad_mixed = low(dot(grad_low1, self_out_t))
    grad_self_out_t = dot_rows(grad_low1, mixed)
    grad_mixed = exchanged(grad_mixed.reshape(rows, parts, cols).transpose(1, 0, 2), part).reshape(width, cols)
    grad_kv_old, grad_query_t = self_bwd(start, query, kv_old, grad_mixed, mixed_t, logs)
    grad_kv_back = turned(grad_kv_old, "wide", -1).astype(jnp.float32)
    grad_kv, grad_query = self_bwd(start, query, kv, grad_mixed, mixed_t, logs, grad_query_t)
    grad_kv = jnp.concatenate([grad_kv[:, :MIN_START], grad_kv[:, MIN_START:] + grad_kv_back], 1)
    grad_kv = low(grad_kv)
    grad_qkv = jnp.concatenate([grad_query, grad_kv[0], grad_kv[1]], 1)

    grad_text_kv = low(grad_text_kv).reshape(2, 2 * texts, parts, cols).transpose(2, 1, 0, 3)
    grad_text_kv = jnp.sum(exchanged(grad_text_kv, part).astype(jnp.float32), 0)
    back = turned(low(grad_text_kv[:texts]), "wide", -1).astype(jnp.float32)
    grad_text_kv = low(grad_text_kv[texts:] + back).reshape(texts, 2 * cols)
    text_term = low(dot_last(grad_text_kv, weights_kv_text))
    text_term = exchanged(jnp.broadcast_to(text_term[None], (parts,) + text_term.shape), part)
    text_grad = jnp.sum(text_term.astype(jnp.float32), 0)

    partial = dot_last(grad_qkv, weights_qkv)
    block32 = block.astype(jnp.float32)
    _, grad_g1, grad_b1 = norm_back(block32, ln1_gain, ln1_bias, partial)
    partial = low(partial).reshape(parts // 2, 2, rows, depth)
    mine = lax.dynamic_index_in_dim(partial, part % 2, 1, keepdims=False).astype(jnp.float32)
    theirs = lax.dynamic_index_in_dim(partial, 1 - part % 2, 1, keepdims=False)
    partial = mine + swapped(theirs, 1).astype(jnp.float32)
    mine = lax.dynamic_index_in_dim(partial, part // 2, 0, keepdims=False)
    theirs = lax.dynamic_index_in_dim(partial, 1 - part // 2, 0, keepdims=False)
    grad_normed1 = mine + swapped(low(theirs), 2).astype(jnp.float32)
    tokens_grad = grad + norm_back(x_in, ln1_gain, ln1_bias, grad_normed1)[0]

    def summed(value):
        return lax.psum_scatter(low(value), "wide", scatter_dimension=0, tiled=True)

    def own_half(value):
        mine, theirs = value[:, : value.shape[1] // 2], value[:, value.shape[1] // 2 :]
        return mine.astype(jnp.float32) + swapped(theirs, 2).astype(jnp.float32)

    fc_out_grad = own_half(summed(grad_fc_out_t)).T
    fc_in_grad = own_half(summed(grad_fc_in))
    grads2 = summed(jnp.concatenate([low(grad_self_out_t), low(grad_cross_query), low(grad_cross_out_t)], 1))
    grads2 = grads2.reshape(-1, 3, parts, cols).transpose(2, 0, 1, 3)
    grads2 = jnp.sum(exchanged(grads2, part).astype(jnp.float32), 0)
    grads1 = summed(
        jnp.concatenate([low(dot_rows(normed1, grad_qkv)), low(dot_rows(text_states, grad_text_kv))], 1)
    ).astype(jnp.float32)
    grads1 = [grads1[:, i * cols : (i + 1) * cols] for i in range(5)]

    norms = lax.psum(jnp.stack([grad_g1, grad_b1, grad_g2, grad_b2, grad_g3, grad_b3]), ("wide", "tp"))
    return (
        layer_out,
        tokens_grad,
        text_grad,
        norms[0],
        norms[1],
        grads1[0],
        grads1[1],
        grads1[2],
        grads2[:, 0].T,
        norms[2],
        norms[3],
        grads2[:, 1],
        grads1[3],
        grads1[4],
        grads2[:, 2].T,
        norms[4],
        norms[5],
        fc_in_grad,
        fc_out_grad,
    )


def solution(mesh):
    in_specs = (
        P(("wide", "tp"), None),
        P("wide", None),
        P(),
        P(),
        P(),
        P("wide", "tp"),
        P("wide", "tp"),
        P("wide", "tp"),
        P("tp", "wide"),
        P(),
        P(),
        P("wide", "tp"),
        P("wide", "tp"),
        P("wide", "tp"),
        P("tp", "wide"),
        P(),
        P(),
        P("wide", "tp"),
        P("tp", "wide"),
        P(("wide", "tp"), None),
    )
    out_specs = (
        P(("wide", "tp"), None),
        P(("wide", "tp"), None),
        P("wide", None),
        P(),
        P(),
        P("wide", "tp"),
        P("wide", "tp"),
        P("wide", "tp"),
        P("tp", "wide"),
        P(),
        P(),
        P("wide", "tp"),
        P("wide", "tp"),
        P("wide", "tp"),
        P("tp", "wide"),
        P(),
        P(),
        P("wide", "tp"),
        P("tp", "wide"),
    )
    return jax.shard_map(
        on_device, mesh=mesh, in_specs=in_specs, out_specs=out_specs, check_vma=False
    )
```

```python
import functools

import jax
import jax.numpy as jnp
from jax import lax
from jax.experimental import pallas as pl
from jax.experimental.pallas import tpu as pltpu
from jax.sharding import PartitionSpec as P

HEAD_DIM = 64
PAIR = 2 * HEAD_DIM
LOG2E = 1.4426950408889634
MIN_START = 512
TILE = 512

COST_SCALE = 1.0

epsilon = 1e-05
masked_score = -1e30


def nn(a, b):
    return lax.dot_general(a, b, (((1,), (0,)), ((), ())), preferred_element_type=jnp.float32)


def nt(a, b):
    return lax.dot_general(a, b, (((1,), (1,)), ((), ())), preferred_element_type=jnp.float32)


def low(value):
    return value.astype(jnp.bfloat16)


def lanes_of(value, head):
    lane = lax.broadcasted_iota(jnp.int32, value.shape, 1)
    return jnp.where((lane >= head * HEAD_DIM) & (lane < (head + 1) * HEAD_DIM), value, 0).astype(value.dtype)


def half(head):
    return slice(head * HEAD_DIM, (head + 1) * HEAD_DIM)


def normed(value):
    centred = value - jnp.mean(value, axis=-1, keepdims=True)
    scale = lax.rsqrt(jnp.mean(centred * centred, axis=-1, keepdims=True) + epsilon)
    return centred * scale, scale


def norm_kernel(value, gain, shift):
    return normed(value)[0] * gain + shift


def norm_back_kernel(value, gain, grad):
    unit, scale = normed(value)
    inner = grad * gain
    back = inner - jnp.mean(inner, axis=-1, keepdims=True) - unit * jnp.mean(inner * unit, axis=-1, keepdims=True)
    return back * scale, jnp.sum(grad * unit, axis=0, keepdims=True), jnp.sum(grad, axis=0, keepdims=True)


def params(mib):
    return pltpu.CompilerParams(vmem_limit_bytes=mib * 2**20)


def cost(micros):
    return pl.CostEstimate(flops=int(micros * 1e9 * COST_SCALE), bytes_accessed=0, transcendentals=0)


def once(shape, at):
    return pl.BlockSpec(shape, at, pipeline_mode=pl.Buffered(1))


ANY = pl.BlockSpec(memory_space=pl.ANY)
SMEM = pl.BlockSpec(memory_space=pltpu.SMEM)


def without(kernel, at, count):
    return lambda *refs: kernel(*refs[:at], *refs[at + count:])


def tie_kernel(*refs):
    pass


def tie(value, *tokens, micros=0):
    return pl.pallas_call(
        tie_kernel,
        in_specs=[ANY] * (1 + len(tokens)),
        out_specs=ANY,
        out_shape=jax.ShapeDtypeStruct(value.shape, value.dtype),
        input_output_aliases={0: 0},
        cost_estimate=cost(micros),
        name="tie",
    )(value, *tokens)


def qkv_kernel(count, first, at_ref, *refs):
    blocks, refs = refs[:count], refs[count:]
    gain_ref, shift_ref, w_ref = refs[:3]
    x_ref, a_ref, at_out_ref, qkv_ref, kept_ref = refs[3 if first else 7:]

    @pl.when(pl.program_id(0) == 0)
    def _():
        value = blocks[0][...]
        for index in range(1, count):
            value = jnp.where(at_ref[1] == index, blocks[index][...], value)
        x_ref[...] = value
        kept_ref[...] = low(norm_kernel(value.astype(jnp.float32), gain_ref[...], shift_ref[...]))
        a_ref[...] = kept_ref[...]
        at_out_ref[...] = kept_ref[...].T

    qkv_ref[...] = low(nn(kept_ref[...], w_ref[...]))


def qkv_block(at, blocks, gain, shift, weights, column, width, cols, before, after=()):
    rows, depth = blocks[0].shape
    first = before is None
    count = len(blocks)
    whole = lambda j, at: (0, 0)
    here = lambda j, at: (at[0], 0)
    return pl.pallas_call(
        without(functools.partial(qkv_kernel, count, first), count + (4 if first else 8), len(after)),
        grid_spec=pltpu.PrefetchScalarGridSpec(
            num_scalar_prefetch=1,
            grid=(3,),
            in_specs=[once((rows, depth), whole)] * count
            + [once((1, depth), whole)] * 2
            + [pl.BlockSpec((depth, cols), lambda j, at: (0, column // cols + j))]
            + ([] if first else [ANY] * 4)
            + [ANY] * len(after),
            out_specs=[
                pl.BlockSpec((rows, depth), here),
                pl.BlockSpec((rows, depth), here),
                pl.BlockSpec((depth, rows), lambda j, at: (0, at[0])),
                pl.BlockSpec((rows, cols), lambda j, at: (at[0], j)),
            ],
            scratch_shapes=[pltpu.VMEM((rows, depth), jnp.bfloat16)],
        ),
        out_shape=[
            jax.ShapeDtypeStruct((width, depth), jnp.bfloat16),
            jax.ShapeDtypeStruct((width, depth), jnp.bfloat16),
            jax.ShapeDtypeStruct((depth, width), jnp.bfloat16),
            jax.ShapeDtypeStruct((width, 3 * cols), jnp.bfloat16),
        ],
        input_output_aliases={} if first else {count + 4 + i: i for i in range(4)},
        compiler_params=params(40),
        cost_estimate=cost(0),
        name="qkv_block",
    )(at, *blocks, gain[None], shift[None], weights, *(before or ()), *after)


def first_of(rows, here, before, width):
    return jnp.where(rows >= here, here, before - width)


def self_fwd_kernel(tile_size, skip, start_ref, q_ref, k_ref, v_ref, kp_ref, vp_ref, o_ref, ot_ref, l_ref, vt_ref, vpt_ref):
    width, old = q_ref.shape[0], kp_ref.shape[0]
    size = tile_size
    here, before = start_ref[0], start_ref[1]
    factor = HEAD_DIM ** (-0.5) * LOG2E
    vt_ref[...] = v_ref[...].T
    vpt_ref[...] = vp_ref[...].T
    for i in range(width // size):
        rows = i * size + lax.broadcasted_iota(jnp.int32, (1, size), 1)
        first = first_of(rows, here, before, width)
        query = q_ref[i * size:(i + 1) * size, :]

        def tile(key_ref, value_ref, j, place, causal, carry):
            at = pl.multiple_of(j * size, size)
            keys = key_ref[pl.ds(at, size), :]
            places = place + j * size + lax.broadcasted_iota(jnp.int32, (size, 1), 0)
            allowed = places >= first
            if causal:
                allowed = allowed & (places <= rows)
            out = []
            for head in range(2):
                top, total, acc = carry[head]
                scores = jnp.where(allowed, nt(lanes_of(keys, head), query) * factor, masked_score)
                peak = jnp.maximum(top, jnp.max(scores, axis=0, keepdims=True))
                shrink = jnp.exp2(top - peak)
                probs = jnp.exp2(scores - peak)
                total = total * shrink + jnp.sum(probs, axis=0, keepdims=True)
                part = nn(value_ref[half(head), pl.ds(at, size)], low(probs))
                out.append((peak, total, acc * shrink + part))
            return tuple(out)

        carry = tuple(
            (
                jnp.full((1, size), masked_score, jnp.float32),
                jnp.zeros((1, size), jnp.float32),
                jnp.zeros((HEAD_DIM, size), jnp.float32),
            )
            for _ in range(2)
        )
        if i * size < skip + old:
            start = jnp.where(here > i * size, (before - skip) // size, old // size)
            carry = lax.fori_loop(
                start, old // size, lambda j, c: tile(kp_ref, vpt_ref, j, skip - width, False, c), carry
            )
        start = jnp.where(here > i * size, 0, here // size)
        carry = lax.fori_loop(start, i, lambda j, c: tile(k_ref, vt_ref, j, 0, False, c), carry)
        carry = tile(k_ref, vt_ref, i, 0, True, carry)
        for head in range(2):
            top, total, acc = carry[head]
            ot_ref[half(head), i * size:(i + 1) * size] = acc / total
            l_ref[0, head:head + 1, i * size:(i + 1) * size] = top + jnp.log2(total)
    o_ref[...] = low(ot_ref[...].T)


def self_fwd(start, qkv, kv_old, after):
    width, cols = qkv.shape[0], qkv.shape[1] // 3
    old = kv_old.shape[0]
    pairs = cols // PAIR
    return pl.pallas_call(
        without(functools.partial(self_fwd_kernel, TILE, width - old), 6, len(after)),
        grid=(pairs,),
        in_specs=[
            SMEM,
            pl.BlockSpec((width, PAIR), lambda p: (0, p)),
            pl.BlockSpec((width, PAIR), lambda p: (0, p + pairs)),
            pl.BlockSpec((width, PAIR), lambda p: (0, p + 2 * pairs)),
            pl.BlockSpec((old, PAIR), lambda p: (0, p)),
            pl.BlockSpec((old, PAIR), lambda p: (0, p + pairs)),
        ]
        + [ANY] * len(after),
        out_specs=[
            pl.BlockSpec((width, PAIR), lambda p: (0, p)),
            pl.BlockSpec((PAIR, width), lambda p: (p, 0)),
            pl.BlockSpec((1, 8, width), lambda p: (p, 0, 0)),
        ],
        out_shape=[
            jax.ShapeDtypeStruct((width, cols), jnp.bfloat16),
            jax.ShapeDtypeStruct((cols, width), jnp.float32),
            jax.ShapeDtypeStruct((pairs, 8, width), jnp.float32),
        ],
        scratch_shapes=[pltpu.VMEM((PAIR, width), jnp.bfloat16), pltpu.VMEM((PAIR, old), jnp.bfloat16)],
        compiler_params=params(40),
        cost_estimate=cost(0),
        name="self_fwd",
    )(start, qkv, qkv, qkv, kv_old, kv_old, *after)


def self_bwd_kernel(tile_size, skip, old, start_ref, q_ref, k_ref, v_ref, go0_ref, go1_ref, go2_ref, go3_ref, ot_ref, l_ref, *rest):
    if old:
        gkv_ref, gq_ref, kt_ref, delta_ref, go_ref = rest
    else:
        gq_in_ref, gkv_ref, gq_ref, kt_ref, delta_ref, go_ref, sum_ref = rest
    width, count = q_ref.shape[0], k_ref.shape[0]
    size = tile_size
    here, before, part = start_ref[0], start_ref[1], start_ref[2]
    factor = HEAD_DIM ** (-0.5) * LOG2E
    rows_each = go1_ref.shape[1]
    for step, ref in enumerate((go0_ref, go1_ref, go2_ref, go3_ref)):
        at = pl.multiple_of(lax.rem(part + 4 - step, 4) * rows_each, rows_each)
        go_ref[pl.ds(at, rows_each), :] = ref[part if step == 0 else 0]
    kt_ref[...] = k_ref[...].T
    got = go_ref[...].T.astype(jnp.float32) * ot_ref[...]
    for head in range(2):
        delta_ref[head:head + 1, :] = jnp.sum(got[half(head), :], axis=0, keepdims=True)
    acc_ref = gq_ref if old else sum_ref
    acc_ref[...] = jnp.zeros_like(acc_ref) if old else gq_in_ref[...]
    for j in range(count // size):
        place = j * size + (skip - width if old else 0)
        keys = k_ref[j * size:(j + 1) * size, :]
        values = v_ref[j * size:(j + 1) * size, :]
        keys_of = [lanes_of(keys, head) for head in range(2)]
        values_of = [lanes_of(values, head) for head in range(2)]
        places = place + lax.broadcasted_iota(jnp.int32, (size, 1), 0)

        def tile(i, causal, carry):
            at = pl.multiple_of(i * size, size)
            query = q_ref[pl.ds(at, size), :]
            grad = go_ref[pl.ds(at, size), :]
            rows = i * size + lax.broadcasted_iota(jnp.int32, (1, size), 1)
            allowed = places >= first_of(rows, here, before, width)
            if causal:
                allowed = allowed & (places <= rows)
            grad_keys, grad_values = carry
            for head in range(2):
                scores = nt(keys_of[head], query) * factor - l_ref[0, head:head + 1, pl.ds(at, size)]
                probs = jnp.where(allowed, jnp.exp2(scores), 0.0)
                grad_probs = nt(values_of[head], grad)
                grad_scores = low(probs * (grad_probs - delta_ref[head:head + 1, pl.ds(at, size)]))
                grad_values = grad_values + nn(low(probs), lanes_of(grad, head))
                grad_keys = grad_keys + nn(grad_scores, lanes_of(query, head))
                acc_ref[half(head), pl.ds(at, size)] += nn(kt_ref[half(head), j * size:(j + 1) * size], grad_scores)
            return (grad_keys, grad_values)

        zero = jnp.zeros((size, PAIR), jnp.float32)
        carry = (zero, zero)
        if old:
            high = jnp.where(before < place + size + width, (here + size - 1) // size, 0)
            carry = lax.fori_loop(0, high, lambda i, c: tile(i, False, c), carry)
        else:
            high = jnp.where(here >= place + size, (here + size - 1) // size, width // size)
            carry = tile(j, True, carry)
            carry = lax.fori_loop(j + 1, high, lambda i, c: tile(i, False, c), carry)
        gkv_ref[0, j * size:(j + 1) * size, :] = (carry[0] * HEAD_DIM ** (-0.5)).astype(gkv_ref.dtype)
        gkv_ref[1, j * size:(j + 1) * size, :] = carry[1].astype(gkv_ref.dtype)
    if not old:
        gq_ref[...] = low((acc_ref[...] * HEAD_DIM ** (-0.5)).T)


def self_bwd(start, qkv, kv_old, grads, mixed_t, logs, sums, after):
    width, cols = qkv.shape[0], qkv.shape[1] // 3
    old = kv_old is not None
    count = kv_old.shape[0] if old else width
    pairs = cols // PAIR
    rows = grads[1].shape[1]
    across = pl.BlockSpec((PAIR, width), lambda p: (p, 0))
    along = pl.BlockSpec((width, PAIR), lambda p: (0, p))
    key_at, value_at = (0, pairs) if old else (pairs, 2 * pairs)
    return pl.pallas_call(
        without(functools.partial(self_bwd_kernel, TILE, width - count, old), 10 if old else 11, len(after)),
        grid=(pairs,),
        in_specs=[
            SMEM,
            along,
            pl.BlockSpec((count, PAIR), lambda p: (0, p + key_at)),
            pl.BlockSpec((count, PAIR), lambda p: (0, p + value_at)),
            pl.BlockSpec((4, rows, PAIR), lambda p: (0, 0, p)),
            pl.BlockSpec((1, rows, PAIR), lambda p: (0, 0, p)),
            pl.BlockSpec((1, rows, PAIR), lambda p: (0, 0, p)),
            pl.BlockSpec((1, rows, PAIR), lambda p: (0, 0, p)),
            across,
            pl.BlockSpec((1, 8, width), lambda p: (p, 0, 0)),
        ]
        + ([] if old else [across])
        + [ANY] * len(after),
        out_specs=[pl.BlockSpec((2, count, PAIR), lambda p: (0, 0, p)), across if old else along],
        out_shape=[
            jax.ShapeDtypeStruct((2, count, cols), jnp.bfloat16 if old else jnp.float32),
            jax.ShapeDtypeStruct((cols, width), jnp.float32)
            if old
            else jax.ShapeDtypeStruct((width, cols), jnp.bfloat16),
        ],
        scratch_shapes=[
            pltpu.VMEM((PAIR, count), jnp.bfloat16),
            pltpu.VMEM((8, width), jnp.float32),
            pltpu.VMEM((width, PAIR), jnp.bfloat16),
        ]
        + ([] if old else [pltpu.VMEM((PAIR, width), jnp.float32)]),
        compiler_params=params(40),
        cost_estimate=cost(0 if old else 2000),
        name="self_bwd_old" if old else "self_bwd_own",
    )(start, qkv, *((kv_old,) * 2 if old else (qkv,) * 2), *grads, mixed_t, logs, *([] if old else [sums]), *after)


def cross_probs(here, place, cq, keys_of, count):
    scores = nt(keys_of, cq) * (HEAD_DIM ** (-0.5) * LOG2E)
    rows = place + lax.broadcasted_iota(jnp.int32, (1, cq.shape[0]), 1)
    places = lax.broadcasted_iota(jnp.int32, (2 * count, 1), 0)
    scores = jnp.where((places < count) == (rows < here), scores, masked_score)
    probs = jnp.exp2(scores - jnp.max(scores, axis=0, keepdims=True))
    return probs / jnp.sum(probs, axis=0, keepdims=True)


def chosen(step, refs, own):
    value = own
    for index in range(1, 4):
        value = jnp.where(step == index, refs[index][...], value)
    return value


def middle_fwd_kernel(
    start_ref, x_ref, o0_ref, o1_ref, o2_ref, o3_ref, t0_ref, t1_ref, t2_ref, t3_ref,
    so_ref, cq_ref, co_ref, g2_ref, b2_ref, g3_ref, b3_ref,
    mixed_ref, h1_ref, a2_ref, cq_out_ref, cmix_ref, h2_ref, a3_ref, acc_ref,
):
    i = pl.program_id(0)
    here, part = start_ref[0], start_ref[2]
    rows, cols = o1_ref.shape[1], o1_ref.shape[2]
    t = lax.rem(i, 4)
    step = lax.rem(part + 4 - t, 4)

    @pl.when(i < 4)
    def _():
        piece = o0_ref[0]
        for index, ref in ((1, o1_ref), (2, o2_ref), (3, o3_ref)):
            piece = jnp.where(step == index, ref[0], piece)
        mixed_ref[...] = piece
        term = nt(piece, so_ref[...])

        @pl.when(i == 0)
        def _():
            acc_ref[...] = term + x_ref[...].astype(jnp.float32)

        @pl.when(i > 0)
        def _():
            acc_ref[...] += term

        @pl.when(i == 3)
        def _():
            h1_ref[...] = acc_ref[...]
            a2_ref[...] = low(norm_kernel(acc_ref[...], g2_ref[...], b2_ref[...]))

    @pl.when(i >= 4)
    def _():
        cq = low(nn(a2_ref[...], cq_ref[...]))
        cq_out_ref[...] = cq
        text = chosen(step, (t0_ref, t1_ref, t2_ref, t3_ref), t0_ref[...])
        count = text.shape[0] // 2
        keys, values = text[:, :cols], text[:, cols:]
        parts = []
        for pair in range(cols // PAIR):
            at = slice(pair * PAIR, (pair + 1) * PAIR)
            values_t = values[:, at].T
            for head in range(2):
                probs = cross_probs(here, part * rows, cq[:, at], lanes_of(keys[:, at], head), count)
                parts.append(nn(values_t[half(head), :], low(probs)))
        cmix = low(jnp.concatenate(parts, 0).T)
        cmix_ref[...] = cmix
        acc_ref[...] += nt(cmix, co_ref[...])

        @pl.when(i == 7)
        def _():
            h2_ref[...] = acc_ref[...]
            a3_ref[...] = low(norm_kernel(acc_ref[...], g3_ref[...], b3_ref[...]))


def middle_fwd(start, tokens, mixed, texts, weights, gain2, shift2, gain3, shift3):
    rows, depth = tokens.shape
    cols = mixed[1].shape[2]
    whole = lambda i, s: (0, 0)
    early = lambda i, s: (0, jnp.minimum(i, 3))
    late = lambda i, s: (0, jnp.maximum(i - 4, 0))
    vector = once((1, depth), whole)
    wide16 = jax.ShapeDtypeStruct((rows, depth), jnp.bfloat16)
    wide32 = jax.ShapeDtypeStruct((rows, depth), jnp.float32)
    return pl.pallas_call(
        middle_fwd_kernel,
        grid_spec=pltpu.PrefetchScalarGridSpec(
            num_scalar_prefetch=1,
            grid=(8,),
            in_specs=[once((rows, depth), whole)]
            + [once((1, rows, cols), lambda i, s: (s[2], 0, 0))]
            + [once((1, rows, cols), lambda i, s: (0, 0, 0))] * 3
            + [once(texts[0].shape, whole)] * 4
            + [
                pl.BlockSpec((depth, cols), lambda i, s: (0, 3 * jnp.minimum(i, 3))),
                pl.BlockSpec((depth, cols), lambda i, s: (0, 3 * jnp.maximum(i - 4, 0) + 1)),
                pl.BlockSpec((depth, cols), lambda i, s: (0, 3 * jnp.maximum(i - 4, 0) + 2)),
            ]
            + [vector] * 4,
            out_specs=[
                pl.BlockSpec((rows, cols), early),
                pl.BlockSpec((rows, depth), whole),
                pl.BlockSpec((rows, depth), whole),
                pl.BlockSpec((rows, cols), late),
                pl.BlockSpec((rows, cols), late),
                pl.BlockSpec((rows, depth), whole),
                pl.BlockSpec((rows, depth), whole),
            ],
            scratch_shapes=[pltpu.VMEM((rows, depth), jnp.float32)],
        ),
        out_shape=[wide16, wide32, wide16, wide16, wide16, wide32, wide16],
        compiler_params=params(48),
        cost_estimate=cost(0),
        name="middle_fwd",
    )(start, tokens, *mixed, *texts, weights, weights, weights, gain2[None], shift2[None], gain3[None], shift3[None])


def mlp_kernel(first, a_ref, g_ref, w1_ref, w2_ref, *refs):
    m_ref, gu_ref, ga_ref, y_ref = refs[-4:]
    i = pl.program_id(0)

    @pl.when(i == 0)
    def _():
        if first:
            ga_ref[...] = jnp.zeros_like(ga_ref)
            y_ref[...] = jnp.zeros_like(y_ref)
        else:
            ga_ref[...] = refs[0][...]
            y_ref[...] = refs[1][...]

    w1, w2 = w1_ref[...], w2_ref[...]
    inner = nn(a_ref[...], w1)
    chance = 0.5 + 0.5 * lax.erf(inner * 0.5**0.5)
    active = low(inner * chance)
    slope = chance + inner * (0.3989422804014327 * jnp.exp(-0.5 * inner * inner))
    grad_inner = low(nn(g_ref[...], w2) * slope)
    m_ref[...] = active
    gu_ref[...] = grad_inner
    y_ref[...] += nt(active, w2)
    ga_ref[...] += nt(grad_inner, w1)


def mlp(normed3, grads, weights, units, row, kept, sums, after=()):
    rows, depth = normed3.shape
    size = 512
    first = sums is None
    whole = lambda i: (0, 0)
    full = once((rows, depth), whole)
    extra = [] if first else list(sums)
    count = 4 + len(extra)
    if kept is not None:
        extra += list(kept)
    return pl.pallas_call(
        functools.partial(mlp_kernel, first),
        grid=(units // size,),
        in_specs=[full, full]
        + [pl.BlockSpec((depth, size), lambda i: (0, i)), pl.BlockSpec((depth, size), lambda i: (0, units // size + i))]
        + ([] if first else [full, full])
        + [ANY] * (len(extra) + 4 - count + len(after)),
        out_specs=[pl.BlockSpec((rows, size), lambda i: (row, i))] * 2 + [pl.BlockSpec((rows, depth), whole)] * 2,
        out_shape=[jax.ShapeDtypeStruct((2 * rows, units), jnp.bfloat16)] * 2
        + [jax.ShapeDtypeStruct((rows, depth), jnp.float32)] * 2,
        input_output_aliases={} if kept is None else {count: 0, count + 1: 1},
        compiler_params=params(48),
        cost_estimate=cost(0),
        name="mlp",
    )(normed3, grads, weights, weights, *extra, *after)


def mlp_grads_kernel(a0_ref, a1_ref, g0_ref, g1_ref, gu0_ref, m0_ref, gu1_ref, m1_ref, out_ref, at_ref, gt_ref):
    i = pl.program_id(0)
    steps = pl.num_programs(0) // 4
    rows = a0_ref.shape[0]

    @pl.when(i == 0)
    def _():
        at_ref[:, :rows] = a0_ref[...].T
        at_ref[:, rows:] = a1_ref[...].T
        gt_ref[:, :rows] = g0_ref[...].T
        gt_ref[:, rows:] = g1_ref[...].T

    for index, (left, right) in enumerate(((gt_ref, m0_ref), (at_ref, gu0_ref), (gt_ref, m1_ref), (at_ref, gu1_ref))):

        @pl.when(i // steps == index)
        def _():
            out_ref[...] = low(nn(left[...], right[...]))


def mlp_grads(normed3, grads, grad_inner, active, grad_inner_other, active_other):
    rows, depth = normed3[0].shape
    units = active.shape[1]
    size = 512
    steps = units // size
    full = once((rows, depth), lambda i: (0, 0))
    block = lambda low_step: pl.BlockSpec(
        (2 * rows, size), lambda i: (0, jnp.clip(i - low_step, 0, steps - 1))
    )
    return pl.pallas_call(
        mlp_grads_kernel,
        grid=(4 * steps,),
        in_specs=[full] * 4 + [block(steps), block(0), block(3 * steps), block(2 * steps)],
        out_specs=pl.BlockSpec(
            (depth, size), lambda i: (0, i // (2 * steps) * (2 * steps) + lax.rem(i + steps, 2 * steps))
        ),
        out_shape=jax.ShapeDtypeStruct((depth, 4 * units), jnp.bfloat16),
        scratch_shapes=[pltpu.VMEM((depth, 2 * rows), jnp.bfloat16)] * 2,
        compiler_params=params(48),
        cost_estimate=cost(0),
        name="mlp_grads",
    )(*normed3, *grads, grad_inner, active, grad_inner_other, active_other)


def middle_bwd_kernel(
    start_ref, gy_ref, ga3_ref, got3_ref, h2_ref, h1_ref, cq_in_ref, t0_ref, t1_ref, t2_ref, t3_ref,
    so_ref, cq_ref, co_ref, g2_ref, g3_ref, _,
    g1_ref, g1b_ref, g2b_ref, gcq_ref, gtext_ref, go_ref, norms_ref, grad_ref, acc_ref,
):
    i = pl.program_id(0)
    here, part = start_ref[0], start_ref[2]
    rows, cols = gcq_ref.shape
    step = lax.rem(part + 4 - lax.rem(i, 4), 4)
    factor = HEAD_DIM ** (-0.5)

    @pl.when(i == 0)
    def _():
        back, gain, shift = norm_back_kernel(
            h2_ref[...], g3_ref[...], ga3_ref[...] + got3_ref[...].astype(jnp.float32)
        )
        grad_ref[...] = gy_ref[...].astype(jnp.float32) + back
        g2b_ref[...] = low(grad_ref[...])
        norms_ref[2:3, :] = gain
        norms_ref[3:4, :] = shift
        acc_ref[...] = jnp.zeros_like(acc_ref)

    @pl.when(i < 4)
    def _():
        gco = low(nn(g2b_ref[...], co_ref[...]))
        cq = cq_in_ref[...]
        text = chosen(step, (t0_ref, t1_ref, t2_ref, t3_ref), t0_ref[...])
        count = text.shape[0] // 2
        keys, values = text[:, :cols], text[:, cols:]
        parts = []
        for pair in range(cols // PAIR):
            at = slice(pair * PAIR, (pair + 1) * PAIR)
            keys_t = keys[:, at].T
            grad_keys = grad_values = 0.0
            for head in range(2):
                probs = cross_probs(here, part * rows, cq[:, at], lanes_of(keys[:, at], head), count)
                grad_probs = nt(lanes_of(values[:, at], head), gco[:, at])
                total = jnp.sum(probs * grad_probs, axis=0, keepdims=True)
                grad_scores = low(probs * (grad_probs - total))
                parts.append(nn(keys_t[half(head), :], grad_scores))
                grad_keys = grad_keys + nn(grad_scores, lanes_of(cq[:, at], head))
                grad_values = grad_values + nn(low(probs), lanes_of(gco[:, at], head))
            gtext_ref[0, 0, :, at] = low(grad_keys * factor)
            gtext_ref[0, 1, :, at] = low(grad_values)
        gcq = low((jnp.concatenate(parts, 0) * factor).T)
        gcq_ref[...] = gcq
        acc_ref[...] += nt(gcq, cq_ref[...])

        @pl.when(i == 3)
        def _():
            back, gain, shift = norm_back_kernel(h1_ref[...], g2_ref[...], acc_ref[...])
            grad = grad_ref[...] + back
            g1_ref[...] = grad
            g1b_ref[...] = low(grad)
            norms_ref[0:1, :] = gain
            norms_ref[1:2, :] = shift

    @pl.when(i >= 4)
    def _():
        go_ref[0] = low(nn(g1b_ref[...], so_ref[...]))


def middle_bwd(start, out_grad, grad3, got3, hidden2, hidden1, cross_q, texts, weights, gain2, gain3, token):
    rows, depth = out_grad.shape
    cols = depth // 4
    count = texts[0].shape[0]
    whole = lambda i, s: (0, 0)
    early = lambda i, s: (0, jnp.minimum(i, 3))
    full = pl.BlockSpec((rows, depth), whole)
    vector = once((1, depth), whole)
    wide16 = jax.ShapeDtypeStruct((rows, depth), jnp.bfloat16)
    fixed = once((rows, depth), whole)
    return pl.pallas_call(
        middle_bwd_kernel,
        grid_spec=pltpu.PrefetchScalarGridSpec(
            num_scalar_prefetch=1,
            grid=(8,),
            in_specs=[fixed] * 5
            + [pl.BlockSpec((rows, cols), early)]
            + [once(texts[0].shape, whole)] * 4
            + [
                pl.BlockSpec((depth, cols), lambda i, s: (0, 3 * jnp.maximum(i - 4, 0))),
                pl.BlockSpec((depth, cols), lambda i, s: (0, 3 * jnp.minimum(i, 3) + 1)),
                pl.BlockSpec((depth, cols), lambda i, s: (0, 3 * jnp.minimum(i, 3) + 2)),
            ]
            + [vector] * 2
            + [ANY],
            out_specs=[
                full,
                full,
                full,
                pl.BlockSpec((rows, cols), early),
                pl.BlockSpec((1, 2, count, cols), lambda i, s: (jnp.minimum(i, 3), 0, 0, 0)),
                pl.BlockSpec((1, rows, cols), lambda i, s: (jnp.maximum(i - 4, 0), 0, 0)),
                pl.BlockSpec((8, depth), whole),
            ],
            scratch_shapes=[pltpu.VMEM((rows, depth), jnp.float32)] * 2,
        ),
        out_shape=[
            jax.ShapeDtypeStruct((rows, depth), jnp.float32),
            wide16,
            wide16,
            wide16,
            jax.ShapeDtypeStruct((4, 2, count, cols), jnp.bfloat16),
            jax.ShapeDtypeStruct((4, rows, cols), jnp.bfloat16),
            jax.ShapeDtypeStruct((8, depth), jnp.float32),
        ],
        compiler_params=params(56),
        cost_estimate=cost(2000),
        name="middle_bwd",
    )(start, out_grad, grad3, got3, hidden2, hidden1, cross_q, *texts, weights, weights, weights,
      gain2[None], gain3[None], token)


def middle_grads_kernel(so_l, cq_l, co_l, so_r, cq_r, co_r, out_ref, l_ref):
    i = pl.program_id(0)
    m = lax.rem(i, 3)

    @pl.when(i == 0)
    def _():
        for index, ref in enumerate((so_l, cq_l, co_l)):
            l_ref[index] = ref[...].T

    for index, ref in enumerate((so_r, cq_r, co_r)):

        @pl.when(m == index)
        def _():
            out_ref[...] = low(nn(l_ref[index], ref[...]))


def middle_grads(grad1, normed2, grad2, mixed, grad_cq, cmix):
    rows, depth = normed2.shape
    cols = depth // 4
    full = once((rows, depth), lambda i: (0, 0))
    quarter = pl.BlockSpec((rows, cols), lambda i: (0, i // 3))
    return pl.pallas_call(
        middle_grads_kernel,
        grid=(12,),
        in_specs=[full] * 3 + [quarter] * 3,
        out_specs=pl.BlockSpec((depth, cols), lambda i: (0, i)),
        out_shape=jax.ShapeDtypeStruct((depth, 3 * depth), jnp.bfloat16),
        scratch_shapes=[pltpu.VMEM((3, depth, rows), jnp.bfloat16)],
        compiler_params=params(40),
        cost_estimate=cost(0),
        name="middle_grads",
    )(grad1, normed2, grad2, mixed, grad_cq, cmix)


def block_grad_kernel(order_ref, x_ref, gq_ref, gkv_ref, back_ref, w0_ref, w1_ref, w2_ref, *refs):
    part_ref, g_ref, norms_ref, padded_ref = refs[-4:]
    i = pl.program_id(0)
    rows = x_ref.shape[0]
    skip = padded_ref.shape[1] - back_ref.shape[1]

    @pl.when(i == 0)
    def _():
        padded_ref[:, :skip, :] = jnp.zeros_like(padded_ref[:, :skip, :])
        padded_ref[:, skip:, :] = back_ref[...]
        norms_ref[...] = jnp.zeros_like(norms_ref)

    at = pl.ds(pl.multiple_of(order_ref[i] * rows, rows), rows)
    cols = gq_ref.shape[1]
    total = 0.0
    for index, w_ref in enumerate((w0_ref, w1_ref, w2_ref)):
        grad = gq_ref[...]
        if index:
            grad = low(gkv_ref[index - 1] + padded_ref[index - 1, at, :].astype(jnp.float32))
        g_ref[:, index * cols:(index + 1) * cols] = grad
        total = total + nt(grad, w_ref[...])
    unit, _ = normed(x_ref[...].astype(jnp.float32))
    norms_ref[0:1, :] += jnp.sum(total * unit, axis=0, keepdims=True)
    norms_ref[1:2, :] += jnp.sum(total, axis=0, keepdims=True)
    part_ref[0] = total.astype(part_ref.dtype)


def block_grad(order, block, grad_q, grad_kv, back, weights, column, kind, before, after):
    width, depth = block.shape
    cols = grad_q.shape[1]
    rows = width // 4
    at = lambda i, order: (order[i], 0)
    w_spec = lambda j: once((depth, cols), lambda i, order: (0, column // cols + j))
    extra = ([] if before is None else [before]) + list(after)
    return pl.pallas_call(
        block_grad_kernel,
        grid_spec=pltpu.PrefetchScalarGridSpec(
            num_scalar_prefetch=1,
            grid=(2,),
            in_specs=[
                pl.BlockSpec((rows, depth), at),
                pl.BlockSpec((rows, cols), at),
                pl.BlockSpec((2, rows, cols), lambda i, order: (0, order[i], 0)),
                once(back.shape, lambda i, order: (0, 0, 0)),
                w_spec(0),
                w_spec(1),
                w_spec(2),
            ]
            + [ANY] * len(extra),
            out_specs=[
                pl.BlockSpec((1, rows, depth), lambda i, order: (i, 0, 0)),
                pl.BlockSpec((rows, 3 * cols), at),
                pl.BlockSpec((8, depth), lambda i, order: (0, 0)),
            ],
            scratch_shapes=[pltpu.VMEM((2, width, cols), jnp.bfloat16)],
        ),
        out_shape=[
            jax.ShapeDtypeStruct((2, rows, depth), kind),
            jax.ShapeDtypeStruct((width, 3 * cols), jnp.bfloat16),
            jax.ShapeDtypeStruct((8, depth), jnp.float32),
        ],
        input_output_aliases={} if before is None else {8: 1},
        compiler_params=params(48),
        cost_estimate=cost(0),
        name="block_grad",
    )(order, block, grad_q, grad_kv, back, weights, weights, weights, *extra)


def block_weights_kernel(at_ref, g_ref, text_ref, gtext_ref, out_ref):
    i = pl.program_id(0)

    @pl.when(i < 3)
    def _():
        out_ref[...] = low(nn(at_ref[...], g_ref[...]))

    @pl.when(i >= 3)
    def _():
        out_ref[...] = low(nn(text_ref[...].T, gtext_ref[...]))


def block_weights(normed1_t, grads, text, grad_text, after):
    depth, width = normed1_t.shape
    cols = grads.shape[1] // 3
    whole = lambda i: (0, 0)
    return pl.pallas_call(
        without(block_weights_kernel, 4, len(after)),
        grid=(5,),
        in_specs=[
            once((depth, width), whole),
            pl.BlockSpec((width, cols), lambda i: (0, jnp.minimum(i, 2))),
            once(text.shape, whole),
            pl.BlockSpec((text.shape[0], cols), lambda i: (0, jnp.maximum(i - 3, 0))),
        ]
        + [ANY] * len(after),
        out_specs=pl.BlockSpec((depth, cols), lambda i: (0, i)),
        out_shape=jax.ShapeDtypeStruct((depth, 5 * cols), jnp.bfloat16),
        compiler_params=params(40),
        cost_estimate=cost(0),
        name="block_weights",
    )(normed1_t, grads, text, grad_text, *after)


def layer_norm(value, gain, shift):
    mean = jnp.mean(value, axis=-1, keepdims=True)
    centred = value - mean
    spread = jnp.mean(centred * centred, axis=-1, keepdims=True)
    return centred * lax.rsqrt(spread + epsilon) * gain + shift


def turned(value, axis, steps):
    count = lax.axis_size(axis)
    return lax.ppermute(value, axis, [(source, (source + steps) % count) for source in range(count)])


def swapped(value, bit):
    return lax.ppermute(value, "tp", [(source, source ^ bit) for source in range(lax.axis_size("tp"))])


def moved(value, steps, round_at):
    count = lax.axis_size("tp")
    holders = range(round_at, count - 1) if steps > 0 else range(1, count - round_at)
    return lax.ppermute(value, "tp", [(source, source + steps) for source in holders])


def picked(value, index):
    return lax.dynamic_index_in_dim(value, index % value.shape[0], 0, keepdims=True)


def exchanged(value, place):
    count = lax.axis_size("tp")
    return [value] + [turned(picked(value, place + step), "tp", step) for step in range(1, count)]


def in_order(parts, place):
    out = jnp.zeros((len(parts),) + parts[0].shape, parts[0].dtype)
    for step, part in enumerate(parts):
        out = lax.dynamic_update_slice_in_dim(out, part[None], (place + len(parts) - step) % len(parts), 0)
    return out


def columns_in_order(parts, place):
    columns = parts[0].shape[1]
    out = jnp.zeros((parts[0].shape[0], len(parts) * columns), parts[0].dtype)
    for step, part in enumerate(parts):
        out = lax.dynamic_update_slice_in_dim(out, part, (place + len(parts) - step) % len(parts) * columns, 1)
    return out


def dot(left, right):
    return jnp.dot(left, right, preferred_element_type=jnp.float32)


def dot_last(left, right):
    return jnp.einsum("ra,ba->rb", left, right, preferred_element_type=jnp.float32)


def split_mlp(values):
    return values[:2], values[2], values[3]


def on_device(
    tokens,
    text_states,
    clip_start,
    ln1_gain,
    ln1_bias,
    self_query,
    self_key,
    self_value,
    self_out,
    ln2_gain,
    ln2_bias,
    cross_query,
    cross_key,
    cross_value,
    cross_out,
    ln3_gain,
    ln3_bias,
    fc_in,
    fc_out,
    out_grad,
):
    place, members = lax.axis_index("wide"), lax.axis_size("wide")
    part, parts = lax.axis_index("tp"), lax.axis_size("tp")
    here = lax.dynamic_index_in_dim(clip_start, place, 0, keepdims=False)
    before = lax.dynamic_index_in_dim(clip_start, (place + members - 1) % members, 0, keepdims=False)
    start = jnp.stack([here, before, part]).astype(jnp.int32)
    rows, depth = tokens.shape
    width = rows * parts
    cols, units = self_query.shape[1], fc_in.shape[1]
    texts = text_states.shape[0]
    scalars = lambda *values: jnp.stack([jnp.asarray(value, jnp.int32) for value in values])

    def gathered(value):
        return lax.all_gather(value, "wide", axis=0, tiled=True)

    weights1 = gathered(jnp.concatenate([self_query, self_key, self_value, cross_key, cross_value], 1))
    fc_shards = jnp.concatenate([fc_in, fc_out.T], 1)
    text_at = 3 * cols
    first, last = part == 0, part == parts - 1
    shards = jnp.concatenate([self_out.T, cross_query, cross_out.T], 1)
    ups, downs = [[tokens], [shards]], [[tokens], [shards]]
    for round_at in range(parts - 1):
        for up, down in zip(ups, downs):
            up.append(moved(up[-1], 1, round_at))
            down.append(moved(down[-1], -1, round_at))
    (_, up1, up2, up3), (_, down1, down2, down3) = ups[0], downs[0]
    shards = [shards] + [
        jnp.where(part >= step, ups[1][step], downs[1][parts - step]) for step in range(1, parts)
    ]
    shards = columns_in_order(shards, part)
    weights2 = gathered(shards)
    block = qkv_block(scalars(part, 0), [tokens], ln1_gain, ln1_bias, weights1, 0, width, cols, None)
    at = scalars(jnp.where(first, 1, part - 1), jnp.where(first, 1, 0))
    block = qkv_block(at, [up1, down1], ln1_gain, ln1_bias, weights1, 0, width, cols, block)
    at = scalars((part + 2) % parts, jnp.where(part >= 2, 0, 1))
    block = qkv_block(at, [up2, down2], ln1_gain, ln1_bias, weights1, 0, width, cols, block)
    at = scalars(jnp.where(first, parts - 1, (part + 1) % parts), jnp.where(first, 2, jnp.where(last, 1, 0)))
    text_kv = low(dot(tie(text_states, block[0]), weights1[:, text_at:]))
    text_kv = jnp.concatenate([turned(text_kv, "wide", 1), text_kv], 0)
    block = qkv_block(
        at, [down1, up3, down3], ln1_gain, ln1_bias, weights1, 0, width, cols, block, [text_kv]
    )
    block, _, normed1_t, qkv = block
    kv_old = turned(qkv[MIN_START:, cols:], "wide", 1)
    fc_in_other = swapped(tie(fc_in, up3, down3), 2)
    fc_out_other = swapped(tie(fc_out.T, fc_in_other), 2)
    text_kv = [text_kv] + [turned(text_kv, "tp", step) for step in range(1, parts)]
    mixed, mixed_t, logs = self_fwd(start, qkv, kv_old, [shards, fc_in_other])
    weights_fc = gathered(tie(fc_shards, mixed))
    mixed = exchanged(tie(mixed, *text_kv).reshape(parts, rows, cols), part)
    weights3 = gathered(tie(jnp.concatenate([fc_in_other, fc_out_other], 1), *mixed[1:]))
    grad_out = [out_grad, swapped(tie(out_grad, *mixed[1:]), 1)]
    mixed, hidden1, normed2, cross_q, cmix, hidden2, normed3 = middle_fwd(
        start, tokens, mixed, text_kv, weights2, ln2_gain, ln2_bias, ln3_gain, ln3_bias
    )

    def summed(value):
        return lax.psum_scatter(value, "wide", scatter_dimension=0, tiled=True)

    normed3 = [normed3, swapped(normed3, 1)]
    kept, *sums_own = split_mlp(mlp(normed3[0], grad_out[0], weights_fc, units, 0, None, None))
    kept, *sums_theirs = split_mlp(mlp(normed3[1], grad_out[1], weights_fc, units, 1, kept, None))
    kept_other, *sums_theirs = split_mlp(mlp(normed3[1], grad_out[1], weights3, units, 1, None, sums_theirs, [kept[0]]))
    got3 = swapped(low(sums_theirs[0]), 1)
    kept_other, *sums_own = split_mlp(mlp(normed3[0], grad_out[0], weights3, units, 0, kept_other, sums_own))
    grads_fc = mlp_grads(normed3, grad_out, kept[1], kept[0], kept_other[1], kept_other[0])

    grad1, grad1_low, grad2_low, grad_cq, grad_text, grad_mixed, norms23 = middle_bwd(
        start, out_grad, sums_own[0], got3, hidden2, hidden1, cross_q, text_kv, weights2, ln2_gain, ln3_gain, grads_fc
    )
    grad_mixed = exchanged(grad_mixed, part)
    grads_middle = middle_grads(grad1_low, normed2, grad2_low, mixed, grad_cq, cmix)
    outer = swapped(tie(low(sums_theirs[1]), *grad_mixed[1:]), 1)
    layer_out = low(hidden2 + sums_own[1] + outer.astype(jnp.float32))

    grad_text = exchanged(tie(grad_text, *grad_mixed[1:]), part)
    grad_kv_old, grad_query_t = self_bwd(start, qkv, kv_old, grad_mixed, mixed_t, logs, None, [])
    grad_kv_back = turned(grad_kv_old, "wide", -1)
    grad_text = [tie(picked(grad_text[0], part), grad_query_t)] + grad_text[1:]
    grad_text = sum(piece[0].astype(jnp.float32) for piece in grad_text)
    back = turned(low(grad_text[:, :texts]), "wide", -1).astype(jnp.float32)
    grads_fc = summed(grads_fc)
    fc_own, fc_theirs = grads_fc[:, : 2 * units], grads_fc[:, 2 * units :]
    grad_kv, grad_query = self_bwd(
        start, qkv, None, grad_mixed, mixed_t, logs, grad_query_t, [grad_text, outer, fc_theirs, grads_middle]
    )
    fc_theirs = swapped(fc_theirs, 2)
    grad_text = low(grad_text[:, texts:] + tie(back, grad_query))
    grad_text = jnp.concatenate([grad_text[0], grad_text[1]], 1)

    block_args = (block, grad_query, grad_kv, grad_kv_back, weights1, 0)
    theirs, grad_qkv, norms_theirs = block_grad(
        scalars(1 - part % 2, 3 - part % 2), *block_args, jnp.bfloat16, None, []
    )
    mine, grad_qkv, norms_mine = block_grad(
        scalars(part % 2, 2 + part % 2), *block_args, jnp.float32, grad_qkv, []
    )
    theirs = swapped(theirs, 1)
    grads_block = block_weights(normed1_t, grad_qkv, text_states, grad_text, [])
    norms = jnp.concatenate([norms_theirs[:2] + norms_mine[:2], norms23[:4]], 0)
    norms = norms + swapped(tie(norms, grads_block), 1)
    mine = mine + tie(theirs, grads_block, fc_theirs, norms, micros=2000).astype(jnp.float32)
    norms = norms + swapped(tie(norms, mine), 2)
    theirs = swapped(tie(low(picked(mine, 1 - part // 2)[0]), norms), 2)
    norms = tie(norms, theirs)
    bit = 1
    while bit < members:
        norms = norms + lax.ppermute(norms, "wide", [(source, source ^ bit) for source in range(members)])
        bit *= 2
    grad_normed1 = picked(mine, part // 2)[0] + theirs.astype(jnp.float32)
    x_in = tokens.astype(jnp.float32)
    tokens_grad = grad1 + jax.vjp(lambda value: layer_norm(value, ln1_gain, ln1_bias), x_in)[1](grad_normed1)[0]

    text_term = low(dot_last(grad_text, weights1[:, text_at:]))
    text_term = [text_term] + [turned(text_term, "tp", step) for step in range(1, parts)]
    text_grad = tie(jnp.sum(in_order(text_term, part).astype(jnp.float32), 0), theirs)

    grads_middle = tie(summed(grads_middle), theirs)
    fc_grads = fc_own.astype(jnp.float32) + fc_theirs.astype(jnp.float32)
    fc_in_grad, fc_out_grad = fc_grads[:, :units], fc_grads[:, units:].T
    pieces = [
        lax.dynamic_slice_in_dim(grads_middle, ((part + step) % parts) * 3 * cols, 3 * cols, 1) for step in range(parts)
    ]
    pieces = [pieces[0]] + [turned(pieces[step], "tp", step) for step in range(1, parts)]
    grads_middle = sum(piece.astype(jnp.float32) for piece in pieces)
    grads_middle = [grads_middle[:, i * cols : (i + 1) * cols] for i in range(3)]
    grads_block = tie(summed(grads_block), *pieces[1:]).astype(jnp.float32)
    grads_block = [grads_block[:, i * cols : (i + 1) * cols] for i in range(5)]

    return (
        layer_out,
        tokens_grad,
        text_grad,
        norms[0],
        norms[1],
        grads_block[0],
        grads_block[1],
        grads_block[2],
        grads_middle[0].T,
        norms[2],
        norms[3],
        grads_middle[1],
        grads_block[3],
        grads_block[4],
        grads_middle[2].T,
        norms[4],
        norms[5],
        fc_in_grad,
        fc_out_grad,
    )


def solution(mesh):
    in_specs = (
        P(("wide", "tp"), None),
        P("wide", None),
        P(),
        P(),
        P(),
        P("wide", "tp"),
        P("wide", "tp"),
        P("wide", "tp"),
        P("tp", "wide"),
        P(),
        P(),
        P("wide", "tp"),
        P("wide", "tp"),
        P("wide", "tp"),
        P("tp", "wide"),
        P(),
        P(),
        P("wide", "tp"),
        P("tp", "wide"),
        P(("wide", "tp"), None),
    )
    out_specs = (
        P(("wide", "tp"), None),
        P(("wide", "tp"), None),
        P("wide", None),
        P(),
        P(),
        P("wide", "tp"),
        P("wide", "tp"),
        P("wide", "tp"),
        P("tp", "wide"),
        P(),
        P(),
        P("wide", "tp"),
        P("wide", "tp"),
        P("wide", "tp"),
        P("tp", "wide"),
        P(),
        P(),
        P("wide", "tp"),
        P("tp", "wide"),
    )
    return jax.shard_map(
        on_device, mesh=mesh, in_specs=in_specs, out_specs=out_specs, check_vma=False
    )
```

```python
import functools

import jax
import jax.numpy as jnp
from jax import lax
from jax.experimental import pallas as pl
from jax.experimental.pallas import tpu as pltpu
from jax.sharding import PartitionSpec as P

HEAD_DIM = 64
PAIR = 2 * HEAD_DIM
LOG2E = 1.4426950408889634
MIN_START = 512
TILE = 512

COST_SCALE = 1.0

epsilon = 1e-05
masked_score = -1e30


def nn(a, b):
    return lax.dot_general(a, b, (((1,), (0,)), ((), ())), preferred_element_type=jnp.float32)


def nt(a, b):
    return lax.dot_general(a, b, (((1,), (1,)), ((), ())), preferred_element_type=jnp.float32)


def low(value):
    return value.astype(jnp.bfloat16)


def lanes_of(value, head):
    lane = lax.broadcasted_iota(jnp.int32, value.shape, 1)
    return jnp.where((lane >= head * HEAD_DIM) & (lane < (head + 1) * HEAD_DIM), value, 0).astype(value.dtype)


def half(head):
    return slice(head * HEAD_DIM, (head + 1) * HEAD_DIM)


def normed(value):
    centred = value - jnp.mean(value, axis=-1, keepdims=True)
    scale = lax.rsqrt(jnp.mean(centred * centred, axis=-1, keepdims=True) + epsilon)
    return centred * scale, scale


def norm_kernel(value, gain, shift):
    return normed(value)[0] * gain + shift


def norm_back_kernel(value, gain, grad):
    unit, scale = normed(value)
    inner = grad * gain
    back = inner - jnp.mean(inner, axis=-1, keepdims=True) - unit * jnp.mean(inner * unit, axis=-1, keepdims=True)
    return back * scale, jnp.sum(grad * unit, axis=0, keepdims=True), jnp.sum(grad, axis=0, keepdims=True)


def params(mib):
    return pltpu.CompilerParams(vmem_limit_bytes=mib * 2**20)


def cost(micros):
    return pl.CostEstimate(flops=int(micros * 1e9 * COST_SCALE), bytes_accessed=0, transcendentals=0)


def once(shape, at):
    return pl.BlockSpec(shape, at, pipeline_mode=pl.Buffered(1))


ANY = pl.BlockSpec(memory_space=pl.ANY)
SMEM = pl.BlockSpec(memory_space=pltpu.SMEM)


def without(kernel, at, count):
    return lambda *refs: kernel(*refs[:at], *refs[at + count:])


def tie_kernel(*refs):
    pass


def tie(value, *tokens, micros=0):
    return pl.pallas_call(
        tie_kernel,
        in_specs=[ANY] * (1 + len(tokens)),
        out_specs=ANY,
        out_shape=jax.ShapeDtypeStruct(value.shape, value.dtype),
        input_output_aliases={0: 0},
        cost_estimate=cost(micros),
        name="tie",
    )(value, *tokens)


def qkv_kernel(count, first, at_ref, *refs):
    blocks, refs = refs[:count], refs[count:]
    gain_ref, shift_ref, w_ref = refs[:3]
    x_ref, a_ref, at_out_ref, qkv_ref, kept_ref = refs[3 if first else 7:]

    @pl.when(pl.program_id(0) == 0)
    def _():
        value = blocks[0][...]
        for index in range(1, count):
            value = jnp.where(at_ref[1] == index, blocks[index][...], value)
        x_ref[...] = value
        kept_ref[...] = low(norm_kernel(value.astype(jnp.float32), gain_ref[...], shift_ref[...]))
        a_ref[...] = kept_ref[...]
        at_out_ref[...] = kept_ref[...].T

    qkv_ref[...] = low(nn(kept_ref[...], w_ref[...]))


def qkv_block(at, blocks, gain, shift, weights, column, width, cols, before, after=()):
    rows, depth = blocks[0].shape
    first = before is None
    count = len(blocks)
    whole = lambda j, at: (0, 0)
    here = lambda j, at: (at[0], 0)
    return pl.pallas_call(
        without(functools.partial(qkv_kernel, count, first), count + (4 if first else 8), len(after)),
        grid_spec=pltpu.PrefetchScalarGridSpec(
            num_scalar_prefetch=1,
            grid=(3,),
            in_specs=[once((rows, depth), whole)] * count
            + [once((1, depth), whole)] * 2
            + [pl.BlockSpec((depth, cols), lambda j, at: (0, column // cols + j))]
            + ([] if first else [ANY] * 4)
            + [ANY] * len(after),
            out_specs=[
                pl.BlockSpec((rows, depth), here),
                pl.BlockSpec((rows, depth), here),
                pl.BlockSpec((depth, rows), lambda j, at: (0, at[0])),
                pl.BlockSpec((rows, cols), lambda j, at: (at[0], j)),
            ],
            scratch_shapes=[pltpu.VMEM((rows, depth), jnp.bfloat16)],
        ),
        out_shape=[
            jax.ShapeDtypeStruct((width, depth), jnp.bfloat16),
            jax.ShapeDtypeStruct((width, depth), jnp.bfloat16),
            jax.ShapeDtypeStruct((depth, width), jnp.bfloat16),
            jax.ShapeDtypeStruct((width, 3 * cols), jnp.bfloat16),
        ],
        input_output_aliases={} if first else {count + 4 + i: i for i in range(4)},
        compiler_params=params(40),
        cost_estimate=cost(0),
        name="qkv_block",
    )(at, *blocks, gain[None], shift[None], weights, *(before or ()), *after)


def first_of(rows, here, before, width):
    return jnp.where(rows >= here, here, before - width)


def self_fwd_kernel(tile_size, skip, start_ref, q_ref, k_ref, v_ref, kp_ref, vp_ref, o_ref, ot_ref, l_ref, vt_ref, vpt_ref):
    width, old = q_ref.shape[0], kp_ref.shape[0]
    size = tile_size
    here, before = start_ref[0], start_ref[1]
    factor = HEAD_DIM ** (-0.5) * LOG2E
    vt_ref[...] = v_ref[...].T
    vpt_ref[...] = vp_ref[...].T
    for i in range(width // size):
        rows = i * size + lax.broadcasted_iota(jnp.int32, (1, size), 1)
        first = first_of(rows, here, before, width)
        query = q_ref[i * size:(i + 1) * size, :]

        def tile(key_ref, value_ref, j, place, causal, carry):
            at = pl.multiple_of(j * size, size)
            keys = key_ref[pl.ds(at, size), :]
            places = place + j * size + lax.broadcasted_iota(jnp.int32, (size, 1), 0)
            allowed = places >= first
            if causal:
                allowed = allowed & (places <= rows)
            out = []
            for head in range(2):
                top, total, acc = carry[head]
                scores = jnp.where(allowed, nt(lanes_of(keys, head), query) * factor, masked_score)
                peak = jnp.maximum(top, jnp.max(scores, axis=0, keepdims=True))
                shrink = jnp.exp2(top - peak)
                probs = jnp.exp2(scores - peak)
                total = total * shrink + jnp.sum(probs, axis=0, keepdims=True)
                part = nn(value_ref[half(head), pl.ds(at, size)], low(probs))
                out.append((peak, total, acc * shrink + part))
            return tuple(out)

        carry = tuple(
            (
                jnp.full((1, size), masked_score, jnp.float32),
                jnp.zeros((1, size), jnp.float32),
                jnp.zeros((HEAD_DIM, size), jnp.float32),
            )
            for _ in range(2)
        )
        if i * size < skip + old:
            start = jnp.where(here > i * size, (before - skip) // size, old // size)
            carry = lax.fori_loop(
                start, old // size, lambda j, c: tile(kp_ref, vpt_ref, j, skip - width, False, c), carry
            )
        start = jnp.where(here > i * size, 0, here // size)
        carry = lax.fori_loop(start, i, lambda j, c: tile(k_ref, vt_ref, j, 0, False, c), carry)
        carry = tile(k_ref, vt_ref, i, 0, True, carry)
        for head in range(2):
            top, total, acc = carry[head]
            ot_ref[half(head), i * size:(i + 1) * size] = acc / total
            l_ref[0, head:head + 1, i * size:(i + 1) * size] = top + jnp.log2(total)
    o_ref[...] = low(ot_ref[...].T)


def self_fwd(start, qkv, kv_old, after):
    width, cols = qkv.shape[0], qkv.shape[1] // 3
    old = kv_old.shape[0]
    pairs = cols // PAIR
    return pl.pallas_call(
        without(functools.partial(self_fwd_kernel, TILE, width - old), 6, len(after)),
        grid=(pairs,),
        in_specs=[
            SMEM,
            pl.BlockSpec((width, PAIR), lambda p: (0, p)),
            pl.BlockSpec((width, PAIR), lambda p: (0, p + pairs)),
            pl.BlockSpec((width, PAIR), lambda p: (0, p + 2 * pairs)),
            pl.BlockSpec((old, PAIR), lambda p: (0, p)),
            pl.BlockSpec((old, PAIR), lambda p: (0, p + pairs)),
        ]
        + [ANY] * len(after),
        out_specs=[
            pl.BlockSpec((width, PAIR), lambda p: (0, p)),
            pl.BlockSpec((PAIR, width), lambda p: (p, 0)),
            pl.BlockSpec((1, 8, width), lambda p: (p, 0, 0)),
        ],
        out_shape=[
            jax.ShapeDtypeStruct((width, cols), jnp.bfloat16),
            jax.ShapeDtypeStruct((cols, width), jnp.float32),
            jax.ShapeDtypeStruct((pairs, 8, width), jnp.float32),
        ],
        scratch_shapes=[pltpu.VMEM((PAIR, width), jnp.bfloat16), pltpu.VMEM((PAIR, old), jnp.bfloat16)],
        compiler_params=params(40),
        cost_estimate=cost(0),
        name="self_fwd",
    )(start, qkv, qkv, qkv, kv_old, kv_old, *after)


def self_bwd_kernel(tile_size, skip, old, start_ref, q_ref, k_ref, v_ref, go0_ref, go1_ref, go2_ref, go3_ref, ot_ref, l_ref, *rest):
    if old:
        gkv_ref, gq_ref, kt_ref, delta_ref, go_ref = rest
    else:
        gq_in_ref, gkv_ref, gq_ref, kt_ref, delta_ref, go_ref, sum_ref = rest
    width, count = q_ref.shape[0], k_ref.shape[0]
    size = tile_size
    here, before, part = start_ref[0], start_ref[1], start_ref[2]
    factor = HEAD_DIM ** (-0.5) * LOG2E
    rows_each = go1_ref.shape[1]
    for step, ref in enumerate((go0_ref, go1_ref, go2_ref, go3_ref)):
        at = pl.multiple_of(lax.rem(part + 4 - step, 4) * rows_each, rows_each)
        go_ref[pl.ds(at, rows_each), :] = ref[part if step == 0 else 0]
    kt_ref[...] = k_ref[...].T
    got = go_ref[...].T.astype(jnp.float32) * ot_ref[...]
    for head in range(2):
        delta_ref[head:head + 1, :] = jnp.sum(got[half(head), :], axis=0, keepdims=True)
    acc_ref = gq_ref if old else sum_ref
    acc_ref[...] = jnp.zeros_like(acc_ref) if old else gq_in_ref[...]
    for j in range(count // size):
        place = j * size + (skip - width if old else 0)
        keys = k_ref[j * size:(j + 1) * size, :]
        values = v_ref[j * size:(j + 1) * size, :]
        keys_of = [lanes_of(keys, head) for head in range(2)]
        values_of = [lanes_of(values, head) for head in range(2)]
        places = place + lax.broadcasted_iota(jnp.int32, (size, 1), 0)

        def tile(i, causal, carry):
            at = pl.multiple_of(i * size, size)
            query = q_ref[pl.ds(at, size), :]
            grad = go_ref[pl.ds(at, size), :]
            rows = i * size + lax.broadcasted_iota(jnp.int32, (1, size), 1)
            allowed = places >= first_of(rows, here, before, width)
            if causal:
                allowed = allowed & (places <= rows)
            grad_keys, grad_values = carry
            for head in range(2):
                scores = nt(keys_of[head], query) * factor - l_ref[0, head:head + 1, pl.ds(at, size)]
                probs = jnp.where(allowed, jnp.exp2(scores), 0.0)
                grad_probs = nt(values_of[head], grad)
                grad_scores = low(probs * (grad_probs - delta_ref[head:head + 1, pl.ds(at, size)]))
                grad_values = grad_values + nn(low(probs), lanes_of(grad, head))
                grad_keys = grad_keys + nn(grad_scores, lanes_of(query, head))
                acc_ref[half(head), pl.ds(at, size)] += nn(kt_ref[half(head), j * size:(j + 1) * size], grad_scores)
            return (grad_keys, grad_values)

        zero = jnp.zeros((size, PAIR), jnp.float32)
        carry = (zero, zero)
        if old:
            high = jnp.where(before < place + size + width, (here + size - 1) // size, 0)
            carry = lax.fori_loop(0, high, lambda i, c: tile(i, False, c), carry)
        else:
            high = jnp.where(here >= place + size, (here + size - 1) // size, width // size)
            carry = tile(j, True, carry)
            carry = lax.fori_loop(j + 1, high, lambda i, c: tile(i, False, c), carry)
        gkv_ref[0, j * size:(j + 1) * size, :] = (carry[0] * HEAD_DIM ** (-0.5)).astype(gkv_ref.dtype)
        gkv_ref[1, j * size:(j + 1) * size, :] = carry[1].astype(gkv_ref.dtype)
    if not old:
        gq_ref[...] = low((acc_ref[...] * HEAD_DIM ** (-0.5)).T)


def self_bwd(start, qkv, kv_old, grads, mixed_t, logs, sums, after):
    width, cols = qkv.shape[0], qkv.shape[1] // 3
    old = kv_old is not None
    count = kv_old.shape[0] if old else width
    pairs = cols // PAIR
    rows = grads[1].shape[1]
    across = pl.BlockSpec((PAIR, width), lambda p: (p, 0))
    along = pl.BlockSpec((width, PAIR), lambda p: (0, p))
    key_at, value_at = (0, pairs) if old else (pairs, 2 * pairs)
    return pl.pallas_call(
        without(functools.partial(self_bwd_kernel, TILE, width - count, old), 10 if old else 11, len(after)),
        grid=(pairs,),
        in_specs=[
            SMEM,
            along,
            pl.BlockSpec((count, PAIR), lambda p: (0, p + key_at)),
            pl.BlockSpec((count, PAIR), lambda p: (0, p + value_at)),
            pl.BlockSpec((4, rows, PAIR), lambda p: (0, 0, p)),
            pl.BlockSpec((1, rows, PAIR), lambda p: (0, 0, p)),
            pl.BlockSpec((1, rows, PAIR), lambda p: (0, 0, p)),
            pl.BlockSpec((1, rows, PAIR), lambda p: (0, 0, p)),
            across,
            pl.BlockSpec((1, 8, width), lambda p: (p, 0, 0)),
        ]
        + ([] if old else [across])
        + [ANY] * len(after),
        out_specs=[pl.BlockSpec((2, count, PAIR), lambda p: (0, 0, p)), across if old else along],
        out_shape=[
            jax.ShapeDtypeStruct((2, count, cols), jnp.bfloat16 if old else jnp.float32),
            jax.ShapeDtypeStruct((cols, width), jnp.float32)
            if old
            else jax.ShapeDtypeStruct((width, cols), jnp.bfloat16),
        ],
        scratch_shapes=[
            pltpu.VMEM((PAIR, count), jnp.bfloat16),
            pltpu.VMEM((8, width), jnp.float32),
            pltpu.VMEM((width, PAIR), jnp.bfloat16),
        ]
        + ([] if old else [pltpu.VMEM((PAIR, width), jnp.float32)]),
        compiler_params=params(40),
        cost_estimate=cost(0 if old else 2000),
        name="self_bwd_old" if old else "self_bwd_own",
    )(start, qkv, *((kv_old,) * 2 if old else (qkv,) * 2), *grads, mixed_t, logs, *([] if old else [sums]), *after)


def cross_probs(here, place, cq, keys_of, count):
    scores = nt(keys_of, cq) * (HEAD_DIM ** (-0.5) * LOG2E)
    rows = place + lax.broadcasted_iota(jnp.int32, (1, cq.shape[0]), 1)
    places = lax.broadcasted_iota(jnp.int32, (2 * count, 1), 0)
    scores = jnp.where((places < count) == (rows < here), scores, masked_score)
    probs = jnp.exp2(scores - jnp.max(scores, axis=0, keepdims=True))
    return probs / jnp.sum(probs, axis=0, keepdims=True)


def chosen(step, refs, own):
    value = own
    for index in range(1, 4):
        value = jnp.where(step == index, refs[index][...], value)
    return value


def middle_fwd_kernel(
    start_ref, x_ref, o0_ref, o1_ref, o2_ref, o3_ref, t0_ref, t1_ref, t2_ref, t3_ref,
    so_ref, cq_ref, co_ref, g2_ref, b2_ref, g3_ref, b3_ref,
    mixed_ref, h1_ref, a2_ref, cq_out_ref, cmix_ref, h2_ref, a3_ref, acc_ref,
):
    i = pl.program_id(0)
    here, part = start_ref[0], start_ref[2]
    rows, cols = o1_ref.shape[1], o1_ref.shape[2]
    t = lax.rem(i, 4)
    step = lax.rem(part + 4 - t, 4)

    @pl.when(i < 4)
    def _():
        piece = o0_ref[0]
        for index, ref in ((1, o1_ref), (2, o2_ref), (3, o3_ref)):
            piece = jnp.where(step == index, ref[0], piece)
        mixed_ref[...] = piece
        term = nt(piece, so_ref[...])

        @pl.when(i == 0)
        def _():
            acc_ref[...] = term + x_ref[...].astype(jnp.float32)

        @pl.when(i > 0)
        def _():
            acc_ref[...] += term

        @pl.when(i == 3)
        def _():
            h1_ref[...] = acc_ref[...]
            a2_ref[...] = low(norm_kernel(acc_ref[...], g2_ref[...], b2_ref[...]))

    @pl.when(i >= 4)
    def _():
        cq = low(nn(a2_ref[...], cq_ref[...]))
        cq_out_ref[...] = cq
        text = chosen(step, (t0_ref, t1_ref, t2_ref, t3_ref), t0_ref[...])
        count = text.shape[0] // 2
        keys, values = text[:, :cols], text[:, cols:]
        parts = []
        for pair in range(cols // PAIR):
            at = slice(pair * PAIR, (pair + 1) * PAIR)
            values_t = values[:, at].T
            for head in range(2):
                probs = cross_probs(here, part * rows, cq[:, at], lanes_of(keys[:, at], head), count)
                parts.append(nn(values_t[half(head), :], low(probs)))
        cmix = low(jnp.concatenate(parts, 0).T)
        cmix_ref[...] = cmix
        acc_ref[...] += nt(cmix, co_ref[...])

        @pl.when(i == 7)
        def _():
            h2_ref[...] = acc_ref[...]
            a3_ref[...] = low(norm_kernel(acc_ref[...], g3_ref[...], b3_ref[...]))


def middle_fwd(start, tokens, mixed, texts, weights, gain2, shift2, gain3, shift3):
    rows, depth = tokens.shape
    cols = mixed[1].shape[2]
    whole = lambda i, s: (0, 0)
    early = lambda i, s: (0, jnp.minimum(i, 3))
    late = lambda i, s: (0, jnp.maximum(i - 4, 0))
    vector = once((1, depth), whole)
    wide16 = jax.ShapeDtypeStruct((rows, depth), jnp.bfloat16)
    wide32 = jax.ShapeDtypeStruct((rows, depth), jnp.float32)
    return pl.pallas_call(
        middle_fwd_kernel,
        grid_spec=pltpu.PrefetchScalarGridSpec(
            num_scalar_prefetch=1,
            grid=(8,),
            in_specs=[once((rows, depth), whole)]
            + [once((1, rows, cols), lambda i, s: (s[2], 0, 0))]
            + [once((1, rows, cols), lambda i, s: (0, 0, 0))] * 3
            + [once(texts[0].shape, whole)] * 4
            + [
                pl.BlockSpec((depth, cols), lambda i, s: (jnp.minimum(i, 3), 0)),
                pl.BlockSpec((depth, cols), lambda i, s: (jnp.maximum(i - 4, 0), 1)),
                pl.BlockSpec((depth, cols), lambda i, s: (jnp.maximum(i - 4, 0), 2)),
            ]
            + [vector] * 4,
            out_specs=[
                pl.BlockSpec((rows, cols), early),
                pl.BlockSpec((rows, depth), whole),
                pl.BlockSpec((rows, depth), whole),
                pl.BlockSpec((rows, cols), late),
                pl.BlockSpec((rows, cols), late),
                pl.BlockSpec((rows, depth), whole),
                pl.BlockSpec((rows, depth), whole),
            ],
            scratch_shapes=[pltpu.VMEM((rows, depth), jnp.float32)],
        ),
        out_shape=[wide16, wide32, wide16, wide16, wide16, wide32, wide16],
        compiler_params=params(48),
        cost_estimate=cost(0),
        name="middle_fwd",
    )(start, tokens, *mixed, *texts, weights, weights, weights, gain2[None], shift2[None], gain3[None], shift3[None])


def mlp_kernel(first, a_ref, g_ref, w1_ref, w2_ref, *refs):
    m_ref, gu_ref, ga_ref, y_ref = refs[-4:]
    i = pl.program_id(0)

    @pl.when(i == 0)
    def _():
        if first:
            ga_ref[...] = jnp.zeros_like(ga_ref)
            y_ref[...] = jnp.zeros_like(y_ref)
        else:
            ga_ref[...] = refs[0][...]
            y_ref[...] = refs[1][...]

    w1, w2 = w1_ref[...], w2_ref[...]
    inner = nn(a_ref[...], w1)
    chance = 0.5 + 0.5 * lax.erf(inner * 0.5**0.5)
    active = low(inner * chance)
    slope = chance + inner * (0.3989422804014327 * jnp.exp(-0.5 * inner * inner))
    grad_inner = low(nn(g_ref[...], w2) * slope)
    m_ref[...] = active
    gu_ref[...] = grad_inner
    y_ref[...] += nt(active, w2)
    ga_ref[...] += nt(grad_inner, w1)


def mlp(normed3, grads, weights, units, row, kept, sums, after=()):
    rows, depth = normed3.shape
    size = 512
    first = sums is None
    whole = lambda i: (0, 0)
    full = once((rows, depth), whole)
    extra = [] if first else list(sums)
    count = 4 + len(extra)
    if kept is not None:
        extra += list(kept)
    return pl.pallas_call(
        functools.partial(mlp_kernel, first),
        grid=(units // size,),
        in_specs=[full, full]
        + [pl.BlockSpec((depth, size), lambda i: (0, i)), pl.BlockSpec((depth, size), lambda i: (0, units // size + i))]
        + ([] if first else [full, full])
        + [ANY] * (len(extra) + 4 - count + len(after)),
        out_specs=[pl.BlockSpec((rows, size), lambda i: (row, i))] * 2 + [pl.BlockSpec((rows, depth), whole)] * 2,
        out_shape=[jax.ShapeDtypeStruct((2 * rows, units), jnp.bfloat16)] * 2
        + [jax.ShapeDtypeStruct((rows, depth), jnp.float32)] * 2,
        input_output_aliases={} if kept is None else {count: 0, count + 1: 1},
        compiler_params=params(48),
        cost_estimate=cost(0),
        name="mlp",
    )(normed3, grads, weights, weights, *extra, *after)


def mlp_grads_kernel(a0_ref, a1_ref, g0_ref, g1_ref, gu_ref, m_ref, out_ref, at_ref, gt_ref):
    i = pl.program_id(0)
    steps = pl.num_programs(0) // 2
    rows = a0_ref.shape[0]

    @pl.when(i == 0)
    def _():
        at_ref[:, :rows] = a0_ref[...].T
        at_ref[:, rows:] = a1_ref[...].T
        gt_ref[:, :rows] = g0_ref[...].T
        gt_ref[:, rows:] = g1_ref[...].T

    @pl.when(i < steps)
    def _():
        out_ref[...] = low(nn(gt_ref[...], m_ref[...]))

    @pl.when(i >= steps)
    def _():
        out_ref[...] = low(nn(at_ref[...], gu_ref[...]))


def mlp_grads(normed3, grads, grad_inner, active):
    rows, depth = normed3[0].shape
    units = active.shape[1]
    size = 512
    steps = units // size
    full = once((rows, depth), lambda i: (0, 0))
    return pl.pallas_call(
        mlp_grads_kernel,
        grid=(2 * steps,),
        in_specs=[full] * 4
        + [
            pl.BlockSpec((2 * rows, size), lambda i: (0, jnp.maximum(i - steps, 0))),
            pl.BlockSpec((2 * rows, size), lambda i: (0, jnp.minimum(i, steps - 1))),
        ],
        out_specs=pl.BlockSpec((depth, size), lambda i: (0, lax.rem(i + steps, 2 * steps))),
        out_shape=jax.ShapeDtypeStruct((depth, 2 * units), jnp.bfloat16),
        scratch_shapes=[pltpu.VMEM((depth, 2 * rows), jnp.bfloat16)] * 2,
        compiler_params=params(48),
        cost_estimate=cost(0),
        name="mlp_grads",
    )(*normed3, *grads, grad_inner, active)


def middle_bwd_kernel(
    start_ref, gy_ref, ga3_ref, got3_ref, h2_ref, h1_ref, cq_in_ref, t0_ref, t1_ref, t2_ref, t3_ref,
    so_ref, cq_ref, co_ref, g2_ref, g3_ref, _,
    g1_ref, g1b_ref, g2b_ref, gcq_ref, gtext_ref, go_ref, norms_ref, grad_ref, acc_ref,
):
    i = pl.program_id(0)
    here, part = start_ref[0], start_ref[2]
    rows, cols = gcq_ref.shape
    step = lax.rem(part + 4 - lax.rem(i, 4), 4)
    factor = HEAD_DIM ** (-0.5)

    @pl.when(i == 0)
    def _():
        back, gain, shift = norm_back_kernel(
            h2_ref[...], g3_ref[...], ga3_ref[...] + got3_ref[...].astype(jnp.float32)
        )
        grad_ref[...] = gy_ref[...].astype(jnp.float32) + back
        g2b_ref[...] = low(grad_ref[...])
        norms_ref[2:3, :] = gain
        norms_ref[3:4, :] = shift
        acc_ref[...] = jnp.zeros_like(acc_ref)

    @pl.when(i < 4)
    def _():
        gco = low(nn(g2b_ref[...], co_ref[...]))
        cq = cq_in_ref[...]
        text = chosen(step, (t0_ref, t1_ref, t2_ref, t3_ref), t0_ref[...])
        count = text.shape[0] // 2
        keys, values = text[:, :cols], text[:, cols:]
        parts = []
        for pair in range(cols // PAIR):
            at = slice(pair * PAIR, (pair + 1) * PAIR)
            keys_t = keys[:, at].T
            grad_keys = grad_values = 0.0
            for head in range(2):
                probs = cross_probs(here, part * rows, cq[:, at], lanes_of(keys[:, at], head), count)
                grad_probs = nt(lanes_of(values[:, at], head), gco[:, at])
                total = jnp.sum(probs * grad_probs, axis=0, keepdims=True)
                grad_scores = low(probs * (grad_probs - total))
                parts.append(nn(keys_t[half(head), :], grad_scores))
                grad_keys = grad_keys + nn(grad_scores, lanes_of(cq[:, at], head))
                grad_values = grad_values + nn(low(probs), lanes_of(gco[:, at], head))
            gtext_ref[0, 0, :, at] = low(grad_keys * factor)
            gtext_ref[0, 1, :, at] = low(grad_values)
        gcq = low((jnp.concatenate(parts, 0) * factor).T)
        gcq_ref[...] = gcq
        acc_ref[...] += nt(gcq, cq_ref[...])

        @pl.when(i == 3)
        def _():
            back, gain, shift = norm_back_kernel(h1_ref[...], g2_ref[...], acc_ref[...])
            grad = grad_ref[...] + back
            g1_ref[...] = grad
            g1b_ref[...] = low(grad)
            norms_ref[0:1, :] = gain
            norms_ref[1:2, :] = shift

    @pl.when(i >= 4)
    def _():
        go_ref[0] = low(nn(g1b_ref[...], so_ref[...]))


def middle_bwd(start, out_grad, grad3, got3, hidden2, hidden1, cross_q, texts, weights, gain2, gain3, token):
    rows, depth = out_grad.shape
    cols = depth // 4
    count = texts[0].shape[0]
    whole = lambda i, s: (0, 0)
    early = lambda i, s: (0, jnp.minimum(i, 3))
    full = pl.BlockSpec((rows, depth), whole)
    vector = once((1, depth), whole)
    wide16 = jax.ShapeDtypeStruct((rows, depth), jnp.bfloat16)
    fixed = once((rows, depth), whole)
    return pl.pallas_call(
        middle_bwd_kernel,
        grid_spec=pltpu.PrefetchScalarGridSpec(
            num_scalar_prefetch=1,
            grid=(8,),
            in_specs=[fixed] * 5
            + [pl.BlockSpec((rows, cols), early)]
            + [once(texts[0].shape, whole)] * 4
            + [
                pl.BlockSpec((depth, cols), lambda i, s: (jnp.maximum(i - 4, 0), 0)),
                pl.BlockSpec((depth, cols), lambda i, s: (jnp.minimum(i, 3), 1)),
                pl.BlockSpec((depth, cols), lambda i, s: (jnp.minimum(i, 3), 2)),
            ]
            + [vector] * 2
            + [ANY],
            out_specs=[
                full,
                full,
                full,
                pl.BlockSpec((rows, cols), early),
                pl.BlockSpec((1, 2, count, cols), lambda i, s: (jnp.minimum(i, 3), 0, 0, 0)),
                pl.BlockSpec((1, rows, cols), lambda i, s: (jnp.maximum(i - 4, 0), 0, 0)),
                pl.BlockSpec((8, depth), whole),
            ],
            scratch_shapes=[pltpu.VMEM((rows, depth), jnp.float32)] * 2,
        ),
        out_shape=[
            jax.ShapeDtypeStruct((rows, depth), jnp.float32),
            wide16,
            wide16,
            wide16,
            jax.ShapeDtypeStruct((4, 2, count, cols), jnp.bfloat16),
            jax.ShapeDtypeStruct((4, rows, cols), jnp.bfloat16),
            jax.ShapeDtypeStruct((8, depth), jnp.float32),
        ],
        compiler_params=params(56),
        cost_estimate=cost(2000),
        name="middle_bwd",
    )(start, out_grad, grad3, got3, hidden2, hidden1, cross_q, *texts, weights, weights, weights,
      gain2[None], gain3[None], token)


def middle_grads_kernel(so_l, cq_l, co_l, so_r, cq_r, co_r, out_ref, l_ref):
    i = pl.program_id(0)
    m = lax.rem(i, 3)

    @pl.when(i == 0)
    def _():
        for index, ref in enumerate((so_l, cq_l, co_l)):
            l_ref[index] = ref[...].T

    for index, ref in enumerate((so_r, cq_r, co_r)):

        @pl.when(m == index)
        def _():
            out_ref[...] = low(nn(l_ref[index], ref[...]))


def middle_grads(grad1, normed2, grad2, mixed, grad_cq, cmix):
    rows, depth = normed2.shape
    cols = depth // 4
    full = once((rows, depth), lambda i: (0, 0))
    quarter = pl.BlockSpec((rows, cols), lambda i: (0, i // 3))
    return pl.pallas_call(
        middle_grads_kernel,
        grid=(12,),
        in_specs=[full] * 3 + [quarter] * 3,
        out_specs=pl.BlockSpec((depth, cols), lambda i: (0, i)),
        out_shape=jax.ShapeDtypeStruct((depth, 3 * depth), jnp.bfloat16),
        scratch_shapes=[pltpu.VMEM((3, depth, rows), jnp.bfloat16)],
        compiler_params=params(40),
        cost_estimate=cost(0),
        name="middle_grads",
    )(grad1, normed2, grad2, mixed, grad_cq, cmix)


def block_grad_kernel(order_ref, x_ref, gq_ref, gkv_ref, back_ref, w0_ref, w1_ref, w2_ref, *refs):
    part_ref, g_ref, norms_ref, padded_ref = refs[-4:]
    i = pl.program_id(0)
    rows = x_ref.shape[0]
    skip = padded_ref.shape[1] - back_ref.shape[1]

    @pl.when(i == 0)
    def _():
        padded_ref[:, :skip, :] = jnp.zeros_like(padded_ref[:, :skip, :])
        padded_ref[:, skip:, :] = back_ref[...]
        norms_ref[...] = jnp.zeros_like(norms_ref)

    at = pl.ds(pl.multiple_of(order_ref[i] * rows, rows), rows)
    cols = gq_ref.shape[1]
    total = 0.0
    for index, w_ref in enumerate((w0_ref, w1_ref, w2_ref)):
        grad = gq_ref[...]
        if index:
            grad = low(gkv_ref[index - 1] + padded_ref[index - 1, at, :].astype(jnp.float32))
        g_ref[:, index * cols:(index + 1) * cols] = grad
        total = total + nt(grad, w_ref[...])
    unit, _ = normed(x_ref[...].astype(jnp.float32))
    norms_ref[0:1, :] += jnp.sum(total * unit, axis=0, keepdims=True)
    norms_ref[1:2, :] += jnp.sum(total, axis=0, keepdims=True)
    part_ref[0] = total.astype(part_ref.dtype)


def block_grad(order, count, block, grad_q, grad_kv, back, weights, before, after=()):
    width, depth = block.shape
    cols = grad_q.shape[1]
    rows = width // 4
    at = lambda i, order: (order[i], 0)
    w_spec = lambda j: once((depth, cols), lambda i, order: (0, j))
    return pl.pallas_call(
        block_grad_kernel,
        grid_spec=pltpu.PrefetchScalarGridSpec(
            num_scalar_prefetch=1,
            grid=(count,),
            in_specs=[
                pl.BlockSpec((rows, depth), at),
                pl.BlockSpec((rows, cols), at),
                pl.BlockSpec((2, rows, cols), lambda i, order: (0, order[i], 0)),
                once(back.shape, lambda i, order: (0, 0, 0)),
                w_spec(0),
                w_spec(1),
                w_spec(2),
            ]
            + [ANY] * (len(before) + len(after)),
            out_specs=[
                pl.BlockSpec((1, rows, depth), lambda i, order: (order[i], 0, 0)),
                pl.BlockSpec((rows, 3 * cols), at),
                pl.BlockSpec((8, depth), lambda i, order: (0, 0)),
            ],
            scratch_shapes=[pltpu.VMEM((2, width, cols), jnp.bfloat16)],
        ),
        out_shape=[
            jax.ShapeDtypeStruct((4, rows, depth), jnp.bfloat16),
            jax.ShapeDtypeStruct((width, 3 * cols), jnp.bfloat16),
            jax.ShapeDtypeStruct((8, depth), jnp.float32),
        ],
        input_output_aliases={8: 0, 9: 1} if before else {},
        compiler_params=params(48),
        cost_estimate=cost(0),
        name="block_grad",
    )(order, block, grad_q, grad_kv, back, weights, weights, weights, *before, *after)


def block_weights_kernel(at_ref, g_ref, text_ref, gtext_ref, out_ref):
    i = pl.program_id(0)

    @pl.when(i < 3)
    def _():
        out_ref[...] = low(nn(at_ref[...], g_ref[...]))

    @pl.when(i >= 3)
    def _():
        out_ref[...] = low(nn(text_ref[...].T, gtext_ref[...]))


def block_weights(normed1_t, grads, text, grad_text, after):
    depth, width = normed1_t.shape
    cols = grads.shape[1] // 3
    whole = lambda i: (0, 0)
    return pl.pallas_call(
        without(block_weights_kernel, 4, len(after)),
        grid=(5,),
        in_specs=[
            once((depth, width), whole),
            pl.BlockSpec((width, cols), lambda i: (0, jnp.minimum(i, 2))),
            once(text.shape, whole),
            pl.BlockSpec((text.shape[0], cols), lambda i: (0, jnp.maximum(i - 3, 0))),
        ]
        + [ANY] * len(after),
        out_specs=pl.BlockSpec((depth, cols), lambda i: (0, i)),
        out_shape=jax.ShapeDtypeStruct((depth, 5 * cols), jnp.bfloat16),
        compiler_params=params(40),
        cost_estimate=cost(0),
        name="block_weights",
    )(normed1_t, grads, text, grad_text, *after)


def round_kernel(_, up_sum_ref, down_sum_ref, up_ref, down_ref, up_out_ref, down_out_ref):
    up_out_ref[...] = low(up_sum_ref[0].astype(jnp.float32) + up_ref[...].astype(jnp.float32))
    down_out_ref[...] = low(down_sum_ref[0].astype(jnp.float32) + down_ref[...].astype(jnp.float32))


def round_sums(targets, sums, up, down, after, micros):
    rows, depth = up.shape
    size = rows // 4
    flat = pl.BlockSpec((size, depth), lambda i, targets: (i, 0))
    return pl.pallas_call(
        without(round_kernel, 5, len(after)),
        grid_spec=pltpu.PrefetchScalarGridSpec(
            num_scalar_prefetch=1,
            grid=(4,),
            in_specs=[
                pl.BlockSpec((1, size, depth), lambda i, targets: (targets[0], i, 0)),
                pl.BlockSpec((1, size, depth), lambda i, targets: (targets[1], i, 0)),
                flat,
                flat,
            ]
            + [ANY] * len(after),
            out_specs=[flat, flat],
        ),
        out_shape=[jax.ShapeDtypeStruct((rows, depth), jnp.bfloat16)] * 2,
        compiler_params=params(24),
        cost_estimate=cost(micros),
        name="round_sums",
    )(targets, sums, sums, up, down, *after)


def last_kernel(_, sum_ref, up_ref, down_ref, x_ref, grad_ref, gain_ref, out_ref):
    total = sum_ref[0].astype(jnp.float32) + up_ref[...].astype(jnp.float32) + down_ref[...].astype(jnp.float32)
    back, _, _ = norm_back_kernel(x_ref[...].astype(jnp.float32), gain_ref[...], total)
    out_ref[...] = grad_ref[...] + back


def last_sums(place, sums, up, down, tokens, grad, gain, after):
    rows, depth = up.shape
    size = rows // 4
    flat = pl.BlockSpec((size, depth), lambda i, place: (i, 0))
    return pl.pallas_call(
        without(last_kernel, 7, len(after)),
        grid_spec=pltpu.PrefetchScalarGridSpec(
            num_scalar_prefetch=1,
            grid=(4,),
            in_specs=[pl.BlockSpec((1, size, depth), lambda i, place: (place[0], i, 0))]
            + [flat] * 4
            + [pl.BlockSpec((1, depth), lambda i, place: (0, 0))]
            + [ANY] * len(after),
            out_specs=flat,
        ),
        out_shape=jax.ShapeDtypeStruct((rows, depth), jnp.float32),
        compiler_params=params(24),
        cost_estimate=cost(0),
        name="last_sums",
    )(place, sums, up, down, tokens, grad, gain[None], *after)


def piece_kernel(own_ref, first_ref, second_ref, third_ref, out_ref):
    out_ref[...] = (own_ref[...].astype(jnp.float32) + first_ref[...].astype(jnp.float32)) + (
        second_ref[...].astype(jnp.float32) + third_ref[...].astype(jnp.float32)
    )


def piece_sums(pieces, after):
    rows, cols = pieces[0].shape
    return pl.pallas_call(
        without(piece_kernel, 4, len(after)),
        in_specs=[pl.BlockSpec(memory_space=pltpu.VMEM)] * 4 + [ANY] * len(after),
        out_specs=pl.BlockSpec(memory_space=pltpu.VMEM),
        out_shape=jax.ShapeDtypeStruct((rows, cols), jnp.float32),
        compiler_params=params(24),
        cost_estimate=cost(0),
        name="piece_sums",
    )(*pieces, *after)


def turned(value, axis, steps):
    count = lax.axis_size(axis)
    return lax.ppermute(value, axis, [(source, (source + steps) % count) for source in range(count)])


def swapped(value, bit):
    return lax.ppermute(value, "tp", [(source, source ^ bit) for source in range(lax.axis_size("tp"))])


def moved(value, steps, senders):
    return lax.ppermute(value, "tp", [(source, source + steps) for source in senders])


def along_line(value):
    count = lax.axis_size("tp")
    up, down = [value], [value]
    for round_at in range(count - 1):
        up.append(moved(up[-1], 1, range(round_at, count - 1)))
        down.append(moved(down[-1], -1, range(1, count - round_at)))
    return up, down


def picked(value, index):
    return lax.dynamic_index_in_dim(value, index % value.shape[0], 0, keepdims=True)


def exchanged(value, place):
    count = lax.axis_size("tp")
    return [value] + [turned(picked(value, place + step), "tp", step) for step in range(1, count)]


def in_order(parts, place):
    out = jnp.zeros((len(parts),) + parts[0].shape, parts[0].dtype)
    for step, part in enumerate(parts):
        out = lax.dynamic_update_slice_in_dim(out, part[None], (place + len(parts) - step) % len(parts), 0)
    return out


def dot(left, right):
    return jnp.dot(left, right, preferred_element_type=jnp.float32)


def dot_last(left, right):
    return jnp.einsum("ra,ba->rb", left, right, preferred_element_type=jnp.float32)


def split_mlp(values):
    return values[:2], values[2], values[3]


def on_device(
    tokens,
    text_states,
    clip_start,
    ln1_gain,
    ln1_bias,
    self_query,
    self_key,
    self_value,
    self_out,
    ln2_gain,
    ln2_bias,
    cross_query,
    cross_key,
    cross_value,
    cross_out,
    ln3_gain,
    ln3_bias,
    fc_in,
    fc_out,
    out_grad,
):
    place, members = lax.axis_index("wide"), lax.axis_size("wide")
    part, parts = lax.axis_index("tp"), lax.axis_size("tp")
    here = lax.dynamic_index_in_dim(clip_start, place, 0, keepdims=False)
    before = lax.dynamic_index_in_dim(clip_start, (place + members - 1) % members, 0, keepdims=False)
    start = jnp.stack([here, before, part]).astype(jnp.int32)
    rows, depth = tokens.shape
    width = rows * parts
    cols, units = self_query.shape[1], fc_in.shape[1]
    texts = text_states.shape[0]
    scalars = lambda *values: jnp.stack([jnp.asarray(value, jnp.int32) for value in values])

    def gathered(value):
        return lax.all_gather(value, "wide", axis=0, tiled=True)

    weights1 = gathered(jnp.concatenate([self_query, self_key, self_value, cross_key, cross_value], 1))
    fc_shards = jnp.concatenate([fc_in, fc_out.T], 1)
    text_at = 3 * cols
    first, last = part == 0, part == parts - 1
    first, last = part == 0, part == parts - 1
    (_, up1, up2, up3), (_, down1, down2, down3) = along_line(tokens)
    shards = jnp.concatenate([self_out.T, cross_query, cross_out.T], 1)
    weights2 = lax.all_gather(shards, ("tp", "wide"), axis=0, tiled=True)

    block = qkv_block(scalars(part, 0), [tokens], ln1_gain, ln1_bias, weights1, 0, width, cols, None)
    at = scalars(jnp.where(first, 1, part - 1), jnp.where(first, 1, 0))
    block = qkv_block(at, [up1, down1], ln1_gain, ln1_bias, weights1, 0, width, cols, block)
    at = scalars((part + 2) % parts, jnp.where(part >= 2, 0, 1))
    block = qkv_block(at, [up2, down2], ln1_gain, ln1_bias, weights1, 0, width, cols, block)
    at = scalars(jnp.where(first, parts - 1, (part + 1) % parts), jnp.where(first, 2, jnp.where(last, 1, 0)))
    text_kv = low(dot(tie(text_states, block[0]), weights1[:, text_at:]))
    text_kv = jnp.concatenate([turned(text_kv, "wide", 1), text_kv], 0)
    block = qkv_block(
        at, [down1, up3, down3], ln1_gain, ln1_bias, weights1, 0, width, cols, block, [text_kv]
    )
    block, _, normed1_t, qkv = block
    kv_old = turned(qkv[MIN_START:, cols:], "wide", 1)
    weights_fc = gathered(tie(fc_shards, qkv))
    grad_out = [out_grad, swapped(tie(out_grad, up3, down3), 1)]
    fc_in_other = swapped(tie(fc_in, up3, down3), 2)
    text_kv = [text_kv] + [turned(text_kv, "tp", step) for step in range(1, parts)]
    mixed, mixed_t, logs = self_fwd(start, qkv, kv_old, [])
    mixed = exchanged(tie(mixed, grad_out[1], fc_in_other, *text_kv).reshape(parts, rows, cols), part)
    fc_out_other = swapped(tie(fc_out.T, *mixed[1:]), 2)
    mixed, hidden1, normed2, cross_q, cmix, hidden2, normed3 = middle_fwd(
        start, tokens, mixed, text_kv, weights2, ln2_gain, ln2_bias, ln3_gain, ln3_bias
    )

    def summed(value):
        return lax.psum_scatter(value, "wide", scatter_dimension=0, tiled=True)

    weights3 = gathered(jnp.concatenate([fc_in_other, tie(fc_out_other, normed3)], 1))

    normed3 = [normed3, swapped(normed3, 1)]
    kept, *sums_own = split_mlp(mlp(normed3[0], grad_out[0], weights_fc, units, 0, None, None))
    kept, *sums_theirs = split_mlp(mlp(normed3[1], grad_out[1], weights_fc, units, 1, kept, None))
    grads_own = mlp_grads(normed3, grad_out, kept[1], kept[0])
    after_own = tie(sums_theirs[0], weights3, grads_own, micros=2000)
    kept_other, *sums_theirs = split_mlp(
        mlp(normed3[1], grad_out[1], weights3, units, 1, None, (after_own, sums_theirs[1]))
    )
    got3 = swapped(low(sums_theirs[0]), 1)
    kept_other, *sums_own = split_mlp(mlp(normed3[0], grad_out[0], weights3, units, 0, kept_other, sums_own))
    grads_other = mlp_grads(normed3, grad_out, kept_other[1], kept_other[0])

    grad1, grad1_low, grad2_low, grad_cq, grad_text, grad_mixed, norms23 = middle_bwd(
        start, out_grad, sums_own[0], got3, hidden2, hidden1, cross_q, text_kv, weights2, ln2_gain, ln3_gain, grads_other
    )
    outer = swapped(low(sums_theirs[1]), 1)
    layer_out = low(hidden2 + sums_own[1] + outer.astype(jnp.float32))
    grad_mixed = exchanged(tie(grad_mixed, outer), part)
    grads_middle = middle_grads(grad1_low, normed2, grad2_low, mixed, grad_cq, cmix)

    grad_text = exchanged(tie(grad_text, grads_middle), part)
    grads_own = summed(grads_own)
    grad_kv_old, grad_query_t = self_bwd(start, qkv, kv_old, grad_mixed, mixed_t, logs, None, [grads_own])
    grad_kv_back = turned(grad_kv_old, "wide", -1)
    grad_text = [tie(picked(grad_text[0], part), grad_query_t)] + grad_text[1:]
    grad_text = sum(piece[0].astype(jnp.float32) for piece in grad_text)
    back = turned(low(grad_text[:, :texts]), "wide", -1).astype(jnp.float32)
    grads_other = summed(grads_other)
    grad_text = low(grad_text[:, texts:] + back)
    grad_text = jnp.concatenate([grad_text[0], grad_text[1]], 1)
    text_term = low(dot_last(grad_text, weights1[:, text_at:]))
    grad_kv, grad_query = self_bwd(
        start, qkv, None, grad_mixed, mixed_t, logs, grad_query_t, [text_term, grads_other]
    )
    text_term = [text_term] + [turned(text_term, "tp", step) for step in range(1, parts)]
    grads_other = swapped(grads_other, 2)

    block_args = (block, grad_query, grad_kv, grad_kv_back, weights1)
    near, far = part < parts // 2, parts - 1
    sums, grad_qkv, norms_first = block_grad(scalars(jnp.where(near, far, 0)), 1, *block_args, [], text_term)
    own_first = picked(sums, jnp.where(near, far, 0))[0]
    up, down = moved(own_first, 1, (0,)), moved(own_first, -1, (far,))
    others = scalars(
        jnp.where(near, 2, 1),
        jnp.where(first, 1, jnp.where(last, 2, jnp.where(near, 0, far))),
        part,
    )
    sums, grad_qkv, norms_rest = block_grad(others, 3, *block_args, [sums, grad_qkv], [grads_other])
    grads_block = block_weights(normed1_t, grad_qkv, text_states, grad_text, [])
    norms = jnp.concatenate([norms_first[:2] + norms_rest[:2], norms23[:4]], 0)
    grads_middle = summed(grads_middle)
    pieces = [
        lax.dynamic_slice_in_dim(grads_middle, ((part + step) % parts) * 3 * cols, 3 * cols, 1) for step in range(parts)
    ]
    after = []
    for round_at in (2, 3):
        targets = scalars((part + parts - round_at) % parts, (part + round_at) % parts)
        up, down = round_sums(targets, sums, up, down, after, 2000 if round_at == 3 else 0)
        norms = norms + tie(swapped(norms, round_at - 1), grads_block, grads_middle)
        up, down = moved(up, 1, range(round_at)), moved(down, -1, range(parts - round_at, parts))
        after = [norms, grads_block, *pieces]
    tokens_grad = last_sums(scalars(part), sums, up, down, tokens, grad1, ln1_gain, [norms])
    bit = 1
    while bit < members:
        norms = norms + lax.ppermute(norms, "wide", [(source, source ^ bit) for source in range(members)])
        bit *= 2
    text_grad = jnp.sum(in_order([tie(text_term[0], up)] + text_term[1:], part).astype(jnp.float32), 0)

    fc_grads = grads_own.astype(jnp.float32) + grads_other.astype(jnp.float32)
    fc_in_grad, fc_out_grad = fc_grads[:, :units], fc_grads[:, units:].T
    grads_block = tie(summed(grads_block), up).astype(jnp.float32)
    grads_block = [grads_block[:, i * cols : (i + 1) * cols] for i in range(5)]
    grads_middle = piece_sums(
        [pieces[0]] + [turned(pieces[step], "tp", step) for step in range(1, parts)],
        [tokens_grad, text_grad, norms, fc_in_grad, fc_out_grad, *grads_block],
    )
    grads_middle = [grads_middle[:, i * cols : (i + 1) * cols] for i in range(3)]

    return (
        layer_out,
        tokens_grad,
        text_grad,
        norms[0],
        norms[1],
        grads_block[0],
        grads_block[1],
        grads_block[2],
        grads_middle[0].T,
        norms[2],
        norms[3],
        grads_middle[1],
        grads_block[3],
        grads_block[4],
        grads_middle[2].T,
        norms[4],
        norms[5],
        fc_in_grad,
        fc_out_grad,
    )


def solution(mesh):
    in_specs = (
        P(("wide", "tp"), None),
        P("wide", None),
        P(),
        P(),
        P(),
        P("wide", "tp"),
        P("wide", "tp"),
        P("wide", "tp"),
        P("tp", "wide"),
        P(),
        P(),
        P("wide", "tp"),
        P("wide", "tp"),
        P("wide", "tp"),
        P("tp", "wide"),
        P(),
        P(),
        P("wide", "tp"),
        P("tp", "wide"),
        P(("wide", "tp"), None),
    )
    out_specs = (
        P(("wide", "tp"), None),
        P(("wide", "tp"), None),
        P("wide", None),
        P(),
        P(),
        P("wide", "tp"),
        P("wide", "tp"),
        P("wide", "tp"),
        P("tp", "wide"),
        P(),
        P(),
        P("wide", "tp"),
        P("wide", "tp"),
        P("wide", "tp"),
        P("tp", "wide"),
        P(),
        P(),
        P("wide", "tp"),
        P("tp", "wide"),
    )
    return jax.shard_map(
        on_device, mesh=mesh, in_specs=in_specs, out_specs=out_specs, check_vma=False
    )
```

```python
import functools

import jax
import jax.numpy as jnp
from jax import lax
from jax.experimental import pallas as pl
from jax.experimental.pallas import tpu as pltpu
from jax.sharding import PartitionSpec as P

HEAD_DIM = 64
PAIR = 2 * HEAD_DIM
LOG2E = 1.4426950408889634
MIN_START = 512
TILE = 512

COST_SCALE = 1.0

epsilon = 1e-05
masked_score = -1e30


def nn(a, b):
    return lax.dot_general(a, b, (((1,), (0,)), ((), ())), preferred_element_type=jnp.float32)


def nt(a, b):
    return lax.dot_general(a, b, (((1,), (1,)), ((), ())), preferred_element_type=jnp.float32)


def low(value):
    return value.astype(jnp.bfloat16)


def lanes_of(value, head):
    lane = lax.broadcasted_iota(jnp.int32, value.shape, 1)
    return jnp.where((lane >= head * HEAD_DIM) & (lane < (head + 1) * HEAD_DIM), value, 0).astype(value.dtype)


def half(head):
    return slice(head * HEAD_DIM, (head + 1) * HEAD_DIM)


def normed(value):
    centred = value - jnp.mean(value, axis=-1, keepdims=True)
    scale = lax.rsqrt(jnp.mean(centred * centred, axis=-1, keepdims=True) + epsilon)
    return centred * scale, scale


def norm_kernel(value, gain, shift):
    return normed(value)[0] * gain + shift


def norm_back_kernel(value, gain, grad):
    unit, scale = normed(value)
    inner = grad * gain
    back = inner - jnp.mean(inner, axis=-1, keepdims=True) - unit * jnp.mean(inner * unit, axis=-1, keepdims=True)
    return back * scale, jnp.sum(grad * unit, axis=0, keepdims=True), jnp.sum(grad, axis=0, keepdims=True)


def params(mib):
    return pltpu.CompilerParams(vmem_limit_bytes=mib * 2**20)


def cost(micros):
    return pl.CostEstimate(flops=int(micros * 1e9 * COST_SCALE), bytes_accessed=0, transcendentals=0)


def once(shape, at):
    return pl.BlockSpec(shape, at, pipeline_mode=pl.Buffered(1))


ANY = pl.BlockSpec(memory_space=pl.ANY)
SMEM = pl.BlockSpec(memory_space=pltpu.SMEM)


def without(kernel, at, count):
    return lambda *refs: kernel(*refs[:at], *refs[at + count:])


def tie_kernel(*refs):
    pass


def tie(value, *tokens, micros=0):
    return pl.pallas_call(
        tie_kernel,
        in_specs=[ANY] * (1 + len(tokens)),
        out_specs=ANY,
        out_shape=jax.ShapeDtypeStruct(value.shape, value.dtype),
        input_output_aliases={0: 0},
        cost_estimate=cost(micros),
        name="tie",
    )(value, *tokens)


def qkv_kernel(count, first, at_ref, *refs):
    blocks, refs = refs[:count], refs[count:]
    gain_ref, shift_ref, w_ref = refs[:3]
    x_ref, a_ref, at_out_ref, qkv_ref, kept_ref = refs[3 if first else 7:]

    @pl.when(pl.program_id(0) == 0)
    def _():
        value = blocks[0][...]
        for index in range(1, count):
            value = jnp.where(at_ref[1] == index, blocks[index][...], value)
        x_ref[...] = value
        kept_ref[...] = low(norm_kernel(value.astype(jnp.float32), gain_ref[...], shift_ref[...]))
        a_ref[...] = kept_ref[...]
        at_out_ref[...] = kept_ref[...].T

    qkv_ref[...] = low(nn(kept_ref[...], w_ref[...]))


def qkv_block(at, blocks, gain, shift, weights, column, width, cols, before, after=()):
    rows, depth = blocks[0].shape
    first = before is None
    count = len(blocks)
    whole = lambda j, at: (0, 0)
    here = lambda j, at: (at[0], 0)
    return pl.pallas_call(
        without(functools.partial(qkv_kernel, count, first), count + (4 if first else 8), len(after)),
        grid_spec=pltpu.PrefetchScalarGridSpec(
            num_scalar_prefetch=1,
            grid=(3,),
            in_specs=[once((rows, depth), whole)] * count
            + [once((1, depth), whole)] * 2
            + [pl.BlockSpec((depth, cols), lambda j, at: (0, column // cols + j))]
            + ([] if first else [ANY] * 4)
            + [ANY] * len(after),
            out_specs=[
                pl.BlockSpec((rows, depth), here),
                pl.BlockSpec((rows, depth), here),
                pl.BlockSpec((depth, rows), lambda j, at: (0, at[0])),
                pl.BlockSpec((rows, cols), lambda j, at: (at[0], j)),
            ],
            scratch_shapes=[pltpu.VMEM((rows, depth), jnp.bfloat16)],
        ),
        out_shape=[
            jax.ShapeDtypeStruct((width, depth), jnp.bfloat16),
            jax.ShapeDtypeStruct((width, depth), jnp.bfloat16),
            jax.ShapeDtypeStruct((depth, width), jnp.bfloat16),
            jax.ShapeDtypeStruct((width, 3 * cols), jnp.bfloat16),
        ],
        input_output_aliases={} if first else {count + 4 + i: i for i in range(4)},
        compiler_params=params(40),
        cost_estimate=cost(0),
        name="qkv_block",
    )(at, *blocks, gain[None], shift[None], weights, *(before or ()), *after)


def first_of(rows, here, before, width):
    return jnp.where(rows >= here, here, before - width)


def self_fwd_kernel(tile_size, skip, start_ref, q_ref, k_ref, v_ref, kp_ref, vp_ref, o_ref, ot_ref, l_ref, vt_ref, vpt_ref):
    width, old = q_ref.shape[0], kp_ref.shape[0]
    size = tile_size
    here, before = start_ref[0], start_ref[1]
    factor = HEAD_DIM ** (-0.5) * LOG2E
    vt_ref[...] = v_ref[...].T
    vpt_ref[...] = vp_ref[...].T
    for i in range(width // size):
        rows = i * size + lax.broadcasted_iota(jnp.int32, (1, size), 1)
        first = first_of(rows, here, before, width)
        query = q_ref[i * size:(i + 1) * size, :]

        def tile(key_ref, value_ref, j, place, causal, carry):
            at = pl.multiple_of(j * size, size)
            keys = key_ref[pl.ds(at, size), :]
            places = place + j * size + lax.broadcasted_iota(jnp.int32, (size, 1), 0)
            allowed = places >= first
            if causal:
                allowed = allowed & (places <= rows)
            out = []
            for head in range(2):
                top, total, acc = carry[head]
                scores = jnp.where(allowed, nt(lanes_of(keys, head), query) * factor, masked_score)
                peak = jnp.maximum(top, jnp.max(scores, axis=0, keepdims=True))
                shrink = jnp.exp2(top - peak)
                probs = jnp.exp2(scores - peak)
                total = total * shrink + jnp.sum(probs, axis=0, keepdims=True)
                part = nn(value_ref[half(head), pl.ds(at, size)], low(probs))
                out.append((peak, total, acc * shrink + part))
            return tuple(out)

        carry = tuple(
            (
                jnp.full((1, size), masked_score, jnp.float32),
                jnp.zeros((1, size), jnp.float32),
                jnp.zeros((HEAD_DIM, size), jnp.float32),
            )
            for _ in range(2)
        )
        if i * size < skip + old:
            start = jnp.where(here > i * size, (before - skip) // size, old // size)
            carry = lax.fori_loop(
                start, old // size, lambda j, c: tile(kp_ref, vpt_ref, j, skip - width, False, c), carry
            )
        start = jnp.where(here > i * size, 0, here // size)
        carry = lax.fori_loop(start, i, lambda j, c: tile(k_ref, vt_ref, j, 0, False, c), carry)
        carry = tile(k_ref, vt_ref, i, 0, True, carry)
        for head in range(2):
            top, total, acc = carry[head]
            ot_ref[half(head), i * size:(i + 1) * size] = acc / total
            l_ref[0, head:head + 1, i * size:(i + 1) * size] = top + jnp.log2(total)
    o_ref[...] = low(ot_ref[...].T)


def self_fwd(start, qkv, kv_old, after):
    width, cols = qkv.shape[0], qkv.shape[1] // 3
    old = kv_old.shape[0]
    pairs = cols // PAIR
    return pl.pallas_call(
        without(functools.partial(self_fwd_kernel, TILE, width - old), 6, len(after)),
        grid=(pairs,),
        in_specs=[
            SMEM,
            pl.BlockSpec((width, PAIR), lambda p: (0, p)),
            pl.BlockSpec((width, PAIR), lambda p: (0, p + pairs)),
            pl.BlockSpec((width, PAIR), lambda p: (0, p + 2 * pairs)),
            pl.BlockSpec((old, PAIR), lambda p: (0, p)),
            pl.BlockSpec((old, PAIR), lambda p: (0, p + pairs)),
        ]
        + [ANY] * len(after),
        out_specs=[
            pl.BlockSpec((width, PAIR), lambda p: (0, p)),
            pl.BlockSpec((PAIR, width), lambda p: (p, 0)),
            pl.BlockSpec((1, 8, width), lambda p: (p, 0, 0)),
        ],
        out_shape=[
            jax.ShapeDtypeStruct((width, cols), jnp.bfloat16),
            jax.ShapeDtypeStruct((cols, width), jnp.float32),
            jax.ShapeDtypeStruct((pairs, 8, width), jnp.float32),
        ],
        scratch_shapes=[pltpu.VMEM((PAIR, width), jnp.bfloat16), pltpu.VMEM((PAIR, old), jnp.bfloat16)],
        compiler_params=params(40),
        cost_estimate=cost(0),
        name="self_fwd",
    )(start, qkv, qkv, qkv, kv_old, kv_old, *after)


def self_bwd_kernel(tile_size, skip, old, start_ref, q_ref, k_ref, v_ref, go0_ref, go1_ref, go2_ref, go3_ref, ot_ref, l_ref, *rest):
    if old:
        gkv_ref, gq_ref, kt_ref, delta_ref, go_ref = rest
    else:
        gq_in_ref, gkv_ref, gq_ref, kt_ref, delta_ref, go_ref, sum_ref = rest
    width, count = q_ref.shape[0], k_ref.shape[0]
    size = tile_size
    here, before, part = start_ref[0], start_ref[1], start_ref[2]
    factor = HEAD_DIM ** (-0.5) * LOG2E
    rows_each = go1_ref.shape[1]
    for step, ref in enumerate((go0_ref, go1_ref, go2_ref, go3_ref)):
        at = pl.multiple_of(lax.rem(part + 4 - step, 4) * rows_each, rows_each)
        go_ref[pl.ds(at, rows_each), :] = ref[part if step == 0 else 0]
    kt_ref[...] = k_ref[...].T
    got = go_ref[...].T.astype(jnp.float32) * ot_ref[...]
    for head in range(2):
        delta_ref[head:head + 1, :] = jnp.sum(got[half(head), :], axis=0, keepdims=True)
    acc_ref = gq_ref if old else sum_ref
    acc_ref[...] = jnp.zeros_like(acc_ref) if old else gq_in_ref[...]
    for j in range(count // size):
        place = j * size + (skip - width if old else 0)
        keys = k_ref[j * size:(j + 1) * size, :]
        values = v_ref[j * size:(j + 1) * size, :]
        keys_of = [lanes_of(keys, head) for head in range(2)]
        values_of = [lanes_of(values, head) for head in range(2)]
        places = place + lax.broadcasted_iota(jnp.int32, (size, 1), 0)

        def tile(i, causal, carry):
            at = pl.multiple_of(i * size, size)
            query = q_ref[pl.ds(at, size), :]
            grad = go_ref[pl.ds(at, size), :]
            rows = i * size + lax.broadcasted_iota(jnp.int32, (1, size), 1)
            allowed = places >= first_of(rows, here, before, width)
            if causal:
                allowed = allowed & (places <= rows)
            grad_keys, grad_values = carry
            for head in range(2):
                scores = nt(keys_of[head], query) * factor - l_ref[0, head:head + 1, pl.ds(at, size)]
                probs = jnp.where(allowed, jnp.exp2(scores), 0.0)
                grad_probs = nt(values_of[head], grad)
                grad_scores = low(probs * (grad_probs - delta_ref[head:head + 1, pl.ds(at, size)]))
                grad_values = grad_values + nn(low(probs), lanes_of(grad, head))
                grad_keys = grad_keys + nn(grad_scores, lanes_of(query, head))
                acc_ref[half(head), pl.ds(at, size)] += nn(kt_ref[half(head), j * size:(j + 1) * size], grad_scores)
            return (grad_keys, grad_values)

        zero = jnp.zeros((size, PAIR), jnp.float32)
        carry = (zero, zero)
        if old:
            high = jnp.where(before < place + size + width, (here + size - 1) // size, 0)
            carry = lax.fori_loop(0, high, lambda i, c: tile(i, False, c), carry)
        else:
            high = jnp.where(here >= place + size, (here + size - 1) // size, width // size)
            carry = tile(j, True, carry)
            carry = lax.fori_loop(j + 1, high, lambda i, c: tile(i, False, c), carry)
        gkv_ref[0, j * size:(j + 1) * size, :] = (carry[0] * HEAD_DIM ** (-0.5)).astype(gkv_ref.dtype)
        gkv_ref[1, j * size:(j + 1) * size, :] = carry[1].astype(gkv_ref.dtype)
    if not old:
        gq_ref[...] = low((acc_ref[...] * HEAD_DIM ** (-0.5)).T)


def self_bwd(start, qkv, kv_old, grads, mixed_t, logs, sums, after):
    width, cols = qkv.shape[0], qkv.shape[1] // 3
    old = kv_old is not None
    count = kv_old.shape[0] if old else width
    pairs = cols // PAIR
    rows = grads[1].shape[1]
    across = pl.BlockSpec((PAIR, width), lambda p: (p, 0))
    along = pl.BlockSpec((width, PAIR), lambda p: (0, p))
    key_at, value_at = (0, pairs) if old else (pairs, 2 * pairs)
    return pl.pallas_call(
        without(functools.partial(self_bwd_kernel, TILE, width - count, old), 10 if old else 11, len(after)),
        grid=(pairs,),
        in_specs=[
            SMEM,
            along,
            pl.BlockSpec((count, PAIR), lambda p: (0, p + key_at)),
            pl.BlockSpec((count, PAIR), lambda p: (0, p + value_at)),
            pl.BlockSpec((4, rows, PAIR), lambda p: (0, 0, p)),
            pl.BlockSpec((1, rows, PAIR), lambda p: (0, 0, p)),
            pl.BlockSpec((1, rows, PAIR), lambda p: (0, 0, p)),
            pl.BlockSpec((1, rows, PAIR), lambda p: (0, 0, p)),
            across,
            pl.BlockSpec((1, 8, width), lambda p: (p, 0, 0)),
        ]
        + ([] if old else [across])
        + [ANY] * len(after),
        out_specs=[pl.BlockSpec((2, count, PAIR), lambda p: (0, 0, p)), across if old else along],
        out_shape=[
            jax.ShapeDtypeStruct((2, count, cols), jnp.bfloat16 if old else jnp.float32),
            jax.ShapeDtypeStruct((cols, width), jnp.float32)
            if old
            else jax.ShapeDtypeStruct((width, cols), jnp.bfloat16),
        ],
        scratch_shapes=[
            pltpu.VMEM((PAIR, count), jnp.bfloat16),
            pltpu.VMEM((8, width), jnp.float32),
            pltpu.VMEM((width, PAIR), jnp.bfloat16),
        ]
        + ([] if old else [pltpu.VMEM((PAIR, width), jnp.float32)]),
        compiler_params=params(40),
        cost_estimate=cost(0 if old else 2000),
        name="self_bwd_old" if old else "self_bwd_own",
    )(start, qkv, *((kv_old,) * 2 if old else (qkv,) * 2), *grads, mixed_t, logs, *([] if old else [sums]), *after)


def cross_probs(here, place, cq, keys_of, count):
    scores = nt(keys_of, cq) * (HEAD_DIM ** (-0.5) * LOG2E)
    rows = place + lax.broadcasted_iota(jnp.int32, (1, cq.shape[0]), 1)
    places = lax.broadcasted_iota(jnp.int32, (2 * count, 1), 0)
    scores = jnp.where((places < count) == (rows < here), scores, masked_score)
    probs = jnp.exp2(scores - jnp.max(scores, axis=0, keepdims=True))
    return probs / jnp.sum(probs, axis=0, keepdims=True)


def chosen(step, refs, own):
    value = own
    for index in range(1, 4):
        value = jnp.where(step == index, refs[index][...], value)
    return value


def middle_fwd_kernel(
    start_ref, x_ref, o0_ref, o1_ref, o2_ref, o3_ref, t0_ref, t1_ref, t2_ref, t3_ref,
    so_ref, cq_ref, co_ref, g2_ref, b2_ref, g3_ref, b3_ref,
    mixed_ref, h1_ref, a2_ref, cq_out_ref, cmix_ref, h2_ref, a3_ref, acc_ref,
):
    i = pl.program_id(0)
    here, part = start_ref[0], start_ref[2]
    rows, cols = o1_ref.shape[1], o1_ref.shape[2]
    t = lax.rem(i, 4)
    step = lax.rem(part + 4 - t, 4)

    @pl.when(i < 4)
    def _():
        piece = o0_ref[0]
        for index, ref in ((1, o1_ref), (2, o2_ref), (3, o3_ref)):
            piece = jnp.where(step == index, ref[0], piece)
        mixed_ref[...] = piece
        term = nt(piece, so_ref[...])

        @pl.when(i == 0)
        def _():
            acc_ref[...] = term + x_ref[...].astype(jnp.float32)

        @pl.when(i > 0)
        def _():
            acc_ref[...] += term

        @pl.when(i == 3)
        def _():
            h1_ref[...] = acc_ref[...]
            a2_ref[...] = low(norm_kernel(acc_ref[...], g2_ref[...], b2_ref[...]))

    @pl.when(i >= 4)
    def _():
        cq = low(nn(a2_ref[...], cq_ref[...]))
        cq_out_ref[...] = cq
        text = chosen(step, (t0_ref, t1_ref, t2_ref, t3_ref), t0_ref[...])
        count = text.shape[0] // 2
        keys, values = text[:, :cols], text[:, cols:]
        parts = []
        for pair in range(cols // PAIR):
            at = slice(pair * PAIR, (pair + 1) * PAIR)
            values_t = values[:, at].T
            for head in range(2):
                probs = cross_probs(here, part * rows, cq[:, at], lanes_of(keys[:, at], head), count)
                parts.append(nn(values_t[half(head), :], low(probs)))
        cmix = low(jnp.concatenate(parts, 0).T)
        cmix_ref[...] = cmix
        acc_ref[...] += nt(cmix, co_ref[...])

        @pl.when(i == 7)
        def _():
            h2_ref[...] = acc_ref[...]
            a3_ref[...] = low(norm_kernel(acc_ref[...], g3_ref[...], b3_ref[...]))


def middle_fwd(start, tokens, mixed, texts, weights, gain2, shift2, gain3, shift3):
    rows, depth = tokens.shape
    cols = mixed[1].shape[2]
    whole = lambda i, s: (0, 0)
    early = lambda i, s: (0, jnp.minimum(i, 3))
    late = lambda i, s: (0, jnp.maximum(i - 4, 0))
    vector = once((1, depth), whole)
    wide16 = jax.ShapeDtypeStruct((rows, depth), jnp.bfloat16)
    wide32 = jax.ShapeDtypeStruct((rows, depth), jnp.float32)
    return pl.pallas_call(
        middle_fwd_kernel,
        grid_spec=pltpu.PrefetchScalarGridSpec(
            num_scalar_prefetch=1,
            grid=(8,),
            in_specs=[once((rows, depth), whole)]
            + [once((1, rows, cols), lambda i, s: (s[2], 0, 0))]
            + [once((1, rows, cols), lambda i, s: (0, 0, 0))] * 3
            + [once(texts[0].shape, whole)] * 4
            + [
                pl.BlockSpec((depth, cols), lambda i, s: (jnp.minimum(i, 3), 0)),
                pl.BlockSpec((depth, cols), lambda i, s: (jnp.maximum(i - 4, 0), 1)),
                pl.BlockSpec((depth, cols), lambda i, s: (jnp.maximum(i - 4, 0), 2)),
            ]
            + [vector] * 4,
            out_specs=[
                pl.BlockSpec((rows, cols), early),
                pl.BlockSpec((rows, depth), whole),
                pl.BlockSpec((rows, depth), whole),
                pl.BlockSpec((rows, cols), late),
                pl.BlockSpec((rows, cols), late),
                pl.BlockSpec((rows, depth), whole),
                pl.BlockSpec((rows, depth), whole),
            ],
            scratch_shapes=[pltpu.VMEM((rows, depth), jnp.float32)],
        ),
        out_shape=[wide16, wide32, wide16, wide16, wide16, wide32, wide16],
        compiler_params=params(48),
        cost_estimate=cost(0),
        name="middle_fwd",
    )(start, tokens, *mixed, *texts, weights, weights, weights, gain2[None], shift2[None], gain3[None], shift3[None])


def mlp_kernel(first, a_ref, g_ref, w1_ref, w2_ref, *refs):
    m_ref, gu_ref, ga_ref, y_ref = refs[-4:]
    i = pl.program_id(0)

    @pl.when(i == 0)
    def _():
        if first:
            ga_ref[...] = jnp.zeros_like(ga_ref)
            y_ref[...] = jnp.zeros_like(y_ref)
        else:
            ga_ref[...] = refs[0][...]
            y_ref[...] = refs[1][...]

    w1, w2 = w1_ref[...], w2_ref[...]
    inner = nn(a_ref[...], w1)
    chance = 0.5 + 0.5 * lax.erf(inner * 0.5**0.5)
    active = low(inner * chance)
    slope = chance + inner * (0.3989422804014327 * jnp.exp(-0.5 * inner * inner))
    grad_inner = low(nn(g_ref[...], w2) * slope)
    m_ref[...] = active
    gu_ref[...] = grad_inner
    y_ref[...] += nt(active, w2)
    ga_ref[...] += nt(grad_inner, w1)


def mlp(normed3, grads, weights, units, row, kept, sums, after=()):
    rows, depth = normed3.shape
    size = 512
    first = sums is None
    whole = lambda i: (0, 0)
    full = once((rows, depth), whole)
    extra = [] if first else list(sums)
    count = 4 + len(extra)
    if kept is not None:
        extra += list(kept)
    return pl.pallas_call(
        functools.partial(mlp_kernel, first),
        grid=(units // size,),
        in_specs=[full, full]
        + [pl.BlockSpec((depth, size), lambda i: (0, i)), pl.BlockSpec((depth, size), lambda i: (0, units // size + i))]
        + ([] if first else [full, full])
        + [ANY] * (len(extra) + 4 - count + len(after)),
        out_specs=[pl.BlockSpec((rows, size), lambda i: (row, i))] * 2 + [pl.BlockSpec((rows, depth), whole)] * 2,
        out_shape=[jax.ShapeDtypeStruct((2 * rows, units), jnp.bfloat16)] * 2
        + [jax.ShapeDtypeStruct((rows, depth), jnp.float32)] * 2,
        input_output_aliases={} if kept is None else {count: 0, count + 1: 1},
        compiler_params=params(48),
        cost_estimate=cost(0),
        name="mlp",
    )(normed3, grads, weights, weights, *extra, *after)


def mlp_grads_kernel(a0_ref, a1_ref, g0_ref, g1_ref, gu_ref, m_ref, out_ref, at_ref, gt_ref):
    i = pl.program_id(0)
    steps = pl.num_programs(0) // 2
    rows = a0_ref.shape[0]

    @pl.when(i == 0)
    def _():
        at_ref[:, :rows] = a0_ref[...].T
        at_ref[:, rows:] = a1_ref[...].T
        gt_ref[:, :rows] = g0_ref[...].T
        gt_ref[:, rows:] = g1_ref[...].T

    @pl.when(i < steps)
    def _():
        out_ref[...] = low(nn(gt_ref[...], m_ref[...]))

    @pl.when(i >= steps)
    def _():
        out_ref[...] = low(nn(at_ref[...], gu_ref[...]))


def mlp_grads(normed3, grads, grad_inner, active):
    rows, depth = normed3[0].shape
    units = active.shape[1]
    size = 512
    steps = units // size
    full = once((rows, depth), lambda i: (0, 0))
    return pl.pallas_call(
        mlp_grads_kernel,
        grid=(2 * steps,),
        in_specs=[full] * 4
        + [
            pl.BlockSpec((2 * rows, size), lambda i: (0, jnp.maximum(i - steps, 0))),
            pl.BlockSpec((2 * rows, size), lambda i: (0, jnp.minimum(i, steps - 1))),
        ],
        out_specs=pl.BlockSpec((depth, size), lambda i: (0, lax.rem(i + steps, 2 * steps))),
        out_shape=jax.ShapeDtypeStruct((depth, 2 * units), jnp.bfloat16),
        scratch_shapes=[pltpu.VMEM((depth, 2 * rows), jnp.bfloat16)] * 2,
        compiler_params=params(48),
        cost_estimate=cost(0),
        name="mlp_grads",
    )(*normed3, *grads, grad_inner, active)


def middle_bwd_kernel(
    start_ref, gy_ref, ga3_ref, got3_ref, h2_ref, h1_ref, cq_in_ref, t0_ref, t1_ref, t2_ref, t3_ref,
    so_ref, cq_ref, co_ref, g2_ref, g3_ref, _,
    g1_ref, g1b_ref, g2b_ref, gcq_ref, gtext_ref, go_ref, norms_ref, grad_ref, acc_ref,
):
    i = pl.program_id(0)
    here, part = start_ref[0], start_ref[2]
    rows, cols = gcq_ref.shape
    step = lax.rem(part + 4 - lax.rem(i, 4), 4)
    factor = HEAD_DIM ** (-0.5)

    @pl.when(i == 0)
    def _():
        back, gain, shift = norm_back_kernel(
            h2_ref[...], g3_ref[...], ga3_ref[...] + got3_ref[...].astype(jnp.float32)
        )
        grad_ref[...] = gy_ref[...].astype(jnp.float32) + back
        g2b_ref[...] = low(grad_ref[...])
        norms_ref[2:3, :] = gain
        norms_ref[3:4, :] = shift
        acc_ref[...] = jnp.zeros_like(acc_ref)

    @pl.when(i < 4)
    def _():
        gco = low(nn(g2b_ref[...], co_ref[...]))
        cq = cq_in_ref[...]
        text = chosen(step, (t0_ref, t1_ref, t2_ref, t3_ref), t0_ref[...])
        count = text.shape[0] // 2
        keys, values = text[:, :cols], text[:, cols:]
        parts = []
        for pair in range(cols // PAIR):
            at = slice(pair * PAIR, (pair + 1) * PAIR)
            keys_t = keys[:, at].T
            grad_keys = grad_values = 0.0
            for head in range(2):
                probs = cross_probs(here, part * rows, cq[:, at], lanes_of(keys[:, at], head), count)
                grad_probs = nt(lanes_of(values[:, at], head), gco[:, at])
                total = jnp.sum(probs * grad_probs, axis=0, keepdims=True)
                grad_scores = low(probs * (grad_probs - total))
                parts.append(nn(keys_t[half(head), :], grad_scores))
                grad_keys = grad_keys + nn(grad_scores, lanes_of(cq[:, at], head))
                grad_values = grad_values + nn(low(probs), lanes_of(gco[:, at], head))
            gtext_ref[0, 0, :, at] = low(grad_keys * factor)
            gtext_ref[0, 1, :, at] = low(grad_values)
        gcq = low((jnp.concatenate(parts, 0) * factor).T)
        gcq_ref[...] = gcq
        acc_ref[...] += nt(gcq, cq_ref[...])

        @pl.when(i == 3)
        def _():
            back, gain, shift = norm_back_kernel(h1_ref[...], g2_ref[...], acc_ref[...])
            grad = grad_ref[...] + back
            g1_ref[...] = grad
            g1b_ref[...] = low(grad)
            norms_ref[0:1, :] = gain
            norms_ref[1:2, :] = shift

    @pl.when(i >= 4)
    def _():
        go_ref[0] = low(nn(g1b_ref[...], so_ref[...]))


def middle_bwd(start, out_grad, grad3, got3, hidden2, hidden1, cross_q, texts, weights, gain2, gain3, token):
    rows, depth = out_grad.shape
    cols = depth // 4
    count = texts[0].shape[0]
    whole = lambda i, s: (0, 0)
    early = lambda i, s: (0, jnp.minimum(i, 3))
    full = pl.BlockSpec((rows, depth), whole)
    vector = once((1, depth), whole)
    wide16 = jax.ShapeDtypeStruct((rows, depth), jnp.bfloat16)
    fixed = once((rows, depth), whole)
    return pl.pallas_call(
        middle_bwd_kernel,
        grid_spec=pltpu.PrefetchScalarGridSpec(
            num_scalar_prefetch=1,
            grid=(8,),
            in_specs=[fixed] * 5
            + [pl.BlockSpec((rows, cols), early)]
            + [once(texts[0].shape, whole)] * 4
            + [
                pl.BlockSpec((depth, cols), lambda i, s: (jnp.maximum(i - 4, 0), 0)),
                pl.BlockSpec((depth, cols), lambda i, s: (jnp.minimum(i, 3), 1)),
                pl.BlockSpec((depth, cols), lambda i, s: (jnp.minimum(i, 3), 2)),
            ]
            + [vector] * 2
            + [ANY],
            out_specs=[
                full,
                full,
                full,
                pl.BlockSpec((rows, cols), early),
                pl.BlockSpec((1, 2, count, cols), lambda i, s: (jnp.minimum(i, 3), 0, 0, 0)),
                pl.BlockSpec((1, rows, cols), lambda i, s: (jnp.maximum(i - 4, 0), 0, 0)),
                pl.BlockSpec((8, depth), whole),
            ],
            scratch_shapes=[pltpu.VMEM((rows, depth), jnp.float32)] * 2,
        ),
        out_shape=[
            jax.ShapeDtypeStruct((rows, depth), jnp.float32),
            wide16,
            wide16,
            wide16,
            jax.ShapeDtypeStruct((4, 2, count, cols), jnp.bfloat16),
            jax.ShapeDtypeStruct((4, rows, cols), jnp.bfloat16),
            jax.ShapeDtypeStruct((8, depth), jnp.float32),
        ],
        compiler_params=params(56),
        cost_estimate=cost(2000),
        name="middle_bwd",
    )(start, out_grad, grad3, got3, hidden2, hidden1, cross_q, *texts, weights, weights, weights,
      gain2[None], gain3[None], token)


def middle_grads_kernel(so_l, cq_l, co_l, so_r, cq_r, co_r, out_ref, l_ref):
    i = pl.program_id(0)
    m = lax.rem(i, 3)

    @pl.when(i == 0)
    def _():
        for index, ref in enumerate((so_l, cq_l, co_l)):
            l_ref[index] = ref[...].T

    for index, ref in enumerate((so_r, cq_r, co_r)):

        @pl.when(m == index)
        def _():
            out_ref[...] = low(nn(l_ref[index], ref[...]))


def middle_grads(grad1, normed2, grad2, mixed, grad_cq, cmix):
    rows, depth = normed2.shape
    cols = depth // 4
    full = once((rows, depth), lambda i: (0, 0))
    quarter = pl.BlockSpec((rows, cols), lambda i: (0, i // 3))
    return pl.pallas_call(
        middle_grads_kernel,
        grid=(12,),
        in_specs=[full] * 3 + [quarter] * 3,
        out_specs=pl.BlockSpec((depth, cols), lambda i: (0, i)),
        out_shape=jax.ShapeDtypeStruct((depth, 3 * depth), jnp.bfloat16),
        scratch_shapes=[pltpu.VMEM((3, depth, rows), jnp.bfloat16)],
        compiler_params=params(40),
        cost_estimate=cost(0),
        name="middle_grads",
    )(grad1, normed2, grad2, mixed, grad_cq, cmix)


def block_grad_kernel(order_ref, x_ref, gq_ref, gkv_ref, back_ref, w0_ref, w1_ref, w2_ref, *refs):
    part_ref, g_ref, norms_ref, padded_ref = refs[-4:]
    i = pl.program_id(0)
    rows = x_ref.shape[0]
    skip = padded_ref.shape[1] - back_ref.shape[1]

    @pl.when(i == 0)
    def _():
        padded_ref[:, :skip, :] = jnp.zeros_like(padded_ref[:, :skip, :])
        padded_ref[:, skip:, :] = back_ref[...]
        norms_ref[...] = jnp.zeros_like(norms_ref)

    at = pl.ds(pl.multiple_of(order_ref[i] * rows, rows), rows)
    cols = gq_ref.shape[1]
    total = 0.0
    for index, w_ref in enumerate((w0_ref, w1_ref, w2_ref)):
        grad = gq_ref[...]
        if index:
            grad = low(gkv_ref[index - 1] + padded_ref[index - 1, at, :].astype(jnp.float32))
        g_ref[:, index * cols:(index + 1) * cols] = grad
        total = total + nt(grad, w_ref[...])
    unit, _ = normed(x_ref[...].astype(jnp.float32))
    norms_ref[0:1, :] += jnp.sum(total * unit, axis=0, keepdims=True)
    norms_ref[1:2, :] += jnp.sum(total, axis=0, keepdims=True)
    part_ref[0] = total.astype(part_ref.dtype)


def block_grad(order, count, block, grad_q, grad_kv, back, weights, before, after=()):
    width, depth = block.shape
    cols = grad_q.shape[1]
    rows = width // 4
    at = lambda i, order: (order[i], 0)
    w_spec = lambda j: once((depth, cols), lambda i, order: (0, j))
    return pl.pallas_call(
        block_grad_kernel,
        grid_spec=pltpu.PrefetchScalarGridSpec(
            num_scalar_prefetch=1,
            grid=(count,),
            in_specs=[
                pl.BlockSpec((rows, depth), at),
                pl.BlockSpec((rows, cols), at),
                pl.BlockSpec((2, rows, cols), lambda i, order: (0, order[i], 0)),
                once(back.shape, lambda i, order: (0, 0, 0)),
                w_spec(0),
                w_spec(1),
                w_spec(2),
            ]
            + [ANY] * (len(before) + len(after)),
            out_specs=[
                pl.BlockSpec((1, rows, depth), lambda i, order: (order[i], 0, 0)),
                pl.BlockSpec((rows, 3 * cols), at),
                pl.BlockSpec((8, depth), lambda i, order: (0, 0)),
            ],
            scratch_shapes=[pltpu.VMEM((2, width, cols), jnp.bfloat16)],
        ),
        out_shape=[
            jax.ShapeDtypeStruct((4, rows, depth), jnp.bfloat16),
            jax.ShapeDtypeStruct((width, 3 * cols), jnp.bfloat16),
            jax.ShapeDtypeStruct((8, depth), jnp.float32),
        ],
        input_output_aliases={8: 0, 9: 1} if before else {},
        compiler_params=params(48),
        cost_estimate=cost(0),
        name="block_grad",
    )(order, block, grad_q, grad_kv, back, weights, weights, weights, *before, *after)


def block_weights_kernel(at_ref, g_ref, text_ref, gtext_ref, out_ref):
    i = pl.program_id(0)

    @pl.when(i < 3)
    def _():
        out_ref[...] = low(nn(at_ref[...], g_ref[...]))

    @pl.when(i >= 3)
    def _():
        out_ref[...] = low(nn(text_ref[...].T, gtext_ref[...]))


def block_weights(normed1_t, grads, text, grad_text, after):
    depth, width = normed1_t.shape
    cols = grads.shape[1] // 3
    whole = lambda i: (0, 0)
    return pl.pallas_call(
        without(block_weights_kernel, 4, len(after)),
        grid=(5,),
        in_specs=[
            once((depth, width), whole),
            pl.BlockSpec((width, cols), lambda i: (0, jnp.minimum(i, 2))),
            once(text.shape, whole),
            pl.BlockSpec((text.shape[0], cols), lambda i: (0, jnp.maximum(i - 3, 0))),
        ]
        + [ANY] * len(after),
        out_specs=pl.BlockSpec((depth, cols), lambda i: (0, i)),
        out_shape=jax.ShapeDtypeStruct((depth, 5 * cols), jnp.bfloat16),
        compiler_params=params(40),
        cost_estimate=cost(0),
        name="block_weights",
    )(normed1_t, grads, text, grad_text, *after)


def round_kernel(_, up_sum_ref, down_sum_ref, up_ref, down_ref, up_out_ref, down_out_ref):
    up_out_ref[...] = low(up_sum_ref[0].astype(jnp.float32) + up_ref[...].astype(jnp.float32))
    down_out_ref[...] = low(down_sum_ref[0].astype(jnp.float32) + down_ref[...].astype(jnp.float32))


def round_sums(targets, sums, up, down, after, micros):
    rows, depth = up.shape
    size = rows // 4
    flat = pl.BlockSpec((size, depth), lambda i, targets: (i, 0))
    return pl.pallas_call(
        without(round_kernel, 5, len(after)),
        grid_spec=pltpu.PrefetchScalarGridSpec(
            num_scalar_prefetch=1,
            grid=(4,),
            in_specs=[
                pl.BlockSpec((1, size, depth), lambda i, targets: (targets[0], i, 0)),
                pl.BlockSpec((1, size, depth), lambda i, targets: (targets[1], i, 0)),
                flat,
                flat,
            ]
            + [ANY] * len(after),
            out_specs=[flat, flat],
        ),
        out_shape=[jax.ShapeDtypeStruct((rows, depth), jnp.bfloat16)] * 2,
        compiler_params=params(24),
        cost_estimate=cost(micros),
        name="round_sums",
    )(targets, sums, sums, up, down, *after)


def last_kernel(_, sum_ref, up_ref, down_ref, x_ref, grad_ref, gain_ref, out_ref):
    total = sum_ref[0].astype(jnp.float32) + up_ref[...].astype(jnp.float32) + down_ref[...].astype(jnp.float32)
    back, _, _ = norm_back_kernel(x_ref[...].astype(jnp.float32), gain_ref[...], total)
    out_ref[...] = grad_ref[...] + back


def last_sums(place, sums, up, down, tokens, grad, gain, after):
    rows, depth = up.shape
    size = rows // 4
    flat = pl.BlockSpec((size, depth), lambda i, place: (i, 0))
    return pl.pallas_call(
        without(last_kernel, 7, len(after)),
        grid_spec=pltpu.PrefetchScalarGridSpec(
            num_scalar_prefetch=1,
            grid=(4,),
            in_specs=[pl.BlockSpec((1, size, depth), lambda i, place: (place[0], i, 0))]
            + [flat] * 4
            + [pl.BlockSpec((1, depth), lambda i, place: (0, 0))]
            + [ANY] * len(after),
            out_specs=flat,
        ),
        out_shape=jax.ShapeDtypeStruct((rows, depth), jnp.float32),
        compiler_params=params(24),
        cost_estimate=cost(0),
        name="last_sums",
    )(place, sums, up, down, tokens, grad, gain[None], *after)


def piece_kernel(own_ref, first_ref, second_ref, third_ref, out_ref):
    out_ref[...] = (own_ref[...].astype(jnp.float32) + first_ref[...].astype(jnp.float32)) + (
        second_ref[...].astype(jnp.float32) + third_ref[...].astype(jnp.float32)
    )


def piece_sums(pieces, after):
    rows, cols = pieces[0].shape
    return pl.pallas_call(
        without(piece_kernel, 4, len(after)),
        in_specs=[pl.BlockSpec(memory_space=pltpu.VMEM)] * 4 + [ANY] * len(after),
        out_specs=pl.BlockSpec(memory_space=pltpu.VMEM),
        out_shape=jax.ShapeDtypeStruct((rows, cols), jnp.float32),
        compiler_params=params(24),
        cost_estimate=cost(0),
        name="piece_sums",
    )(*pieces, *after)


def turned(value, axis, steps):
    count = lax.axis_size(axis)
    return lax.ppermute(value, axis, [(source, (source + steps) % count) for source in range(count)])


def swapped(value, bit):
    return lax.ppermute(value, "tp", [(source, source ^ bit) for source in range(lax.axis_size("tp"))])


def moved(value, steps, senders):
    return lax.ppermute(value, "tp", [(source, source + steps) for source in senders])


def along_line(value):
    count = lax.axis_size("tp")
    up, down = [value], [value]
    for round_at in range(count - 1):
        up.append(moved(up[-1], 1, range(round_at, count - 1)))
        down.append(moved(down[-1], -1, range(1, count - round_at)))
    return up, down


def picked(value, index):
    return lax.dynamic_index_in_dim(value, index % value.shape[0], 0, keepdims=True)


def exchanged(value, place):
    count = lax.axis_size("tp")
    return [value] + [turned(picked(value, place + step), "tp", step) for step in range(1, count)]


def in_order(parts, place):
    out = jnp.zeros((len(parts),) + parts[0].shape, parts[0].dtype)
    for step, part in enumerate(parts):
        out = lax.dynamic_update_slice_in_dim(out, part[None], (place + len(parts) - step) % len(parts), 0)
    return out


def dot(left, right):
    return jnp.dot(left, right, preferred_element_type=jnp.float32)


def dot_last(left, right):
    return jnp.einsum("ra,ba->rb", left, right, preferred_element_type=jnp.float32)


def split_mlp(values):
    return values[:2], values[2], values[3]


def on_device(
    tokens,
    text_states,
    clip_start,
    ln1_gain,
    ln1_bias,
    self_query,
    self_key,
    self_value,
    self_out,
    ln2_gain,
    ln2_bias,
    cross_query,
    cross_key,
    cross_value,
    cross_out,
    ln3_gain,
    ln3_bias,
    fc_in,
    fc_out,
    out_grad,
):
    place, members = lax.axis_index("wide"), lax.axis_size("wide")
    part, parts = lax.axis_index("tp"), lax.axis_size("tp")
    here = lax.dynamic_index_in_dim(clip_start, place, 0, keepdims=False)
    before = lax.dynamic_index_in_dim(clip_start, (place + members - 1) % members, 0, keepdims=False)
    start = jnp.stack([here, before, part]).astype(jnp.int32)
    rows, depth = tokens.shape
    width = rows * parts
    cols, units = self_query.shape[1], fc_in.shape[1]
    texts = text_states.shape[0]
    scalars = lambda *values: jnp.stack([jnp.asarray(value, jnp.int32) for value in values])

    def gathered(value):
        return lax.all_gather(value, "wide", axis=0, tiled=True)

    weights1 = gathered(jnp.concatenate([self_query, self_key, self_value, cross_key, cross_value], 1))
    fc_shards = jnp.concatenate([fc_in, fc_out.T], 1)
    text_at = 3 * cols
    first, last = part == 0, part == parts - 1
    first, last = part == 0, part == parts - 1
    (_, up1, up2, up3), (_, down1, down2, down3) = along_line(tokens)
    shards = jnp.concatenate([self_out.T, cross_query, cross_out.T], 1)
    weights2 = lax.all_gather(shards, ("tp", "wide"), axis=0, tiled=True)

    block = qkv_block(scalars(part, 0), [tokens], ln1_gain, ln1_bias, weights1, 0, width, cols, None)
    at = scalars(jnp.where(first, 1, part - 1), jnp.where(first, 1, 0))
    block = qkv_block(at, [up1, down1], ln1_gain, ln1_bias, weights1, 0, width, cols, block)
    at = scalars((part + 2) % parts, jnp.where(part >= 2, 0, 1))
    block = qkv_block(at, [up2, down2], ln1_gain, ln1_bias, weights1, 0, width, cols, block)
    at = scalars(jnp.where(first, parts - 1, (part + 1) % parts), jnp.where(first, 2, jnp.where(last, 1, 0)))
    text_kv = low(dot(tie(text_states, block[0]), weights1[:, text_at:]))
    text_kv = jnp.concatenate([turned(text_kv, "wide", 1), text_kv], 0)
    block = qkv_block(
        at, [down1, up3, down3], ln1_gain, ln1_bias, weights1, 0, width, cols, block, [text_kv]
    )
    block, _, normed1_t, qkv = block
    kv_old = turned(qkv[MIN_START:, cols:], "wide", 1)
    weights_fc = gathered(tie(fc_shards, qkv))
    grad_out = [out_grad, swapped(tie(out_grad, up3, down3), 1)]
    fc_in_other = swapped(tie(fc_in, up3, down3), 2)
    text_kv = [text_kv] + [turned(text_kv, "tp", step) for step in range(1, parts)]
    mixed, mixed_t, logs = self_fwd(start, qkv, kv_old, [])
    mixed = exchanged(tie(mixed, grad_out[1], fc_in_other, *text_kv).reshape(parts, rows, cols), part)
    fc_out_other = swapped(tie(fc_out.T, *mixed[1:]), 2)
    mixed, hidden1, normed2, cross_q, cmix, hidden2, normed3 = middle_fwd(
        start, tokens, mixed, text_kv, weights2, ln2_gain, ln2_bias, ln3_gain, ln3_bias
    )

    def summed(value):
        return lax.psum_scatter(value, "wide", scatter_dimension=0, tiled=True)

    weights3 = gathered(jnp.concatenate([fc_in_other, tie(fc_out_other, normed3)], 1))

    normed3 = [normed3, swapped(normed3, 1)]
    kept, *sums_own = split_mlp(mlp(normed3[0], grad_out[0], weights_fc, units, 0, None, None))
    kept, *sums_theirs = split_mlp(mlp(normed3[1], grad_out[1], weights_fc, units, 1, kept, None))
    grads_own = mlp_grads(normed3, grad_out, kept[1], kept[0])
    after_own = tie(sums_theirs[0], weights3, grads_own, micros=2000)
    kept_other, *sums_theirs = split_mlp(
        mlp(normed3[1], grad_out[1], weights3, units, 1, None, (after_own, sums_theirs[1]))
    )
    got3 = swapped(low(sums_theirs[0]), 1)
    kept_other, *sums_own = split_mlp(mlp(normed3[0], grad_out[0], weights3, units, 0, kept_other, sums_own))
    grads_other = mlp_grads(normed3, grad_out, kept_other[1], kept_other[0])

    grad1, grad1_low, grad2_low, grad_cq, grad_text, grad_mixed, norms23 = middle_bwd(
        start, out_grad, sums_own[0], got3, hidden2, hidden1, cross_q, text_kv, weights2, ln2_gain, ln3_gain, grads_other
    )
    outer = swapped(low(sums_theirs[1]), 1)
    layer_out = low(hidden2 + sums_own[1] + outer.astype(jnp.float32))
    grad_mixed = exchanged(tie(grad_mixed, outer), part)
    grads_middle = middle_grads(grad1_low, normed2, grad2_low, mixed, grad_cq, cmix)

    grad_text = exchanged(tie(grad_text, grads_middle), part)
    grads_own = summed(grads_own)
    grad_kv_old, grad_query_t = self_bwd(start, qkv, kv_old, grad_mixed, mixed_t, logs, None, [grads_own])
    grad_kv_back = turned(grad_kv_old, "wide", -1)
    grad_text = [tie(picked(grad_text[0], part), grad_query_t)] + grad_text[1:]
    grad_text = sum(piece[0].astype(jnp.float32) for piece in grad_text)
    back = turned(low(grad_text[:, :texts]), "wide", -1).astype(jnp.float32)
    grads_other = summed(grads_other)
    grad_text = low(grad_text[:, texts:] + back)
    grad_text = jnp.concatenate([grad_text[0], grad_text[1]], 1)
    text_term = low(dot_last(grad_text, weights1[:, text_at:]))
    grad_kv, grad_query = self_bwd(
        start, qkv, None, grad_mixed, mixed_t, logs, grad_query_t, [text_term, grads_other]
    )
    text_term = [text_term] + [turned(text_term, "tp", step) for step in range(1, parts)]
    grads_other = swapped(grads_other, 2)

    block_args = (block, grad_query, grad_kv, grad_kv_back, weights1)
    near, far = part < parts // 2, parts - 1
    sums, grad_qkv, norms_first = block_grad(scalars(jnp.where(near, far, 0)), 1, *block_args, [], text_term)
    own_first = picked(sums, jnp.where(near, far, 0))[0]
    up, down = moved(own_first, 1, (0,)), moved(own_first, -1, (far,))
    others = scalars(
        jnp.where(near, 2, 1),
        jnp.where(first, 1, jnp.where(last, 2, jnp.where(near, 0, far))),
        part,
    )
    sums, grad_qkv, norms_rest = block_grad(others, 3, *block_args, [sums, grad_qkv], [grads_other])
    grads_block = block_weights(normed1_t, grad_qkv, text_states, grad_text, [])
    norms = jnp.concatenate([norms_first[:2] + norms_rest[:2], norms23[:4]], 0)
    grads_middle = summed(grads_middle)
    pieces = [
        lax.dynamic_slice_in_dim(grads_middle, ((part + step) % parts) * 3 * cols, 3 * cols, 1) for step in range(parts)
    ]
    grads_middle = piece_sums([pieces[0]] + [turned(pieces[step], "tp", step) for step in range(1, parts)], [])
    after = []
    for round_at in (2, 3):
        targets = scalars((part + parts - round_at) % parts, (part + round_at) % parts)
        up, down = round_sums(targets, sums, up, down, after, 2000 if round_at == 3 else 0)
        norms = norms + tie(swapped(norms, round_at - 1), grads_block, pieces[0])
        up, down = moved(up, 1, range(round_at)), moved(down, -1, range(parts - round_at, parts))
        after = [norms, grads_block, grads_middle]
    tokens_grad = last_sums(scalars(part), sums, up, down, tokens, grad1, ln1_gain, [norms])
    bit = 1
    while bit < members:
        norms = norms + lax.ppermute(norms, "wide", [(source, source ^ bit) for source in range(members)])
        bit *= 2
    text_grad = jnp.sum(in_order([tie(text_term[0], up)] + text_term[1:], part).astype(jnp.float32), 0)

    fc_grads = grads_own.astype(jnp.float32) + grads_other.astype(jnp.float32)
    fc_in_grad, fc_out_grad = fc_grads[:, :units], fc_grads[:, units:].T
    grads_block = tie(summed(grads_block), up).astype(jnp.float32)
    grads_block = [grads_block[:, i * cols : (i + 1) * cols] for i in range(5)]
    grads_middle = [grads_middle[:, i * cols : (i + 1) * cols] for i in range(3)]

    return (
        layer_out,
        tokens_grad,
        text_grad,
        norms[0],
        norms[1],
        grads_block[0],
        grads_block[1],
        grads_block[2],
        grads_middle[0].T,
        norms[2],
        norms[3],
        grads_middle[1],
        grads_block[3],
        grads_block[4],
        grads_middle[2].T,
        norms[4],
        norms[5],
        fc_in_grad,
        fc_out_grad,
    )


def solution(mesh):
    in_specs = (
        P(("wide", "tp"), None),
        P("wide", None),
        P(),
        P(),
        P(),
        P("wide", "tp"),
        P("wide", "tp"),
        P("wide", "tp"),
        P("tp", "wide"),
        P(),
        P(),
        P("wide", "tp"),
        P("wide", "tp"),
        P("wide", "tp"),
        P("tp", "wide"),
        P(),
        P(),
        P("wide", "tp"),
        P("tp", "wide"),
        P(("wide", "tp"), None),
    )
    out_specs = (
        P(("wide", "tp"), None),
        P(("wide", "tp"), None),
        P("wide", None),
        P(),
        P(),
        P("wide", "tp"),
        P("wide", "tp"),
        P("wide", "tp"),
        P("tp", "wide"),
        P(),
        P(),
        P("wide", "tp"),
        P("wide", "tp"),
        P("wide", "tp"),
        P("tp", "wide"),
        P(),
        P(),
        P("wide", "tp"),
        P("tp", "wide"),
    )
    return jax.shard_map(
        on_device, mesh=mesh, in_specs=in_specs, out_specs=out_specs, check_vma=False
    )
```

```python
import functools

import jax
import jax.numpy as jnp
from jax import lax
from jax.experimental import pallas as pl
from jax.experimental.pallas import tpu as pltpu
from jax.sharding import PartitionSpec as P

HEAD_DIM = 64
PAIR = 2 * HEAD_DIM
LOG2E = 1.4426950408889634
MIN_START = 512
TILE = 512

COST_SCALE = 1.0

epsilon = 1e-05
masked_score = -1e30


def nn(a, b):
    return lax.dot_general(a, b, (((1,), (0,)), ((), ())), preferred_element_type=jnp.float32)


def nt(a, b):
    return lax.dot_general(a, b, (((1,), (1,)), ((), ())), preferred_element_type=jnp.float32)


def low(value):
    return value.astype(jnp.bfloat16)


def lanes_of(value, head):
    lane = lax.broadcasted_iota(jnp.int32, value.shape, 1)
    return jnp.where((lane >= head * HEAD_DIM) & (lane < (head + 1) * HEAD_DIM), value, 0).astype(value.dtype)


def half(head):
    return slice(head * HEAD_DIM, (head + 1) * HEAD_DIM)


def normed(value):
    centred = value - jnp.mean(value, axis=-1, keepdims=True)
    scale = lax.rsqrt(jnp.mean(centred * centred, axis=-1, keepdims=True) + epsilon)
    return centred * scale, scale


def norm_kernel(value, gain, shift):
    return normed(value)[0] * gain + shift


def norm_back_kernel(value, gain, grad):
    unit, scale = normed(value)
    inner = grad * gain
    back = inner - jnp.mean(inner, axis=-1, keepdims=True) - unit * jnp.mean(inner * unit, axis=-1, keepdims=True)
    return back * scale, jnp.sum(grad * unit, axis=0, keepdims=True), jnp.sum(grad, axis=0, keepdims=True)


def params(mib):
    return pltpu.CompilerParams(vmem_limit_bytes=mib * 2**20)


def cost(micros):
    return pl.CostEstimate(flops=int(micros * 1e9 * COST_SCALE), bytes_accessed=0, transcendentals=0)


def once(shape, at):
    return pl.BlockSpec(shape, at, pipeline_mode=pl.Buffered(1))


ANY = pl.BlockSpec(memory_space=pl.ANY)
SMEM = pl.BlockSpec(memory_space=pltpu.SMEM)


def without(kernel, at, count):
    return lambda *refs: kernel(*refs[:at], *refs[at + count:])


def tie_kernel(*refs):
    pass


def tie(value, *tokens, micros=0):
    return pl.pallas_call(
        tie_kernel,
        in_specs=[ANY] * (1 + len(tokens)),
        out_specs=ANY,
        out_shape=jax.ShapeDtypeStruct(value.shape, value.dtype),
        input_output_aliases={0: 0},
        cost_estimate=cost(micros),
        name="tie",
    )(value, *tokens)


def qkv_kernel(count, first, at_ref, *refs):
    blocks, refs = refs[:count], refs[count:]
    gain_ref, shift_ref, w_ref = refs[:3]
    x_ref, a_ref, at_out_ref, qkv_ref, kept_ref = refs[3 if first else 7:]

    @pl.when(pl.program_id(0) == 0)
    def _():
        value = blocks[0][...]
        for index in range(1, count):
            value = jnp.where(at_ref[1] == index, blocks[index][...], value)
        x_ref[...] = value
        kept_ref[...] = low(norm_kernel(value.astype(jnp.float32), gain_ref[...], shift_ref[...]))
        a_ref[...] = kept_ref[...]
        at_out_ref[...] = kept_ref[...].T

    qkv_ref[...] = low(nn(kept_ref[...], w_ref[...]))


def qkv_block(at, blocks, gain, shift, weights, column, width, cols, before, after=()):
    rows, depth = blocks[0].shape
    first = before is None
    count = len(blocks)
    whole = lambda j, at: (0, 0)
    here = lambda j, at: (at[0], 0)
    return pl.pallas_call(
        without(functools.partial(qkv_kernel, count, first), count + (4 if first else 8), len(after)),
        grid_spec=pltpu.PrefetchScalarGridSpec(
            num_scalar_prefetch=1,
            grid=(3,),
            in_specs=[once((rows, depth), whole)] * count
            + [once((1, depth), whole)] * 2
            + [pl.BlockSpec((depth, cols), lambda j, at: (0, column // cols + j))]
            + ([] if first else [ANY] * 4)
            + [ANY] * len(after),
            out_specs=[
                pl.BlockSpec((rows, depth), here),
                pl.BlockSpec((rows, depth), here),
                pl.BlockSpec((depth, rows), lambda j, at: (0, at[0])),
                pl.BlockSpec((rows, cols), lambda j, at: (at[0], j)),
            ],
            scratch_shapes=[pltpu.VMEM((rows, depth), jnp.bfloat16)],
        ),
        out_shape=[
            jax.ShapeDtypeStruct((width, depth), jnp.bfloat16),
            jax.ShapeDtypeStruct((width, depth), jnp.bfloat16),
            jax.ShapeDtypeStruct((depth, width), jnp.bfloat16),
            jax.ShapeDtypeStruct((width, 3 * cols), jnp.bfloat16),
        ],
        input_output_aliases={} if first else {count + 4 + i: i for i in range(4)},
        compiler_params=params(40),
        cost_estimate=cost(0),
        name="qkv_block",
    )(at, *blocks, gain[None], shift[None], weights, *(before or ()), *after)


def first_of(rows, here, before, width):
    return jnp.where(rows >= here, here, before - width)


def self_fwd_kernel(tile_size, skip, start_ref, q_ref, k_ref, v_ref, kp_ref, vp_ref, o_ref, ot_ref, l_ref, vt_ref, vpt_ref):
    width, old = q_ref.shape[0], kp_ref.shape[0]
    size = tile_size
    here, before = start_ref[0], start_ref[1]
    factor = HEAD_DIM ** (-0.5) * LOG2E
    vt_ref[...] = v_ref[...].T
    vpt_ref[...] = vp_ref[...].T
    for i in range(width // size):
        rows = i * size + lax.broadcasted_iota(jnp.int32, (1, size), 1)
        first = first_of(rows, here, before, width)
        query = q_ref[i * size:(i + 1) * size, :]

        def tile(key_ref, value_ref, j, place, causal, carry):
            at = pl.multiple_of(j * size, size)
            keys = key_ref[pl.ds(at, size), :]
            places = place + j * size + lax.broadcasted_iota(jnp.int32, (size, 1), 0)
            allowed = places >= first
            if causal:
                allowed = allowed & (places <= rows)
            out = []
            for head in range(2):
                top, total, acc = carry[head]
                scores = jnp.where(allowed, nt(lanes_of(keys, head), query) * factor, masked_score)
                peak = jnp.maximum(top, jnp.max(scores, axis=0, keepdims=True))
                shrink = jnp.exp2(top - peak)
                probs = jnp.exp2(scores - peak)
                total = total * shrink + jnp.sum(probs, axis=0, keepdims=True)
                part = nn(value_ref[half(head), pl.ds(at, size)], low(probs))
                out.append((peak, total, acc * shrink + part))
            return tuple(out)

        carry = tuple(
            (
                jnp.full((1, size), masked_score, jnp.float32),
                jnp.zeros((1, size), jnp.float32),
                jnp.zeros((HEAD_DIM, size), jnp.float32),
            )
            for _ in range(2)
        )
        if i * size < skip + old:
            start = jnp.where(here > i * size, (before - skip) // size, old // size)
            carry = lax.fori_loop(
                start, old // size, lambda j, c: tile(kp_ref, vpt_ref, j, skip - width, False, c), carry
            )
        start = jnp.where(here > i * size, 0, here // size)
        carry = lax.fori_loop(start, i, lambda j, c: tile(k_ref, vt_ref, j, 0, False, c), carry)
        carry = tile(k_ref, vt_ref, i, 0, True, carry)
        for head in range(2):
            top, total, acc = carry[head]
            ot_ref[half(head), i * size:(i + 1) * size] = acc / total
            l_ref[0, head:head + 1, i * size:(i + 1) * size] = top + jnp.log2(total)
    o_ref[...] = low(ot_ref[...].T)


def self_fwd(start, qkv, kv_old, after):
    width, cols = qkv.shape[0], qkv.shape[1] // 3
    old = kv_old.shape[0]
    pairs = cols // PAIR
    return pl.pallas_call(
        without(functools.partial(self_fwd_kernel, TILE, width - old), 6, len(after)),
        grid=(pairs,),
        in_specs=[
            SMEM,
            pl.BlockSpec((width, PAIR), lambda p: (0, p)),
            pl.BlockSpec((width, PAIR), lambda p: (0, p + pairs)),
            pl.BlockSpec((width, PAIR), lambda p: (0, p + 2 * pairs)),
            pl.BlockSpec((old, PAIR), lambda p: (0, p)),
            pl.BlockSpec((old, PAIR), lambda p: (0, p + pairs)),
        ]
        + [ANY] * len(after),
        out_specs=[
            pl.BlockSpec((width, PAIR), lambda p: (0, p)),
            pl.BlockSpec((PAIR, width), lambda p: (p, 0)),
            pl.BlockSpec((1, 8, width), lambda p: (p, 0, 0)),
        ],
        out_shape=[
            jax.ShapeDtypeStruct((width, cols), jnp.bfloat16),
            jax.ShapeDtypeStruct((cols, width), jnp.float32),
            jax.ShapeDtypeStruct((pairs, 8, width), jnp.float32),
        ],
        scratch_shapes=[pltpu.VMEM((PAIR, width), jnp.bfloat16), pltpu.VMEM((PAIR, old), jnp.bfloat16)],
        compiler_params=params(40),
        cost_estimate=cost(0),
        name="self_fwd",
    )(start, qkv, qkv, qkv, kv_old, kv_old, *after)


def self_bwd_kernel(tile_size, skip, old, start_ref, q_ref, k_ref, v_ref, go0_ref, go1_ref, go2_ref, go3_ref, ot_ref, l_ref, *rest):
    if old:
        gkv_ref, gq_ref, kt_ref, delta_ref, go_ref = rest
    else:
        gq_in_ref, gkv_ref, gq_ref, kt_ref, delta_ref, go_ref, sum_ref = rest
    width, count = q_ref.shape[0], k_ref.shape[0]
    size = tile_size
    here, before, part = start_ref[0], start_ref[1], start_ref[2]
    factor = HEAD_DIM ** (-0.5) * LOG2E
    rows_each = go1_ref.shape[1]
    for step, ref in enumerate((go0_ref, go1_ref, go2_ref, go3_ref)):
        at = pl.multiple_of(lax.rem(part + 4 - step, 4) * rows_each, rows_each)
        go_ref[pl.ds(at, rows_each), :] = ref[part if step == 0 else 0]
    kt_ref[...] = k_ref[...].T
    got = go_ref[...].T.astype(jnp.float32) * ot_ref[...]
    for head in range(2):
        delta_ref[head:head + 1, :] = jnp.sum(got[half(head), :], axis=0, keepdims=True)
    acc_ref = gq_ref if old else sum_ref
    acc_ref[...] = jnp.zeros_like(acc_ref) if old else gq_in_ref[...]
    for j in range(count // size):
        place = j * size + (skip - width if old else 0)
        keys = k_ref[j * size:(j + 1) * size, :]
        values = v_ref[j * size:(j + 1) * size, :]
        keys_of = [lanes_of(keys, head) for head in range(2)]
        values_of = [lanes_of(values, head) for head in range(2)]
        places = place + lax.broadcasted_iota(jnp.int32, (size, 1), 0)

        def tile(i, causal, carry):
            at = pl.multiple_of(i * size, size)
            query = q_ref[pl.ds(at, size), :]
            grad = go_ref[pl.ds(at, size), :]
            rows = i * size + lax.broadcasted_iota(jnp.int32, (1, size), 1)
            allowed = places >= first_of(rows, here, before, width)
            if causal:
                allowed = allowed & (places <= rows)
            grad_keys, grad_values = carry
            for head in range(2):
                scores = nt(keys_of[head], query) * factor - l_ref[0, head:head + 1, pl.ds(at, size)]
                probs = jnp.where(allowed, jnp.exp2(scores), 0.0)
                grad_probs = nt(values_of[head], grad)
                grad_scores = low(probs * (grad_probs - delta_ref[head:head + 1, pl.ds(at, size)]))
                grad_values = grad_values + nn(low(probs), lanes_of(grad, head))
                grad_keys = grad_keys + nn(grad_scores, lanes_of(query, head))
                acc_ref[half(head), pl.ds(at, size)] += nn(kt_ref[half(head), j * size:(j + 1) * size], grad_scores)
            return (grad_keys, grad_values)

        zero = jnp.zeros((size, PAIR), jnp.float32)
        carry = (zero, zero)
        if old:
            high = jnp.where(before < place + size + width, (here + size - 1) // size, 0)
            carry = lax.fori_loop(0, high, lambda i, c: tile(i, False, c), carry)
        else:
            high = jnp.where(here >= place + size, (here + size - 1) // size, width // size)
            carry = tile(j, True, carry)
            carry = lax.fori_loop(j + 1, high, lambda i, c: tile(i, False, c), carry)
        gkv_ref[0, j * size:(j + 1) * size, :] = (carry[0] * HEAD_DIM ** (-0.5)).astype(gkv_ref.dtype)
        gkv_ref[1, j * size:(j + 1) * size, :] = carry[1].astype(gkv_ref.dtype)
    if not old:
        gq_ref[...] = low((acc_ref[...] * HEAD_DIM ** (-0.5)).T)


def self_bwd(start, qkv, kv_old, grads, mixed_t, logs, sums, after):
    width, cols = qkv.shape[0], qkv.shape[1] // 3
    old = kv_old is not None
    count = kv_old.shape[0] if old else width
    pairs = cols // PAIR
    rows = grads[1].shape[1]
    across = pl.BlockSpec((PAIR, width), lambda p: (p, 0))
    along = pl.BlockSpec((width, PAIR), lambda p: (0, p))
    key_at, value_at = (0, pairs) if old else (pairs, 2 * pairs)
    return pl.pallas_call(
        without(functools.partial(self_bwd_kernel, TILE, width - count, old), 10 if old else 11, len(after)),
        grid=(pairs,),
        in_specs=[
            SMEM,
            along,
            pl.BlockSpec((count, PAIR), lambda p: (0, p + key_at)),
            pl.BlockSpec((count, PAIR), lambda p: (0, p + value_at)),
            pl.BlockSpec((4, rows, PAIR), lambda p: (0, 0, p)),
            pl.BlockSpec((1, rows, PAIR), lambda p: (0, 0, p)),
            pl.BlockSpec((1, rows, PAIR), lambda p: (0, 0, p)),
            pl.BlockSpec((1, rows, PAIR), lambda p: (0, 0, p)),
            across,
            pl.BlockSpec((1, 8, width), lambda p: (p, 0, 0)),
        ]
        + ([] if old else [across])
        + [ANY] * len(after),
        out_specs=[pl.BlockSpec((2, count, PAIR), lambda p: (0, 0, p)), across if old else along],
        out_shape=[
            jax.ShapeDtypeStruct((2, count, cols), jnp.bfloat16 if old else jnp.float32),
            jax.ShapeDtypeStruct((cols, width), jnp.float32)
            if old
            else jax.ShapeDtypeStruct((width, cols), jnp.bfloat16),
        ],
        scratch_shapes=[
            pltpu.VMEM((PAIR, count), jnp.bfloat16),
            pltpu.VMEM((8, width), jnp.float32),
            pltpu.VMEM((width, PAIR), jnp.bfloat16),
        ]
        + ([] if old else [pltpu.VMEM((PAIR, width), jnp.float32)]),
        compiler_params=params(40),
        cost_estimate=cost(0 if old else 2000),
        name="self_bwd_old" if old else "self_bwd_own",
    )(start, qkv, *((kv_old,) * 2 if old else (qkv,) * 2), *grads, mixed_t, logs, *([] if old else [sums]), *after)


def cross_probs(here, place, cq, keys_of, count):
    scores = nt(keys_of, cq) * (HEAD_DIM ** (-0.5) * LOG2E)
    rows = place + lax.broadcasted_iota(jnp.int32, (1, cq.shape[0]), 1)
    places = lax.broadcasted_iota(jnp.int32, (2 * count, 1), 0)
    scores = jnp.where((places < count) == (rows < here), scores, masked_score)
    probs = jnp.exp2(scores - jnp.max(scores, axis=0, keepdims=True))
    return probs / jnp.sum(probs, axis=0, keepdims=True)


def chosen(step, refs, own):
    value = own
    for index in range(1, 4):
        value = jnp.where(step == index, refs[index][...], value)
    return value


def middle_fwd_kernel(
    start_ref, x_ref, o0_ref, o1_ref, o2_ref, o3_ref, t0_ref, t1_ref, t2_ref, t3_ref,
    so_ref, cq_ref, co_ref, g2_ref, b2_ref, g3_ref, b3_ref,
    mixed_ref, h1_ref, a2_ref, cq_out_ref, cmix_ref, h2_ref, a3_ref, acc_ref,
):
    i = pl.program_id(0)
    here, part = start_ref[0], start_ref[2]
    rows, cols = o1_ref.shape[1], o1_ref.shape[2]
    t = lax.rem(i, 4)
    step = lax.rem(part + 4 - t, 4)

    @pl.when(i < 4)
    def _():
        piece = o0_ref[0]
        for index, ref in ((1, o1_ref), (2, o2_ref), (3, o3_ref)):
            piece = jnp.where(step == index, ref[0], piece)
        mixed_ref[...] = piece
        term = nt(piece, so_ref[...])

        @pl.when(i == 0)
        def _():
            acc_ref[...] = term + x_ref[...].astype(jnp.float32)

        @pl.when(i > 0)
        def _():
            acc_ref[...] += term

        @pl.when(i == 3)
        def _():
            h1_ref[...] = acc_ref[...]
            a2_ref[...] = low(norm_kernel(acc_ref[...], g2_ref[...], b2_ref[...]))

    @pl.when(i >= 4)
    def _():
        cq = low(nn(a2_ref[...], cq_ref[...]))
        cq_out_ref[...] = cq
        text = chosen(step, (t0_ref, t1_ref, t2_ref, t3_ref), t0_ref[...])
        count = text.shape[0] // 2
        keys, values = text[:, :cols], text[:, cols:]
        parts = []
        for pair in range(cols // PAIR):
            at = slice(pair * PAIR, (pair + 1) * PAIR)
            values_t = values[:, at].T
            for head in range(2):
                probs = cross_probs(here, part * rows, cq[:, at], lanes_of(keys[:, at], head), count)
                parts.append(nn(values_t[half(head), :], low(probs)))
        cmix = low(jnp.concatenate(parts, 0).T)
        cmix_ref[...] = cmix
        acc_ref[...] += nt(cmix, co_ref[...])

        @pl.when(i == 7)
        def _():
            h2_ref[...] = acc_ref[...]
            a3_ref[...] = low(norm_kernel(acc_ref[...], g3_ref[...], b3_ref[...]))


def middle_fwd(start, tokens, mixed, texts, weights, gain2, shift2, gain3, shift3):
    rows, depth = tokens.shape
    cols = mixed[1].shape[2]
    whole = lambda i, s: (0, 0)
    early = lambda i, s: (0, jnp.minimum(i, 3))
    late = lambda i, s: (0, jnp.maximum(i - 4, 0))
    vector = once((1, depth), whole)
    wide16 = jax.ShapeDtypeStruct((rows, depth), jnp.bfloat16)
    wide32 = jax.ShapeDtypeStruct((rows, depth), jnp.float32)
    return pl.pallas_call(
        middle_fwd_kernel,
        grid_spec=pltpu.PrefetchScalarGridSpec(
            num_scalar_prefetch=1,
            grid=(8,),
            in_specs=[once((rows, depth), whole)]
            + [once((1, rows, cols), lambda i, s: (s[2], 0, 0))]
            + [once((1, rows, cols), lambda i, s: (0, 0, 0))] * 3
            + [once(texts[0].shape, whole)] * 4
            + [
                pl.BlockSpec((depth, cols), lambda i, s: (jnp.minimum(i, 3), 0)),
                pl.BlockSpec((depth, cols), lambda i, s: (jnp.maximum(i - 4, 0), 1)),
                pl.BlockSpec((depth, cols), lambda i, s: (jnp.maximum(i - 4, 0), 2)),
            ]
            + [vector] * 4,
            out_specs=[
                pl.BlockSpec((rows, cols), early),
                pl.BlockSpec((rows, depth), whole),
                pl.BlockSpec((rows, depth), whole),
                pl.BlockSpec((rows, cols), late),
                pl.BlockSpec((rows, cols), late),
                pl.BlockSpec((rows, depth), whole),
                pl.BlockSpec((rows, depth), whole),
            ],
            scratch_shapes=[pltpu.VMEM((rows, depth), jnp.float32)],
        ),
        out_shape=[wide16, wide32, wide16, wide16, wide16, wide32, wide16],
        compiler_params=params(48),
        cost_estimate=cost(0),
        name="middle_fwd",
    )(start, tokens, *mixed, *texts, weights, weights, weights, gain2[None], shift2[None], gain3[None], shift3[None])


def mlp_kernel(first, a_ref, g_ref, w1_ref, w2_ref, *refs):
    m_ref, gu_ref, ga_ref, y_ref = refs[-4:]
    i = pl.program_id(0)

    @pl.when(i == 0)
    def _():
        if first:
            ga_ref[...] = jnp.zeros_like(ga_ref)
            y_ref[...] = jnp.zeros_like(y_ref)
        else:
            ga_ref[...] = refs[0][...]
            y_ref[...] = refs[1][...]

    w1, w2 = w1_ref[...], w2_ref[...]
    inner = nn(a_ref[...], w1)
    chance = 0.5 + 0.5 * lax.erf(inner * 0.5**0.5)
    active = low(inner * chance)
    slope = chance + inner * (0.3989422804014327 * jnp.exp(-0.5 * inner * inner))
    grad_inner = low(nn(g_ref[...], w2) * slope)
    m_ref[...] = active
    gu_ref[...] = grad_inner
    y_ref[...] += nt(active, w2)
    ga_ref[...] += nt(grad_inner, w1)


def mlp(normed3, grads, weights, units, row, kept, sums, after=()):
    rows, depth = normed3.shape
    size = 512
    first = sums is None
    whole = lambda i: (0, 0)
    full = once((rows, depth), whole)
    extra = [] if first else list(sums)
    count = 4 + len(extra)
    if kept is not None:
        extra += list(kept)
    return pl.pallas_call(
        functools.partial(mlp_kernel, first),
        grid=(units // size,),
        in_specs=[full, full]
        + [pl.BlockSpec((depth, size), lambda i: (0, i)), pl.BlockSpec((depth, size), lambda i: (0, units // size + i))]
        + ([] if first else [full, full])
        + [ANY] * (len(extra) + 4 - count + len(after)),
        out_specs=[pl.BlockSpec((rows, size), lambda i: (row, i))] * 2 + [pl.BlockSpec((rows, depth), whole)] * 2,
        out_shape=[jax.ShapeDtypeStruct((2 * rows, units), jnp.bfloat16)] * 2
        + [jax.ShapeDtypeStruct((rows, depth), jnp.float32)] * 2,
        input_output_aliases={} if kept is None else {count: 0, count + 1: 1},
        compiler_params=params(48),
        cost_estimate=cost(0),
        name="mlp",
    )(normed3, grads, weights, weights, *extra, *after)


def mlp_grads_kernel(a0_ref, a1_ref, g0_ref, g1_ref, gu_ref, m_ref, out_ref, at_ref, gt_ref):
    i = pl.program_id(0)
    steps = pl.num_programs(0) // 2
    rows = a0_ref.shape[0]

    @pl.when(i == 0)
    def _():
        at_ref[:, :rows] = a0_ref[...].T
        at_ref[:, rows:] = a1_ref[...].T
        gt_ref[:, :rows] = g0_ref[...].T
        gt_ref[:, rows:] = g1_ref[...].T

    @pl.when(i < steps)
    def _():
        out_ref[...] = low(nn(gt_ref[...], m_ref[...]))

    @pl.when(i >= steps)
    def _():
        out_ref[...] = low(nn(at_ref[...], gu_ref[...]))


def mlp_grads(normed3, grads, grad_inner, active):
    rows, depth = normed3[0].shape
    units = active.shape[1]
    size = 512
    steps = units // size
    full = once((rows, depth), lambda i: (0, 0))
    return pl.pallas_call(
        mlp_grads_kernel,
        grid=(2 * steps,),
        in_specs=[full] * 4
        + [
            pl.BlockSpec((2 * rows, size), lambda i: (0, jnp.maximum(i - steps, 0))),
            pl.BlockSpec((2 * rows, size), lambda i: (0, jnp.minimum(i, steps - 1))),
        ],
        out_specs=pl.BlockSpec((depth, size), lambda i: (0, lax.rem(i + steps, 2 * steps))),
        out_shape=jax.ShapeDtypeStruct((depth, 2 * units), jnp.bfloat16),
        scratch_shapes=[pltpu.VMEM((depth, 2 * rows), jnp.bfloat16)] * 2,
        compiler_params=params(48),
        cost_estimate=cost(0),
        name="mlp_grads",
    )(*normed3, *grads, grad_inner, active)


def middle_bwd_kernel(
    start_ref, gy_ref, ga3_ref, got3_ref, h2_ref, h1_ref, cq_in_ref, t0_ref, t1_ref, t2_ref, t3_ref,
    so_ref, cq_ref, co_ref, g2_ref, g3_ref, _,
    g1_ref, g1b_ref, g2b_ref, gcq_ref, gtext_ref, go_ref, norms_ref, grad_ref, acc_ref,
):
    i = pl.program_id(0)
    here, part = start_ref[0], start_ref[2]
    rows, cols = gcq_ref.shape
    step = lax.rem(part + 4 - lax.rem(i, 4), 4)
    factor = HEAD_DIM ** (-0.5)

    @pl.when(i == 0)
    def _():
        back, gain, shift = norm_back_kernel(
            h2_ref[...], g3_ref[...], ga3_ref[...] + got3_ref[...].astype(jnp.float32)
        )
        grad_ref[...] = gy_ref[...].astype(jnp.float32) + back
        g2b_ref[...] = low(grad_ref[...])
        norms_ref[2:3, :] = gain
        norms_ref[3:4, :] = shift
        acc_ref[...] = jnp.zeros_like(acc_ref)

    @pl.when(i < 4)
    def _():
        gco = low(nn(g2b_ref[...], co_ref[...]))
        cq = cq_in_ref[...]
        text = chosen(step, (t0_ref, t1_ref, t2_ref, t3_ref), t0_ref[...])
        count = text.shape[0] // 2
        keys, values = text[:, :cols], text[:, cols:]
        parts = []
        for pair in range(cols // PAIR):
            at = slice(pair * PAIR, (pair + 1) * PAIR)
            keys_t = keys[:, at].T
            grad_keys = grad_values = 0.0
            for head in range(2):
                probs = cross_probs(here, part * rows, cq[:, at], lanes_of(keys[:, at], head), count)
                grad_probs = nt(lanes_of(values[:, at], head), gco[:, at])
                total = jnp.sum(probs * grad_probs, axis=0, keepdims=True)
                grad_scores = low(probs * (grad_probs - total))
                parts.append(nn(keys_t[half(head), :], grad_scores))
                grad_keys = grad_keys + nn(grad_scores, lanes_of(cq[:, at], head))
                grad_values = grad_values + nn(low(probs), lanes_of(gco[:, at], head))
            gtext_ref[0, 0, :, at] = low(grad_keys * factor)
            gtext_ref[0, 1, :, at] = low(grad_values)
        gcq = low((jnp.concatenate(parts, 0) * factor).T)
        gcq_ref[...] = gcq
        acc_ref[...] += nt(gcq, cq_ref[...])

        @pl.when(i == 3)
        def _():
            back, gain, shift = norm_back_kernel(h1_ref[...], g2_ref[...], acc_ref[...])
            grad = grad_ref[...] + back
            g1_ref[...] = grad
            g1b_ref[...] = low(grad)
            norms_ref[0:1, :] = gain
            norms_ref[1:2, :] = shift

    @pl.when(i >= 4)
    def _():
        go_ref[0] = low(nn(g1b_ref[...], so_ref[...]))


def middle_bwd(start, out_grad, grad3, got3, hidden2, hidden1, cross_q, texts, weights, gain2, gain3, token):
    rows, depth = out_grad.shape
    cols = depth // 4
    count = texts[0].shape[0]
    whole = lambda i, s: (0, 0)
    early = lambda i, s: (0, jnp.minimum(i, 3))
    full = pl.BlockSpec((rows, depth), whole)
    vector = once((1, depth), whole)
    wide16 = jax.ShapeDtypeStruct((rows, depth), jnp.bfloat16)
    fixed = once((rows, depth), whole)
    return pl.pallas_call(
        middle_bwd_kernel,
        grid_spec=pltpu.PrefetchScalarGridSpec(
            num_scalar_prefetch=1,
            grid=(8,),
            in_specs=[fixed] * 5
            + [pl.BlockSpec((rows, cols), early)]
            + [once(texts[0].shape, whole)] * 4
            + [
                pl.BlockSpec((depth, cols), lambda i, s: (jnp.maximum(i - 4, 0), 0)),
                pl.BlockSpec((depth, cols), lambda i, s: (jnp.minimum(i, 3), 1)),
                pl.BlockSpec((depth, cols), lambda i, s: (jnp.minimum(i, 3), 2)),
            ]
            + [vector] * 2
            + [ANY],
            out_specs=[
                full,
                full,
                full,
                pl.BlockSpec((rows, cols), early),
                pl.BlockSpec((1, 2, count, cols), lambda i, s: (jnp.minimum(i, 3), 0, 0, 0)),
                pl.BlockSpec((1, rows, cols), lambda i, s: (jnp.maximum(i - 4, 0), 0, 0)),
                pl.BlockSpec((8, depth), whole),
            ],
            scratch_shapes=[pltpu.VMEM((rows, depth), jnp.float32)] * 2,
        ),
        out_shape=[
            jax.ShapeDtypeStruct((rows, depth), jnp.float32),
            wide16,
            wide16,
            wide16,
            jax.ShapeDtypeStruct((4, 2, count, cols), jnp.bfloat16),
            jax.ShapeDtypeStruct((4, rows, cols), jnp.bfloat16),
            jax.ShapeDtypeStruct((8, depth), jnp.float32),
        ],
        compiler_params=params(56),
        cost_estimate=cost(2000),
        name="middle_bwd",
    )(start, out_grad, grad3, got3, hidden2, hidden1, cross_q, *texts, weights, weights, weights,
      gain2[None], gain3[None], token)


def middle_grads_kernel(so_l, cq_l, co_l, so_r, cq_r, co_r, out_ref, l_ref):
    i = pl.program_id(0)
    m = lax.rem(i, 3)

    @pl.when(i == 0)
    def _():
        for index, ref in enumerate((so_l, cq_l, co_l)):
            l_ref[index] = ref[...].T

    for index, ref in enumerate((so_r, cq_r, co_r)):

        @pl.when(m == index)
        def _():
            out_ref[...] = low(nn(l_ref[index], ref[...]))


def middle_grads(grad1, normed2, grad2, mixed, grad_cq, cmix):
    rows, depth = normed2.shape
    cols = depth // 4
    full = once((rows, depth), lambda i: (0, 0))
    quarter = pl.BlockSpec((rows, cols), lambda i: (0, i // 3))
    return pl.pallas_call(
        middle_grads_kernel,
        grid=(12,),
        in_specs=[full] * 3 + [quarter] * 3,
        out_specs=pl.BlockSpec((depth, cols), lambda i: (0, i)),
        out_shape=jax.ShapeDtypeStruct((depth, 3 * depth), jnp.bfloat16),
        scratch_shapes=[pltpu.VMEM((3, depth, rows), jnp.bfloat16)],
        compiler_params=params(40),
        cost_estimate=cost(0),
        name="middle_grads",
    )(grad1, normed2, grad2, mixed, grad_cq, cmix)


def block_grad_kernel(order_ref, x_ref, gq_ref, gkv_ref, back_ref, w0_ref, w1_ref, w2_ref, *refs):
    part_ref, g_ref, norms_ref, padded_ref = refs[-4:]
    i = pl.program_id(0)
    rows = x_ref.shape[0]
    skip = padded_ref.shape[1] - back_ref.shape[1]

    @pl.when(i == 0)
    def _():
        padded_ref[:, :skip, :] = jnp.zeros_like(padded_ref[:, :skip, :])
        padded_ref[:, skip:, :] = back_ref[...]
        norms_ref[...] = jnp.zeros_like(norms_ref)

    at = pl.ds(pl.multiple_of(order_ref[i] * rows, rows), rows)
    cols = gq_ref.shape[1]
    total = 0.0
    for index, w_ref in enumerate((w0_ref, w1_ref, w2_ref)):
        grad = gq_ref[...]
        if index:
            grad = low(gkv_ref[index - 1] + padded_ref[index - 1, at, :].astype(jnp.float32))
        g_ref[:, index * cols:(index + 1) * cols] = grad
        total = total + nt(grad, w_ref[...])
    unit, _ = normed(x_ref[...].astype(jnp.float32))
    norms_ref[0:1, :] += jnp.sum(total * unit, axis=0, keepdims=True)
    norms_ref[1:2, :] += jnp.sum(total, axis=0, keepdims=True)
    part_ref[0] = total.astype(part_ref.dtype)


def block_grad(order, count, block, grad_q, grad_kv, back, weights, before, after=()):
    width, depth = block.shape
    cols = grad_q.shape[1]
    rows = width // 4
    at = lambda i, order: (order[i], 0)
    w_spec = lambda j: once((depth, cols), lambda i, order: (0, j))
    return pl.pallas_call(
        block_grad_kernel,
        grid_spec=pltpu.PrefetchScalarGridSpec(
            num_scalar_prefetch=1,
            grid=(count,),
            in_specs=[
                pl.BlockSpec((rows, depth), at),
                pl.BlockSpec((rows, cols), at),
                pl.BlockSpec((2, rows, cols), lambda i, order: (0, order[i], 0)),
                once(back.shape, lambda i, order: (0, 0, 0)),
                w_spec(0),
                w_spec(1),
                w_spec(2),
            ]
            + [ANY] * (len(before) + len(after)),
            out_specs=[
                pl.BlockSpec((1, rows, depth), lambda i, order: (order[i], 0, 0)),
                pl.BlockSpec((rows, 3 * cols), at),
                pl.BlockSpec((8, depth), lambda i, order: (0, 0)),
            ],
            scratch_shapes=[pltpu.VMEM((2, width, cols), jnp.bfloat16)],
        ),
        out_shape=[
            jax.ShapeDtypeStruct((4, rows, depth), jnp.bfloat16),
            jax.ShapeDtypeStruct((width, 3 * cols), jnp.bfloat16),
            jax.ShapeDtypeStruct((8, depth), jnp.float32),
        ],
        input_output_aliases={8: 0, 9: 1} if before else {},
        compiler_params=params(48),
        cost_estimate=cost(0),
        name="block_grad",
    )(order, block, grad_q, grad_kv, back, weights, weights, weights, *before, *after)


def block_weights_kernel(at_ref, g_ref, text_ref, gtext_ref, out_ref):
    i = pl.program_id(0)

    @pl.when(i < 3)
    def _():
        out_ref[...] = low(nn(at_ref[...], g_ref[...]))

    @pl.when(i >= 3)
    def _():
        out_ref[...] = low(nn(text_ref[...].T, gtext_ref[...]))


def block_weights(normed1_t, grads, text, grad_text, after):
    depth, width = normed1_t.shape
    cols = grads.shape[1] // 3
    whole = lambda i: (0, 0)
    return pl.pallas_call(
        without(block_weights_kernel, 4, len(after)),
        grid=(5,),
        in_specs=[
            once((depth, width), whole),
            pl.BlockSpec((width, cols), lambda i: (0, jnp.minimum(i, 2))),
            once(text.shape, whole),
            pl.BlockSpec((text.shape[0], cols), lambda i: (0, jnp.maximum(i - 3, 0))),
        ]
        + [ANY] * len(after),
        out_specs=pl.BlockSpec((depth, cols), lambda i: (0, i)),
        out_shape=jax.ShapeDtypeStruct((depth, 5 * cols), jnp.bfloat16),
        compiler_params=params(40),
        cost_estimate=cost(0),
        name="block_weights",
    )(normed1_t, grads, text, grad_text, *after)


def round_kernel(_, up_sum_ref, down_sum_ref, up_ref, down_ref, up_out_ref, down_out_ref):
    up_out_ref[...] = low(up_sum_ref[0].astype(jnp.float32) + up_ref[...].astype(jnp.float32))
    down_out_ref[...] = low(down_sum_ref[0].astype(jnp.float32) + down_ref[...].astype(jnp.float32))


def round_sums(targets, sums, up, down, after, micros):
    rows, depth = up.shape
    size = rows // 4
    flat = pl.BlockSpec((size, depth), lambda i, targets: (i, 0))
    return pl.pallas_call(
        without(round_kernel, 5, len(after)),
        grid_spec=pltpu.PrefetchScalarGridSpec(
            num_scalar_prefetch=1,
            grid=(4,),
            in_specs=[
                pl.BlockSpec((1, size, depth), lambda i, targets: (targets[0], i, 0)),
                pl.BlockSpec((1, size, depth), lambda i, targets: (targets[1], i, 0)),
                flat,
                flat,
            ]
            + [ANY] * len(after),
            out_specs=[flat, flat],
        ),
        out_shape=[jax.ShapeDtypeStruct((rows, depth), jnp.bfloat16)] * 2,
        compiler_params=params(24),
        cost_estimate=cost(micros),
        name="round_sums",
    )(targets, sums, sums, up, down, *after)


def last_kernel(_, sum_ref, up_ref, down_ref, x_ref, grad_ref, gain_ref, out_ref):
    total = sum_ref[0].astype(jnp.float32) + up_ref[...].astype(jnp.float32) + down_ref[...].astype(jnp.float32)
    back, _, _ = norm_back_kernel(x_ref[...].astype(jnp.float32), gain_ref[...], total)
    out_ref[...] = grad_ref[...] + back


def last_sums(place, sums, up, down, tokens, grad, gain, after):
    rows, depth = up.shape
    size = rows // 4
    flat = pl.BlockSpec((size, depth), lambda i, place: (i, 0))
    return pl.pallas_call(
        without(last_kernel, 7, len(after)),
        grid_spec=pltpu.PrefetchScalarGridSpec(
            num_scalar_prefetch=1,
            grid=(4,),
            in_specs=[pl.BlockSpec((1, size, depth), lambda i, place: (place[0], i, 0))]
            + [flat] * 4
            + [pl.BlockSpec((1, depth), lambda i, place: (0, 0))]
            + [ANY] * len(after),
            out_specs=flat,
        ),
        out_shape=jax.ShapeDtypeStruct((rows, depth), jnp.float32),
        compiler_params=params(24),
        cost_estimate=cost(0),
        name="last_sums",
    )(place, sums, up, down, tokens, grad, gain[None], *after)


def piece_kernel(own_ref, first_ref, second_ref, third_ref, out_ref):
    out_ref[...] = (own_ref[...].astype(jnp.float32) + first_ref[...].astype(jnp.float32)) + (
        second_ref[...].astype(jnp.float32) + third_ref[...].astype(jnp.float32)
    )


def piece_sums(pieces, after):
    rows, cols = pieces[0].shape
    return pl.pallas_call(
        without(piece_kernel, 4, len(after)),
        in_specs=[pl.BlockSpec(memory_space=pltpu.VMEM)] * 4 + [ANY] * len(after),
        out_specs=pl.BlockSpec(memory_space=pltpu.VMEM),
        out_shape=jax.ShapeDtypeStruct((rows, cols), jnp.float32),
        compiler_params=params(24),
        cost_estimate=cost(0),
        name="piece_sums",
    )(*pieces, *after)


def turned(value, axis, steps):
    count = lax.axis_size(axis)
    return lax.ppermute(value, axis, [(source, (source + steps) % count) for source in range(count)])


def swapped(value, bit):
    return lax.ppermute(value, "tp", [(source, source ^ bit) for source in range(lax.axis_size("tp"))])


def moved(value, steps, senders):
    return lax.ppermute(value, "tp", [(source, source + steps) for source in senders])


def along_line(value):
    count = lax.axis_size("tp")
    up, down = [value], [value]
    for round_at in range(count - 1):
        up.append(moved(up[-1], 1, range(round_at, count - 1)))
        down.append(moved(down[-1], -1, range(1, count - round_at)))
    return up, down


def picked(value, index):
    return lax.dynamic_index_in_dim(value, index % value.shape[0], 0, keepdims=True)


def exchanged(value, place):
    count = lax.axis_size("tp")
    return [value] + [turned(picked(value, place + step), "tp", step) for step in range(1, count)]


def in_order(parts, place):
    out = jnp.zeros((len(parts),) + parts[0].shape, parts[0].dtype)
    for step, part in enumerate(parts):
        out = lax.dynamic_update_slice_in_dim(out, part[None], (place + len(parts) - step) % len(parts), 0)
    return out


def dot(left, right):
    return jnp.dot(left, right, preferred_element_type=jnp.float32)


def dot_last(left, right):
    return jnp.einsum("ra,ba->rb", left, right, preferred_element_type=jnp.float32)


def split_mlp(values):
    return values[:2], values[2], values[3]


def on_device(
    tokens,
    text_states,
    clip_start,
    ln1_gain,
    ln1_bias,
    self_query,
    self_key,
    self_value,
    self_out,
    ln2_gain,
    ln2_bias,
    cross_query,
    cross_key,
    cross_value,
    cross_out,
    ln3_gain,
    ln3_bias,
    fc_in,
    fc_out,
    out_grad,
):
    place, members = lax.axis_index("wide"), lax.axis_size("wide")
    part, parts = lax.axis_index("tp"), lax.axis_size("tp")
    here = lax.dynamic_index_in_dim(clip_start, place, 0, keepdims=False)
    before = lax.dynamic_index_in_dim(clip_start, (place + members - 1) % members, 0, keepdims=False)
    start = jnp.stack([here, before, part]).astype(jnp.int32)
    rows, depth = tokens.shape
    width = rows * parts
    cols, units = self_query.shape[1], fc_in.shape[1]
    texts = text_states.shape[0]
    scalars = lambda *values: jnp.stack([jnp.asarray(value, jnp.int32) for value in values])

    def gathered(value):
        return lax.all_gather(value, "wide", axis=0, tiled=True)

    weights1 = gathered(jnp.concatenate([self_query, self_key, self_value, cross_key, cross_value], 1))
    fc_shards = jnp.concatenate([fc_in, fc_out.T], 1)
    text_at = 3 * cols
    first, last = part == 0, part == parts - 1
    first, last = part == 0, part == parts - 1
    (_, up1, up2, up3), (_, down1, down2, down3) = along_line(tokens)
    shards = jnp.concatenate([self_out.T, cross_query, cross_out.T], 1)
    weights2 = lax.all_gather(shards, ("tp", "wide"), axis=0, tiled=True)

    block = qkv_block(scalars(part, 0), [tokens], ln1_gain, ln1_bias, weights1, 0, width, cols, None)
    at = scalars(jnp.where(first, 1, part - 1), jnp.where(first, 1, 0))
    block = qkv_block(at, [up1, down1], ln1_gain, ln1_bias, weights1, 0, width, cols, block)
    at = scalars((part + 2) % parts, jnp.where(part >= 2, 0, 1))
    block = qkv_block(at, [up2, down2], ln1_gain, ln1_bias, weights1, 0, width, cols, block)
    at = scalars(jnp.where(first, parts - 1, (part + 1) % parts), jnp.where(first, 2, jnp.where(last, 1, 0)))
    text_kv = low(dot(tie(text_states, block[0]), weights1[:, text_at:]))
    text_kv = jnp.concatenate([turned(text_kv, "wide", 1), text_kv], 0)
    block = qkv_block(
        at, [down1, up3, down3], ln1_gain, ln1_bias, weights1, 0, width, cols, block, [text_kv]
    )
    block, _, normed1_t, qkv = block
    kv_old = turned(qkv[MIN_START:, cols:], "wide", 1)
    weights_fc = gathered(tie(fc_shards, qkv))
    grad_out = [out_grad, swapped(tie(out_grad, up3, down3), 1)]
    fc_in_other = swapped(tie(fc_in, up3, down3), 2)
    text_kv = [text_kv] + [turned(text_kv, "tp", step) for step in range(1, parts)]
    mixed, mixed_t, logs = self_fwd(start, qkv, kv_old, [])
    mixed = exchanged(tie(mixed, grad_out[1], fc_in_other, *text_kv).reshape(parts, rows, cols), part)
    fc_out_other = swapped(tie(fc_out.T, *mixed[1:]), 2)
    mixed, hidden1, normed2, cross_q, cmix, hidden2, normed3 = middle_fwd(
        start, tokens, mixed, text_kv, weights2, ln2_gain, ln2_bias, ln3_gain, ln3_bias
    )

    def summed(value):
        return lax.psum_scatter(value, "wide", scatter_dimension=0, tiled=True)

    weights3 = gathered(jnp.concatenate([fc_in_other, tie(fc_out_other, normed3)], 1))

    normed3 = [normed3, swapped(normed3, 1)]
    kept, *sums_own = split_mlp(mlp(normed3[0], grad_out[0], weights_fc, units, 0, None, None))
    kept, *sums_theirs = split_mlp(mlp(normed3[1], grad_out[1], weights_fc, units, 1, kept, None))
    grads_own = mlp_grads(normed3, grad_out, kept[1], kept[0])
    after_own = tie(sums_theirs[0], weights3, grads_own, micros=2000)
    kept_other, *sums_theirs = split_mlp(
        mlp(normed3[1], grad_out[1], weights3, units, 1, None, (after_own, sums_theirs[1]))
    )
    got3 = swapped(low(sums_theirs[0]), 1)
    kept_other, *sums_own = split_mlp(mlp(normed3[0], grad_out[0], weights3, units, 0, kept_other, sums_own))
    grads_other = mlp_grads(normed3, grad_out, kept_other[1], kept_other[0])

    grad1, grad1_low, grad2_low, grad_cq, grad_text, grad_mixed, norms23 = middle_bwd(
        start, out_grad, sums_own[0], got3, hidden2, hidden1, cross_q, text_kv, weights2, ln2_gain, ln3_gain, grads_other
    )
    outer = swapped(low(sums_theirs[1]), 1)
    layer_out = low(hidden2 + sums_own[1] + outer.astype(jnp.float32))
    grad_mixed = exchanged(tie(grad_mixed, outer), part)
    grads_middle = middle_grads(grad1_low, normed2, grad2_low, mixed, grad_cq, cmix)

    grad_text = exchanged(tie(grad_text, grads_middle), part)
    grads_own = summed(grads_own)
    grad_kv_old, grad_query_t = self_bwd(start, qkv, kv_old, grad_mixed, mixed_t, logs, None, [grads_own])
    grad_kv_back = turned(grad_kv_old, "wide", -1)
    grad_text = [tie(picked(grad_text[0], part), grad_query_t)] + grad_text[1:]
    grad_text = sum(piece[0].astype(jnp.float32) for piece in grad_text)
    back = turned(low(grad_text[:, :texts]), "wide", -1).astype(jnp.float32)
    grads_other = summed(grads_other)
    grad_text = low(grad_text[:, texts:] + back)
    grad_text = jnp.concatenate([grad_text[0], grad_text[1]], 1)
    text_term = low(dot_last(grad_text, weights1[:, text_at:]))
    grad_kv, grad_query = self_bwd(
        start, qkv, None, grad_mixed, mixed_t, logs, grad_query_t, [text_term, grads_other]
    )
    text_term = [text_term] + [turned(text_term, "tp", step) for step in range(1, parts)]
    grads_other = swapped(grads_other, 2)

    block_args = (block, grad_query, grad_kv, grad_kv_back, weights1)
    near, far = part < parts // 2, parts - 1
    sums, grad_qkv, norms_first = block_grad(scalars(jnp.where(near, far, 0)), 1, *block_args, [], text_term)
    own_first = picked(sums, jnp.where(near, far, 0))[0]
    up, down = moved(own_first, 1, (0,)), moved(own_first, -1, (far,))
    others = scalars(
        jnp.where(near, 2, 1),
        jnp.where(first, 1, jnp.where(last, 2, jnp.where(near, 0, far))),
        part,
    )
    sums, grad_qkv, norms_rest = block_grad(others, 3, *block_args, [sums, grad_qkv], [grads_other])
    grads_block = block_weights(normed1_t, grad_qkv, text_states, grad_text, [])
    norms = jnp.concatenate([norms_first[:2] + norms_rest[:2], norms23[:4]], 0)
    grads_middle = summed(grads_middle)
    pieces = [
        lax.dynamic_slice_in_dim(grads_middle, ((part + step) % parts) * 3 * cols, 3 * cols, 1) for step in range(parts)
    ]
    grads_middle = piece_sums([pieces[0]] + [turned(pieces[step], "tp", step) for step in range(1, parts)], [])
    after = []
    for round_at in (2, 3):
        targets = scalars((part + parts - round_at) % parts, (part + round_at) % parts)
        up, down = round_sums(targets, sums, up, down, after, 2000 if round_at == 3 else 0)
        norms = norms + tie(swapped(norms, round_at - 1), grads_block, pieces[0])
        sent = up
        up, down = moved(up, 1, range(round_at)), moved(down, -1, range(parts - round_at, parts))
        after = [norms, grads_block, grads_middle]
    tokens_grad = last_sums(scalars(part), sums, up, down, tokens, grad1, ln1_gain, [norms])
    bit = 1
    while bit < members:
        norms = norms + lax.ppermute(norms, "wide", [(source, source ^ bit) for source in range(members)])
        bit *= 2
    text_grad = jnp.sum(in_order([tie(text_term[0], sent)] + text_term[1:], part).astype(jnp.float32), 0)

    fc_grads = grads_own.astype(jnp.float32) + grads_other.astype(jnp.float32)
    fc_in_grad, fc_out_grad = fc_grads[:, :units], fc_grads[:, units:].T
    grads_block = tie(summed(grads_block), sent).astype(jnp.float32)
    grads_block = [grads_block[:, i * cols : (i + 1) * cols] for i in range(5)]
    grads_middle = [grads_middle[:, i * cols : (i + 1) * cols] for i in range(3)]

    return (
        layer_out,
        tokens_grad,
        text_grad,
        norms[0],
        norms[1],
        grads_block[0],
        grads_block[1],
        grads_block[2],
        grads_middle[0].T,
        norms[2],
        norms[3],
        grads_middle[1],
        grads_block[3],
        grads_block[4],
        grads_middle[2].T,
        norms[4],
        norms[5],
        fc_in_grad,
        fc_out_grad,
    )


def solution(mesh):
    in_specs = (
        P(("wide", "tp"), None),
        P("wide", None),
        P(),
        P(),
        P(),
        P("wide", "tp"),
        P("wide", "tp"),
        P("wide", "tp"),
        P("tp", "wide"),
        P(),
        P(),
        P("wide", "tp"),
        P("wide", "tp"),
        P("wide", "tp"),
        P("tp", "wide"),
        P(),
        P(),
        P("wide", "tp"),
        P("tp", "wide"),
        P(("wide", "tp"), None),
    )
    out_specs = (
        P(("wide", "tp"), None),
        P(("wide", "tp"), None),
        P("wide", None),
        P(),
        P(),
        P("wide", "tp"),
        P("wide", "tp"),
        P("wide", "tp"),
        P("tp", "wide"),
        P(),
        P(),
        P("wide", "tp"),
        P("wide", "tp"),
        P("wide", "tp"),
        P("tp", "wide"),
        P(),
        P(),
        P("wide", "tp"),
        P("tp", "wide"),
    )
    return jax.shard_map(
        on_device, mesh=mesh, in_specs=in_specs, out_specs=out_specs, check_vma=False
    )
```
